256 devices in a mesh: pipe: 8 (over x_lo, y), dp: 32 (over x_hi, z, core).
Axes of the slice: x: 4 (x_hi: 2, x_lo: 2; x = x_hi * 2 + x_lo), y: 4, z: 8, core: 2. Of those that a mesh axis runs over, the one named last changes fastest.
Arguments:
- x_down: bfloat16 [4096, 4096], P('dp'), may hold values from -6 to 6
- x_up: bfloat16 [4096, 4096], P('dp'), may hold values from -6 to 6
- cot_down: bfloat16 [4096, 4096], P('dp'), may hold values from -6 to 6
- cot_up: bfloat16 [4096, 4096], P('dp'), may hold values from -6 to 6
- w_qkv: bfloat16 [8, 4096, 384], P('pipe', 'dp'), may hold values from -0.09375 to 0.09375
- w_out: bfloat16 [8, 128, 4096], P('pipe', None, 'dp'), may hold values from -0.5 to 0.5
- block_mask: int32 [4, 4], replicated, may hold values from 0 to 1, as said below
Outputs:
- grad_qkv: float32 [8, 4096, 384], P('pipe', 'dp')
- grad_out: float32 [8, 128, 4096], P('pipe', None, 'dp')
The draws below stay inside these ranges and needn't reach their ends.
Inputs may be any that keep to these rules, and one draw needn't show every extreme that they name: block_mask is 1 on the diagonal and 0 above it.
All inputs are finite; a program needn't handle non-finite values.
Results may differ from the reference program's by a relative error of at most 0.04.
Values may be sent and summed in bfloat16 or wider, within the bound.
A program may use at most 128 MiB of HBM per device.

```python
import jax
import jax.numpy as jnp
from jax import lax

D = 4096
HD = 128
BLK = 32
MB = 128
NB = 4
LAYERS = 8
TOKENS = 4096
N_PIPE = 8
N_DP = 32


def draw_block_mask(key, part):
    key = jax.random.fold_in(key, 7)
    stride_key, entry_key = jax.random.split(key)
    stride = jax.random.randint(stride_key, (), 2, 4)
    entry_bits = jax.random.randint(entry_key, (NB, NB), 0, 2)
    row_index = lax.broadcasted_iota(jnp.int32, (NB, NB), 0)
    col_index = lax.broadcasted_iota(jnp.int32, (NB, NB), 1)
    strided = (row_index - col_index) % stride == 0
    chosen = strided | (entry_bits == 1)
    below_diag = (col_index < row_index) & chosen
    return jnp.where((col_index == row_index) | below_diag, 1, 0).astype(jnp.int32)


def level_of(key, dims, cuts, low, largest):
    factor_of, own = 1.0, jax.random.fold_in(key, 6)
    for axis_at, parts in cuts:
        draws = jnp.exp(jax.random.uniform(jax.random.fold_in(own, axis_at), (parts,), jnp.float32, low / len(cuts), largest / len(cuts)))
        factor_of = factor_of * jnp.repeat(draws, dims[axis_at] // parts).reshape([-1 if axis == axis_at else 1 for axis in range(len(dims))])
    return factor_of


def noise(own_key, dims, spread, limit, cuts=(), kind=jnp.bfloat16):
    values = jax.random.normal(own_key, dims, jnp.float32) * spread
    if len(cuts) > 0:
        values = level_of(own_key, dims, cuts, -0.22, 0.18) * values
    return jnp.clip(values, min=-limit, max=limit).astype(kind)


def setup_inputs(seed: int = 0) -> dict:
    splits = jax.random.split(jax.random.key(seed), 8)
    return {
        "x_down": noise(splits[0], (TOKENS, D), 1.0, 6.0, ((0, 32),)),
        "x_up": noise(splits[1], (TOKENS, D), 1.0, 6.0, ((0, 32),)),
        "cot_down": noise(splits[2], (TOKENS, D), 1.0, 6.0, ((0, 32),)),
        "cot_up": noise(splits[3], (TOKENS, D), 1.0, 6.0, ((0, 32),)),
        "w_qkv": noise(splits[4], (LAYERS, D, 3 * HD), D ** -0.5, 0.09375, ((0, 8), (1, 32))),
        "w_out": noise(splits[5], (LAYERS, HD, D), HD ** -0.5, 0.5, ((0, 8), (2, 32))),
        "block_mask": draw_block_mask(jax.random.fold_in(splits[7], 71), 0),
    }


def allowed_pairs(block_mask, block_len):
    expanded = jnp.repeat(jnp.repeat(block_mask, block_len, axis=0), block_len, axis=1)
    row_index = lax.broadcasted_iota(jnp.int32, expanded.shape, 0)
    col_index = lax.broadcasted_iota(jnp.int32, expanded.shape, 1)
    return (expanded == 1) & (col_index <= row_index)

def section_layer(tokens, qkv_weight, out_weight, allowed):
    head_size = out_weight.shape[0]
    inputs_f = tokens.astype(jnp.float32)
    normed = (inputs_f * lax.rsqrt(lax.optimization_barrier(jnp.mean(inputs_f * inputs_f, axis=-1, keepdims=True)) + 1e-06)).astype(jnp.bfloat16)
    projected = jnp.dot(normed, qkv_weight, preferred_element_type=jnp.float32).astype(jnp.bfloat16)
    queries = projected[:, :head_size]
    key_proj = projected[:, head_size:2 * head_size]
    values = projected[:, 2 * head_size:]
    scores = jnp.dot(queries, key_proj.T, preferred_element_type=jnp.float32) * head_size ** (-0.5)
    scores = jnp.where(allowed, scores, -1e+30)
    top_score = lax.optimization_barrier(jnp.max(scores, axis=-1, keepdims=True))
    exp_scores = jnp.exp(scores - top_score)
    soft_weights = (exp_scores / lax.optimization_barrier(jnp.sum(exp_scores, axis=-1, keepdims=True))).astype(jnp.bfloat16)
    attended = jnp.dot(soft_weights, values, preferred_element_type=jnp.float32).astype(jnp.bfloat16)
    return (inputs_f + jnp.dot(attended, out_weight, preferred_element_type=jnp.float32)).astype(jnp.bfloat16)

def layer_grads(saved_in, cotangent, qkv_weight, out_weight, allowed):

    def apply_layer(tokens, first_weight, second_weight):
        return section_layer(tokens, first_weight, second_weight, allowed)
    outputs, pullback = jax.vjp(apply_layer, saved_in, qkv_weight, out_weight)
    return pullback(cotangent)

def chain_grads(inputs, cotangent, w_qkv, w_out, allowed):
    saved = []
    current = inputs
    for layer_num in range(N_PIPE):
        saved.append(current)
        if layer_num + 1 < N_PIPE:
            current = section_layer(current, w_qkv[layer_num], w_out[layer_num], allowed)
    grads_first = [None] * N_PIPE
    grads_second = [None] * N_PIPE
    moving = cotangent
    for layer_num in reversed(range(N_PIPE)):
        moving, grads_first[layer_num], grads_second[layer_num] = layer_grads(saved[layer_num], moving, w_qkv[layer_num], w_out[layer_num], allowed)
    return (jnp.stack(grads_first).astype(jnp.float32), jnp.stack(grads_second).astype(jnp.float32))

def reference(x_down, x_up, cot_down, cot_up, w_qkv, w_out, block_mask):
    allowed = allowed_pairs(block_mask, BLK)

    def one_group(totals, group_num):
        start = (group_num * MB).astype(jnp.int32)
        down_in = lax.dynamic_slice_in_dim(x_down, start, MB, 0)
        up_in = lax.dynamic_slice_in_dim(x_up, start, MB, 0)
        down_cot = lax.dynamic_slice_in_dim(cot_down, start, MB, 0)
        up_cot = lax.dynamic_slice_in_dim(cot_up, start, MB, 0)
        qkv_down, out_down = chain_grads(down_in, down_cot, w_qkv, w_out, allowed)
        qkv_up, out_up = chain_grads(up_in, up_cot, w_qkv, w_out, allowed)
        return ((totals[0] + qkv_down + qkv_up, totals[1] + out_down + out_up), None)
    initial = (jnp.zeros(w_qkv.shape, jnp.float32), jnp.zeros(w_out.shape, jnp.float32))
    totals, unused = lax.scan(one_group, initial, jnp.arange(N_DP, dtype=jnp.int32))
    return (totals[0], totals[1])
```

```python
import functools

import jax
import jax.numpy as jnp
from jax import lax
from jax.experimental import pallas as pl
from jax.experimental.pallas import tpu as pltpu
from jax.sharding import PartitionSpec as P

BLK = 32
HEAD = 128
XH = 2
CORES = 2
BF = jnp.bfloat16
F32 = jnp.float32

NT = (((1,), (1,)), ((), ()))
TN = (((0,), (0,)), ((), ()))


def mm(a, b):
    return jnp.dot(a, b, preferred_element_type=F32)


def mm_nt(a, b):
    return lax.dot_general(a, b, NT, preferred_element_type=F32)


def mm_tn(a, b):
    return lax.dot_general(a, b, TN, preferred_element_type=F32)


def kernel(
    n_pipe,
    n_dp,
    x_down, x_up, cot_down, cot_up, wq_ref, wo_ref, bias_ref,
    gq_ref, go_ref,
    wpack, w, x, dy, p, soft, att, e_buf,
    rs_send, rs_recv, ds_send, ds_recv, da,
    g, gd, gz, gx, gxr, gf, out,
    load_sem, w1_send, w1_recv, wx_send, wx_recv, wz_send, wz_recv, wc_send, wc_recv,
    rs_ssem, rs_rsem, ag_ssem, ag_rsem,
    gc_send, gc_recv, gz_send, gz_recv, gx_send, gx_recv, gf_send, gf_recv,
):
    layers = n_pipe
    n_z = n_dp // (XH * CORES)
    n_i = n_dp // n_pipe
    rows = x.shape[2]
    feat = x.shape[3]
    dim = feat * n_pipe
    piece = w.shape[3] // XH
    rb = rows // n_pipe
    last = layers - 1
    q3 = 3 * HEAD
    scale = HEAD ** (-0.5)

    me = lax.axis_index("pipe")
    d = lax.axis_index("dp")
    xh = d // (n_z * CORES)
    z = (d // CORES) % n_z
    c = d % CORES

    def dp_at(xh_, z_, c_):
        return xh_ * (n_z * CORES) + z_ * CORES + c_

    def peer(k):
        return lax.rem(me + 1 + k, n_pipe)

    def z_peer(k):
        return dp_at(xh, lax.rem(z + 1 + k, n_z), c)

    xh_peer = dp_at(1 - xh, z, c)
    sibling = dp_at(xh, z, 1 - c)

    def spread_to(j):
        q = (d % n_i) * n_pipe + j
        return d // n_i, dp_at(q % XH, q // (XH * CORES), (q // XH) % CORES), q

    my_q = (z * CORES + c) * XH + xh
    my_i = my_q // n_pipe
    my_j = my_q % n_pipe
    home_dp = n_i * me + my_i

    def remote(src, dst, ssem, rsem, pp, dd):
        return pltpu.make_async_remote_copy(
            src_ref=src, dst_ref=dst, send_sem=ssem, recv_sem=rsem,
            device_id={"pipe": pp, "dp": dd}, device_id_type=pl.DeviceIdType.MESH,
        )

    def wait_bytes(ref, sem):
        pltpu.make_async_copy(ref, ref, sem).wait()

    cols = pl.ds(pl.multiple_of(me * feat, feat), feat)
    loads = [
        pltpu.make_async_copy(x_down.at[:, cols], x.at[0, 0], load_sem.at[0]),
        pltpu.make_async_copy(x_up.at[:, cols], x.at[0, 1], load_sem.at[1]),
        pltpu.make_async_copy(cot_down.at[:, cols], dy.at[last, 0], load_sem.at[2]),
        pltpu.make_async_copy(cot_up.at[:, cols], dy.at[last, 1], load_sem.at[3]),
    ]
    for copy in loads:
        copy.start()

    barrier = pltpu.get_barrier_semaphore()

    def greet(pp, dd):
        pl.semaphore_signal(
            barrier, inc=1, device_id={"pipe": pp, "dp": dd},
            device_id_type=pl.DeviceIdType.MESH,
        )

    for k in range(n_pipe - 1):
        greet(peer(k), d)
    for k in range(n_z - 1):
        greet(me, z_peer(k))
    greet(me, xh_peer)
    greet(me, sibling)
    for j in range(n_pipe):
        pp, dd, _ = spread_to(j)

        @pl.when((pp != me) | (dd != d))
        def _():
            greet(pp, dd)

        @pl.when((j != me) | (home_dp != d))
        def _():
            greet(j, home_dp)

    wpack[:, :q3] = wq_ref[0]
    wpack[:, q3:] = wo_ref[0].astype(F32).T.astype(BF)

    keeps_one = jnp.where(home_dp == d, 1, 0)
    pl.semaphore_wait(barrier, n_pipe + n_z + 2 * n_pipe - 2 * keeps_one)

    for j in range(n_pipe):
        pp, dd, q = spread_to(j)
        src = wpack.at[pl.ds(j * piece, piece)]
        dst = w.at[me, q // (XH * CORES), (q // XH) % CORES, pl.ds(pl.multiple_of((q % XH) * piece, piece), piece)]

        @pl.when((pp != me) | (dd != d))
        def _():
            remote(src, dst, w1_send.at[j], w1_recv.at[0], pp, dd).start()

        @pl.when((pp == me) & (dd == d))
        def _():
            pltpu.make_async_copy(src, dst, w1_recv.at[0]).start()

    mine = w.at[:, z, c, pl.ds(pl.multiple_of(xh * piece, piece), piece)]
    other = w.at[:, z, c, pl.ds(pl.multiple_of((1 - xh) * piece, piece), piece)]
    wait_bytes(mine, w1_recv.at[0])
    cx = remote(mine, mine, wx_send.at[0], wx_recv.at[0], me, xh_peer)
    cx.start()
    wait_bytes(other, wx_recv.at[0])

    def start_wz(layer):
        for k in range(n_z - 1):
            remote(
                w.at[layer, z, c], w.at[layer, z, c], wz_send.at[layer], wz_recv.at[layer], me, z_peer(k)
            ).start()

    def start_wc(layer):
        wait_bytes(w.at[layer, pl.ds(0, n_z - 1), c], wz_recv.at[layer])
        remote(w.at[layer, :, c], w.at[layer, :, c], wc_send.at[layer], wc_recv.at[layer], me, sibling).start()

    def wait_wc(layer):
        wait_bytes(w.at[layer, :, 1 - c], wc_recv.at[layer])

    def weight(layer):
        return w[layer].reshape(feat, q3 + HEAD)

    start_wz(0)
    start_wz(1)
    for copy in loads:
        copy.wait()

    own = pl.ds(pl.multiple_of(me * rb, rb), rb)

    def start_rs(cas, xl, wl):
        xf = xl.astype(F32)
        rs_send[cas, :, :q3] = mm(xl, wl[:, :q3]).astype(BF)
        sq = jnp.sum(xf * xf, axis=-1, keepdims=True)
        rs_send[cas, :, q3:] = jnp.broadcast_to(sq, (rows, HEAD)).astype(BF)
        for k in range(n_pipe - 1):
            to = peer(k)
            remote(
                rs_send.at[cas, pl.ds(pl.multiple_of(to * rb, rb), rb)],
                rs_recv.at[cas, n_pipe - 2 - k],
                rs_ssem.at[cas], rs_rsem.at[cas], to, d,
            ).start()

    def start_ag(layer, cas):
        wait_bytes(rs_recv.at[cas], rs_rsem.at[cas])
        wait_bytes(rs_recv.at[cas], rs_ssem.at[cas])
        total = rs_send[cas, own].astype(F32)
        for k in range(n_pipe - 1):
            total = total + rs_recv[cas, k].astype(F32)
        r = lax.rsqrt(total[:, q3:] * (1.0 / dim) + 1e-6)
        p[layer, cas, own, :q3] = (total[:, :q3] * r[:, :1]).astype(BF)
        high = r.astype(BF)
        low = (r - high.astype(F32)).astype(BF)
        lane = lax.broadcasted_iota(jnp.int32, r.shape, 1)
        p[layer, cas, own, q3:] = jnp.where(lane < HEAD // 2, high.astype(F32), low.astype(F32)).astype(BF)
        for k in range(n_pipe - 1):
            remote(
                p.at[layer, cas, own], p.at[layer, cas, own], ag_ssem.at[cas], ag_rsem.at[cas], peer(k), d
            ).start()

    def attend(layer, cas):
        part = p.at[layer, cas, pl.ds(0, rows - rb)]
        wait_bytes(part, ag_rsem.at[cas])
        wait_bytes(part, ag_ssem.at[cas])
        pr = p[layer, cas]
        s = mm_nt(pr[:, :HEAD], pr[:, HEAD : 2 * HEAD]) * scale
        s = jnp.where(bias_ref[...] > 0.5, s, -1e30)
        ex = jnp.exp(s - jnp.max(s, axis=-1, keepdims=True))
        sm = (ex / jnp.sum(ex, axis=-1, keepdims=True)).astype(BF)
        soft[layer, cas] = sm
        a = mm(sm, pr[:, 2 * HEAD : q3]).astype(BF)
        att[layer, cas] = a
        return a

    start_wc(0)
    wait_wc(0)
    for cas in range(2):
        start_rs(cas, x[0, cas], weight(0))

    def forward(layer, carry):
        for cas in range(2):
            start_ag(layer, cas)

        @pl.when(layer < last)
        def _():
            start_wc(layer + 1)

        @pl.when(layer + 2 < layers)
        def _():
            start_wz(layer + 2)

        for cas in range(2):
            a = attend(layer, cas)

            @pl.when(layer < last)
            def _():
                if cas == 0:
                    wait_wc(layer + 1)
                x_new = (x[layer, cas].astype(F32) + mm_nt(a, weight(layer)[:, q3:])).astype(BF)
                x[layer + 1, cas] = x_new
                start_rs(cas, x_new, weight(layer + 1))

        return carry

    lax.fori_loop(0, layers, forward, 0)

    def start_ds(cas, dyl, layer):
        ds_send[cas] = mm(dyl, weight(layer)[:, q3:]).astype(BF)
        for k in range(n_pipe - 1):
            to = peer(k)
            remote(
                ds_send.at[cas, pl.ds(pl.multiple_of(to * rb, rb), rb)],
                ds_recv.at[cas, n_pipe - 2 - k],
                rs_ssem.at[cas], rs_rsem.at[cas], to, d,
            ).start()

    def start_da(cas):
        wait_bytes(ds_recv.at[cas], rs_rsem.at[cas])
        wait_bytes(ds_recv.at[cas], rs_ssem.at[cas])
        total = ds_send[cas, own].astype(F32)
        for k in range(n_pipe - 1):
            total = total + ds_recv[cas, k].astype(F32)
        da[cas, own] = total.astype(BF)
        for k in range(n_pipe - 1):
            remote(da.at[cas, own], da.at[cas, own], ag_ssem.at[cas], ag_rsem.at[cas], peer(k), d).start()

    def backward_attend(layer, cas):
        part = da.at[cas, pl.ds(0, rows - rb)]
        wait_bytes(part, ag_rsem.at[cas])
        wait_bytes(part, ag_ssem.at[cas])
        dal = da[cas]
        pr = p[layer, cas]
        sm = soft[layer, cas]
        smf = sm.astype(F32)
        dv = mm_tn(sm, dal)
        dsm = mm_nt(dal, pr[:, 2 * HEAD : q3])
        ds = (smf * (dsm - jnp.sum(dsm * smf, axis=-1, keepdims=True)) * scale).astype(BF)
        dq = mm(ds, pr[:, HEAD : 2 * HEAD])
        dk = mm_tn(ds, pr[:, :HEAD])
        prf = pr[:, :q3].astype(F32)
        r = pr[:, q3 : q3 + 1].astype(F32) + pr[:, q3 + HEAD // 2 : q3 + HEAD // 2 + 1].astype(F32)
        dot = jnp.sum(
            dq * prf[:, :HEAD] + dk * prf[:, HEAD : 2 * HEAD] + dv * prf[:, 2 * HEAD :], axis=-1, keepdims=True
        )
        e_buf[cas, :, :HEAD] = (dq * r).astype(BF)
        e_buf[cas, :, HEAD : 2 * HEAD] = (dk * r).astype(BF)
        e_buf[cas, :, 2 * HEAD :] = (dv * r).astype(BF)
        return r * r * dot * (1.0 / dim)

    for cas in range(2):
        start_ds(cas, dy[last, cas], last)

    def backward(t, carry):
        layer = last - t

        @pl.when(t < layers)
        def _():
            for cas in range(2):
                start_da(cas)

        @pl.when((t >= 3) & (t < layers + 3))
        def _():
            la = layer + 3
            wait_bytes(gxr.at[la], gx_recv.at[la])
            gf[la] = (gx[la, pl.ds(xh, 1)][0].astype(F32) + gxr[la].astype(F32)).astype(BF)

            @pl.when((la != me) | (home_dp != d))
            def _():
                remote(gf.at[la], out.at[my_j], gf_send.at[la], gf_recv.at[0], la, home_dp).start()

            @pl.when((la == me) & (home_dp == d))
            def _():
                pltpu.make_async_copy(gf.at[la], out.at[my_j], gf_recv.at[0]).start()

        @pl.when((t >= 2) & (t < layers + 2))
        def _():
            la = layer + 2
            wait_bytes(gz.at[la], gz_recv.at[la])
            total = g[la, z, c].astype(F32)
            for k in range(n_z - 1):
                total = total + gz[la, k].astype(F32)
            gx[la] = total.astype(BF).reshape(XH, piece, q3 + HEAD)
            remote(gx.at[la, 1 - xh], gxr.at[la], gx_send.at[la], gx_recv.at[la], me, xh_peer).start()

        @pl.when((t >= 1) & (t < layers + 1))
        def _():
            la = layer + 1
            wait_bytes(gd.at[la], gc_recv.at[la])
            g[la, :, pl.ds(c, 1)] = (
                g[la, :, pl.ds(c, 1)].astype(F32) + gd[la][:, None].astype(F32)
            ).astype(BF)
            for k in range(n_z - 1):
                to_z = lax.rem(z + 1 + k, n_z)
                remote(
                    g.at[la, to_z, c], gz.at[la, n_z - 2 - k], gz_send.at[la], gz_recv.at[la], me, z_peer(k)
                ).start()

        @pl.when(t < layers)
        def _():
            wl = weight(layer)
            for cas in range(2):
                cc = backward_attend(layer, cas)

                @pl.when(layer > 0)
                def _():
                    dy_new = (
                        dy[layer, cas].astype(F32)
                        + mm_nt(e_buf[cas], wl[:, :q3])
                        - x[layer, cas].astype(F32) * cc
                    ).astype(BF)
                    dy[layer - 1, cas] = dy_new
                    start_ds(cas, dy_new, layer - 1)

            xl = x[layer].reshape(2 * rows, feat)
            dyl = dy[layer].reshape(2 * rows, feat)
            gq = mm_tn(xl, e_buf[...].reshape(2 * rows, q3)).astype(BF)
            go = mm_tn(dyl, att[layer].reshape(2 * rows, HEAD)).astype(BF)
            g[layer, :, :, :, :q3] = gq.reshape(n_z, CORES, XH * piece, q3)
            g[layer, :, :, :, q3:] = go.reshape(n_z, CORES, XH * piece, HEAD)
            remote(g.at[layer, :, 1 - c], gd.at[layer], gc_send.at[layer], gc_recv.at[layer], me, sibling).start()

        return carry

    lax.fori_loop(0, layers + 3, backward, 0)

    wait_bytes(out, gf_recv.at[0])
    full = out[...].reshape(n_pipe * piece, q3 + HEAD).astype(F32)
    gq_ref[0] = full[:, :q3]
    go_ref[0] = full[:, q3:].T

    for j in range(n_pipe):
        pp, dd, _ = spread_to(j)

        @pl.when((pp != me) | (dd != d))
        def _():
            wait_bytes(wpack.at[pl.ds(j * piece, piece)], w1_send.at[j])

    cx.wait_send()

    def drain(la, carry):
        wait_bytes(w.at[la, pl.ds(0, n_z - 1), c], wz_send.at[la])
        wait_bytes(w.at[la, :, c], wc_send.at[la])
        wait_bytes(gd.at[la], gc_send.at[la])
        wait_bytes(gz.at[la], gz_send.at[la])
        wait_bytes(gxr.at[la], gx_send.at[la])

        @pl.when((la != me) | (home_dp != d))
        def _():
            wait_bytes(gf.at[la], gf_send.at[la])

        return carry

    lax.fori_loop(0, layers, drain, 0)


def per_device(x_down, x_up, cot_down, cot_up, w_qkv, w_out, block_mask):
    n_pipe, n_dp = lax.axis_size("pipe"), lax.axis_size("dp")
    rows, dim = x_down.shape
    block = rows // block_mask.shape[0]
    row = lax.broadcasted_iota(jnp.int32, (rows, rows), 0)
    col = lax.broadcasted_iota(jnp.int32, (rows, rows), 1)
    expanded = jnp.repeat(jnp.repeat(block_mask, block, axis=0), block, axis=1)
    allowed = ((expanded == 1) & (col <= row)).astype(F32)

    feat = dim // n_pipe
    n_z = n_dp // (XH * CORES)
    piece = dim // (n_pipe * n_dp)
    group = XH * piece
    width = 4 * HEAD
    rb = rows // n_pipe
    layers = n_pipe
    any_spec = pl.BlockSpec(memory_space=pl.ANY)
    vmem = pl.BlockSpec(memory_space=pltpu.VMEM)
    dma = pltpu.SemaphoreType.DMA
    return pl.pallas_call(
        functools.partial(kernel, n_pipe, n_dp),
        out_shape=(
            jax.ShapeDtypeStruct(w_qkv.shape, F32),
            jax.ShapeDtypeStruct(w_out.shape, F32),
        ),
        in_specs=[any_spec] * 4 + [vmem] * 3,
        out_specs=(vmem, vmem),
        scratch_shapes=[
            pltpu.VMEM((n_pipe * piece, width), BF),
            pltpu.VMEM((layers, n_z, CORES, group, width), BF),
            pltpu.VMEM((layers, 2, rows, feat), BF),
            pltpu.VMEM((layers, 2, rows, feat), BF),
            pltpu.VMEM((layers, 2, rows, width), BF),
            pltpu.VMEM((layers, 2, rows, rows), BF),
            pltpu.VMEM((layers, 2, rows, HEAD), BF),
            pltpu.VMEM((2, rows, 3 * HEAD), BF),
            pltpu.VMEM((2, rows, width), BF),
            pltpu.VMEM((2, n_pipe - 1, rb, width), BF),
            pltpu.VMEM((2, rows, HEAD), BF),
            pltpu.VMEM((2, n_pipe - 1, rb, HEAD), BF),
            pltpu.VMEM((2, rows, HEAD), BF),
            pltpu.VMEM((layers, n_z, CORES, group, width), BF),
            pltpu.VMEM((layers, n_z, group, width), BF),
            pltpu.VMEM((layers, n_z - 1, group, width), BF),
            pltpu.VMEM((layers, XH, piece, width), BF),
            pltpu.VMEM((layers, piece, width), BF),
            pltpu.VMEM((layers, piece, width), BF),
            pltpu.VMEM((n_pipe, piece, width), BF),
            dma((4,)),
            dma((n_pipe,)), dma((1,)),
            dma((1,)), dma((1,)),
            dma((layers,)), dma((layers,)),
            dma((layers,)), dma((layers,)),
            dma((2,)), dma((2,)), dma((2,)), dma((2,)),
            dma((layers,)), dma((layers,)),
            dma((layers,)), dma((layers,)),
            dma((layers,)), dma((layers,)),
            dma((layers,)), dma((1,)),
        ],
        compiler_params=pltpu.CompilerParams(
            collective_id=0, has_side_effects=True, vmem_limit_bytes=48 * 1024 * 1024
        ),
    )(x_down, x_up, cot_down, cot_up, w_qkv, w_out, allowed)


def solution(mesh):
    placed = (
        P("dp", None),
        P("dp", None),
        P("dp", None),
        P("dp", None),
        P("pipe", "dp", None),
        P("pipe", None, "dp"),
        P(),
    )
    return jax.shard_map(
        per_device,
        mesh=mesh,
        in_specs=placed,
        out_specs=(P("pipe", "dp", None), P("pipe", None, "dp")),
        check_vma=False,
    )
```

```python
import functools

import jax
import jax.numpy as jnp
from jax import lax
from jax.experimental import pallas as pl
from jax.experimental.pallas import tpu as pltpu
from jax.sharding import PartitionSpec as P

BLK = 32
HEAD = 128
XH = 2
CORES = 2
BF = jnp.bfloat16
F32 = jnp.float32

NT = (((1,), (1,)), ((), ()))
TN = (((0,), (0,)), ((), ()))


def mm(a, b):
    return jnp.dot(a, b, preferred_element_type=F32)


def mm_nt(a, b):
    return lax.dot_general(a, b, NT, preferred_element_type=F32)


def mm_tn(a, b):
    return lax.dot_general(a, b, TN, preferred_element_type=F32)


def kernel(
    n_pipe,
    n_dp,
    x_down, x_up, cot_down, cot_up, wq_ref, wo_ref, mask_ref,
    gq_ref, go_ref,
    wpack, w, x, dy, agb, p1, soft, att, t1, rbuf, e_buf,
    rs_send, rs_recv, gh_send, gh_recv, ghb, ds_send, ds_recv,
    g, gd, gz, gx, out,
    load_sem, w1_send, w1_recv, wz_send, wz_recv, wc_send, wc_recv,
    rs_ssem, rs_rsem, ag_ssem, ag_rsem, ds_ssem, ds_rsem,
    gc_send, gc_recv, gz_send, gz_recv, gf_send, gf_recv,
):
    pairs = n_pipe // 2
    n_z = n_dp // (XH * CORES)
    n_i = n_dp // n_pipe
    rows = x.shape[2]
    feat = x.shape[3]
    dim = feat * n_pipe
    group = w.shape[3]
    per_block = n_pipe // XH
    rb = rows // n_pipe
    end = pairs - 1
    q3 = 3 * HEAD
    width = 4 * HEAD
    scale = HEAD ** (-0.5)

    me = lax.axis_index("pipe")
    d = lax.axis_index("dp")
    xh = d // (n_z * CORES)
    z = (d // CORES) % n_z
    c = d % CORES

    def dp_at(xh_, z_, c_):
        return xh_ * (n_z * CORES) + z_ * CORES + c_

    def peer(k):
        return lax.rem(me + 1 + k, n_pipe)

    def z_peer(k):
        return dp_at(xh, lax.rem(z + 1 + k, n_z), c)

    sibling = dp_at(xh, z, 1 - c)

    def spread_to(s):
        u = (d % n_i) * per_block + s
        return u // CORES, u % CORES

    to_pipe = d // n_i
    my_u = z * CORES + c
    home_dp = n_i * me + my_u // per_block
    my_s = my_u % per_block
    keeps_one = home_dp == d

    def remote(src, dst, ssem, rsem, pp, dd):
        return pltpu.make_async_remote_copy(
            src_ref=src, dst_ref=dst, send_sem=ssem, recv_sem=rsem,
            device_id={"pipe": pp, "dp": dd}, device_id_type=pl.DeviceIdType.MESH,
        )

    def wait_bytes(ref, sem):
        pltpu.make_async_copy(ref, ref, sem).wait()

    def layers_of(pair):
        return pl.ds(2 * pair, 2)

    barrier = pltpu.get_barrier_semaphore()

    def greet(pp, dd):
        pl.semaphore_signal(
            barrier, inc=1, device_id={"pipe": pp, "dp": dd},
            device_id_type=pl.DeviceIdType.MESH,
        )

    for s in range(per_block):
        uz, uc = spread_to(s)
        for h in range(XH):
            dd = dp_at(h, uz, uc)

            @pl.when((to_pipe != me) | (dd != d))
            def _():
                greet(to_pipe, dd)

    for j in range(n_pipe):

        @pl.when((j != me) | (home_dp != d))
        def _():
            greet(j, home_dp)

    for k in range(n_z - 1):
        greet(me, z_peer(k))
    greet(me, sibling)
    for k in range(n_pipe - 1):
        greet(peer(k), d)

    cols = pl.ds(pl.multiple_of(me * feat, feat), feat)
    top = 2 * pairs - 1
    loads = [
        pltpu.make_async_copy(x_down.at[:, cols], x.at[0, 0], load_sem.at[0]),
        pltpu.make_async_copy(x_up.at[:, cols], x.at[0, 1], load_sem.at[1]),
        pltpu.make_async_copy(cot_down.at[:, cols], dy.at[top, 0], load_sem.at[2]),
        pltpu.make_async_copy(cot_up.at[:, cols], dy.at[top, 1], load_sem.at[3]),
    ]
    for copy in loads:
        copy.start()

    wpack[:, :q3] = wq_ref[0]
    wpack[:, q3:] = wo_ref[0].astype(F32).T.astype(BF)

    pl.semaphore_wait(barrier, 3 * n_pipe + n_z - 1 - 2 * jnp.where(keeps_one, 1, 0))

    for s in range(per_block):
        uz, uc = spread_to(s)
        src = wpack.at[pl.ds(s * group, group)]
        dst = w.at[me, uz, uc]
        for h in range(XH):
            dd = dp_at(h, uz, uc)

            @pl.when((to_pipe != me) | (dd != d))
            def _():
                remote(src, dst, w1_send.at[XH * s + h], w1_recv.at[0], to_pipe, dd).start()

            @pl.when((to_pipe == me) & (dd == d))
            def _():
                pltpu.make_async_copy(src, dst, w1_recv.at[0]).start()

    wait_bytes(w.at[:, z, c], w1_recv.at[0])

    def start_wz(pair):
        mine = w.at[layers_of(pair), z, c]
        for k in range(n_z - 1):
            remote(mine, mine, wz_send.at[pair], wz_recv.at[pair], me, z_peer(k)).start()

    def start_wc(pair):
        wait_bytes(w.at[layers_of(pair), pl.ds(0, n_z - 1), c], wz_recv.at[pair])
        mine = w.at[layers_of(pair), :, c]
        remote(mine, mine, wc_send.at[pair], wc_recv.at[pair], me, sibling).start()

    def wait_wc(pair):
        wait_bytes(w.at[layers_of(pair), :, 1 - c], wc_recv.at[pair])

    def weight(layer):
        return w[layer].reshape(feat, width)

    for pair in range(pairs):
        start_wz(pair)
    for copy in loads:
        copy.wait()

    own = pl.ds(pl.multiple_of(me * rb, rb), rb)

    def scatter(src, dst, ssem, rsem):
        for k in range(n_pipe - 1):
            to = peer(k)
            remote(
                src.at[pl.ds(pl.multiple_of(to * rb, rb), rb)], dst.at[n_pipe - 2 - k], ssem, rsem, to, d
            ).start()

    def gather(ref, ssem, rsem):
        for k in range(n_pipe - 1):
            remote(ref.at[own], ref.at[own], ssem, rsem, peer(k), d).start()

    def wait_gather(ref, ssem, rsem):
        part = ref.at[pl.ds(0, rows - rb)]
        wait_bytes(part, rsem)
        wait_bytes(part, ssem)

    def start_rs(cas, xl, pair):
        xf = xl.astype(F32)
        rs_send[cas, :, :width] = mm(xl, weight(2 * pair)).astype(BF)
        rs_send[cas, :, width : width + q3] = mm(xl, weight(2 * pair + 1)[:, :q3]).astype(BF)
        sq = jnp.sum(xf * xf, axis=-1, keepdims=True)
        rs_send[cas, :, width + q3 :] = jnp.broadcast_to(sq, (rows, HEAD)).astype(BF)
        scatter(rs_send.at[cas], rs_recv.at[cas], rs_ssem.at[cas], rs_rsem.at[cas])

    def start_ag(pair, cas):
        wait_bytes(rs_recv.at[cas], rs_rsem.at[cas])
        wait_bytes(rs_recv.at[cas], rs_ssem.at[cas])
        total = rs_send[cas, own].astype(F32)
        for k in range(n_pipe - 1):
            total = total + rs_recv[cas, k].astype(F32)
        norm = total[:, width + q3 :]
        r = lax.rsqrt(norm * (1.0 / dim) + 1e-6)
        high = norm.astype(BF).astype(F32)
        lane = lax.broadcasted_iota(jnp.int32, norm.shape, 1)
        agb[pair, cas, own, :q3] = (total[:, :q3] * r[:, :1]).astype(BF)
        agb[pair, cas, own, q3 : width + q3] = total[:, q3 : width + q3].astype(BF)
        agb[pair, cas, own, width + q3 :] = jnp.where(lane < HEAD // 2, high, norm - high).astype(BF)
        gather(agb.at[pair, cas], ag_ssem.at[cas], ag_rsem.at[cas])

    def start_rs_gh(pair):
        w0 = weight(2 * pair)[:, q3:]
        gh_send[:, :q3] = mm_tn(w0, weight(2 * pair + 1)[:, :q3]).astype(BF)
        gh_send[:, q3:] = mm_tn(w0, w0).astype(BF)
        for k in range(n_pipe - 1):
            to = peer(k)
            gr = HEAD // n_pipe
            remote(
                gh_send.at[pl.ds(pl.multiple_of(to * gr, gr), gr)], gh_recv.at[n_pipe - 2 - k],
                rs_ssem.at[2], rs_rsem.at[2], to, d,
            ).start()

    gh_own = pl.ds(pl.multiple_of(me * (HEAD // n_pipe), HEAD // n_pipe), HEAD // n_pipe)

    def start_ag_gh(pair):
        wait_bytes(gh_recv, rs_rsem.at[2])
        wait_bytes(gh_recv, rs_ssem.at[2])
        total = gh_send[gh_own].astype(F32)
        for k in range(n_pipe - 1):
            total = total + gh_recv[k].astype(F32)
        ghb[pair, gh_own] = total.astype(BF)
        ref = ghb.at[pair, gh_own]
        for k in range(n_pipe - 1):
            remote(ref, ref, ag_ssem.at[2], ag_rsem.at[2], peer(k), d).start()

    def wait_ag_gh(pair):
        part = ghb.at[pair, pl.ds(0, HEAD - HEAD // n_pipe)]
        wait_bytes(part, ag_rsem.at[2])
        wait_bytes(part, ag_ssem.at[2])

    def attend(layer, cas, pr):
        s = mm_nt(pr[:, :HEAD], pr[:, HEAD : 2 * HEAD]) * scale
        s = jnp.where(mask_ref[...] > 0.5, s, -1e30)
        ex = jnp.exp(s - jnp.max(s, axis=-1, keepdims=True))
        sm = (ex / jnp.sum(ex, axis=-1, keepdims=True)).astype(BF)
        soft[layer, cas] = sm
        a = mm(sm, pr[:, 2 * HEAD : q3]).astype(BF)
        att[layer, cas] = a
        return a

    start_wc(0)
    wait_wc(0)
    for cas in range(2):
        start_rs(cas, x[0, cas], 0)
    start_rs_gh(0)

    def forward(pair, carry):
        l0 = 2 * pair
        l1 = l0 + 1
        for cas in range(2):
            start_ag(pair, cas)
        start_ag_gh(pair)

        @pl.when(pair < end)
        def _():
            start_wc(pair + 1)

        for cas in range(2):
            wait_gather(agb.at[pair, cas], ag_ssem.at[cas], ag_rsem.at[cas])
            a0 = attend(l0, cas, agb[pair, cas, :, :q3])
            n0 = (
                agb[pair, cas, :, width + q3 : width + q3 + 1].astype(F32)
                + agb[pair, cas, :, 2 * width - HEAD // 2 : 2 * width - HEAD // 2 + 1].astype(F32)
            )
            x1 = (x[l0, cas].astype(F32) + mm_nt(a0, weight(l0)[:, q3:])).astype(BF)
            x[l1, cas] = x1
            if cas == 0:
                wait_ag_gh(pair)
            agh = mm(a0, ghb[pair])
            c0 = agb[pair, cas, :, q3:width].astype(F32)
            v = agh[:, q3:]
            n1 = n0 + jnp.sum(a0.astype(F32) * (2.0 * c0 + v), axis=-1, keepdims=True)
            t1[pair, cas] = c0 + v
            r0 = lax.rsqrt(n0 * (1.0 / dim) + 1e-6)
            r1 = lax.rsqrt(jnp.maximum(n1, 0.0) * (1.0 / dim) + 1e-6)
            rbuf[l0, cas] = jnp.broadcast_to(r0, (rows, HEAD))
            rbuf[l1, cas] = jnp.broadcast_to(r1, (rows, HEAD))
            pr1 = ((agb[pair, cas, :, width : width + q3].astype(F32) + agh[:, :q3]) * r1).astype(BF)
            p1[pair, cas] = pr1
            a1 = attend(l1, cas, pr1)

            @pl.when(pair < end)
            def _():
                if cas == 0:
                    wait_wc(pair + 1)
                x2 = (x1.astype(F32) + mm_nt(a1, weight(l1)[:, q3:])).astype(BF)
                x[l1 + 1, cas] = x2
                start_rs(cas, x2, pair + 1)

        @pl.when(pair < end)
        def _():
            start_rs_gh(pair + 1)

        return carry

    lax.fori_loop(0, pairs, forward, 0)

    def start_ds(cas, dyl, pair):
        ds_send[cas, :, :HEAD] = mm(dyl, weight(2 * pair)[:, q3:]).astype(BF)
        ds_send[cas, :, HEAD:] = mm(dyl, weight(2 * pair + 1)[:, q3:]).astype(BF)
        for k in range(n_pipe - 1):
            remote(
                ds_send.at[cas], ds_recv.at[pair, cas, n_pipe - 2 - k],
                ds_ssem.at[cas], ds_rsem.at[pair, cas], peer(k), d,
            ).start()

    def attend_back(layer, cas, slot, pr, da):
        sm = soft[layer, cas]
        smf = sm.astype(F32)
        r = rbuf[layer, cas]
        dv = mm_tn(sm, da)
        dsm = mm_nt(da, pr[:, 2 * HEAD :])
        ds = (smf * (dsm - jnp.sum(dsm * smf, axis=-1, keepdims=True)) * scale).astype(BF)
        dq = mm(ds, pr[:, HEAD : 2 * HEAD])
        dk = mm_tn(ds, pr[:, :HEAD])
        prf = pr.astype(F32)
        dot = jnp.sum(
            dq * prf[:, :HEAD] + dk * prf[:, HEAD : 2 * HEAD] + dv * prf[:, 2 * HEAD :], axis=-1, keepdims=True
        )
        e_buf[slot, cas, :, :HEAD] = (dq * r).astype(BF)
        e_buf[slot, cas, :, HEAD : 2 * HEAD] = (dk * r).astype(BF)
        e_buf[slot, cas, :, 2 * HEAD :] = (dv * r).astype(BF)
        return r[:, :1] * r[:, :1] * dot * (1.0 / dim)

    for cas in range(2):
        start_ds(cas, dy[top, cas], end)

    def backward(t, carry):
        pair = end - t
        l0 = 2 * pair
        l1 = l0 + 1

        @pl.when(t < pairs)
        def _():
            for cas in range(2):
                wait_bytes(ds_recv.at[pair, cas], ds_rsem.at[pair, cas])
                wait_bytes(ds_recv.at[pair, cas], ds_ssem.at[cas])
                total = ds_send[cas].astype(F32)
                for k in range(n_pipe - 1):
                    total = total + ds_recv[pair, cas, k].astype(F32)
                cc1 = attend_back(l1, cas, 1, p1[pair, cas], total[:, HEAD:].astype(BF))
                e1 = e_buf[1, cas]
                da0 = (total[:, :HEAD] + mm_nt(e1, ghb[pair][:, :q3]) - cc1 * t1[pair, cas]).astype(BF)
                dy0 = (
                    dy[l1, cas].astype(F32) + mm_nt(e1, weight(l1)[:, :q3]) - x[l1, cas].astype(F32) * cc1
                ).astype(BF)
                dy[l0, cas] = dy0
                cc0 = attend_back(l0, cas, 0, agb[pair, cas, :, :q3], da0)

                @pl.when(pair > 0)
                def _():
                    dy_new = (
                        dy0.astype(F32)
                        + mm_nt(e_buf[0, cas], weight(l0)[:, :q3])
                        - x[l0, cas].astype(F32) * cc0
                    ).astype(BF)
                    dy[l0 - 1, cas] = dy_new
                    start_ds(cas, dy_new, pair - 1)

        @pl.when((t >= 1) & (t < pairs + 1))
        def _():
            la = pair + 1
            wait_bytes(gd.at[la], gc_recv.at[la])
            mine = (layers_of(la), slice(None), pl.ds(c, 1))
            g[mine] = (g[mine].astype(F32) + gd[la][:, :, None].astype(F32)).astype(BF)
            for k in range(n_z - 1):
                to_z = lax.rem(z + 1 + k, n_z)
                remote(
                    g.at[layers_of(la), to_z, c], gz.at[la, n_z - 2 - k],
                    gz_send.at[la], gz_recv.at[la], me, z_peer(k),
                ).start()

        @pl.when((t >= 2) & (t < pairs + 2))
        def _():
            la = pair + 2
            wait_bytes(gz.at[la], gz_recv.at[la])
            total = g[layers_of(la), z, c].astype(F32)
            for k in range(n_z - 1):
                total = total + gz[la, k].astype(F32)
            gx[la] = total.astype(BF)
            for i in range(2):
                lay = 2 * la + i

                @pl.when((lay != me) | (home_dp != d))
                def _():
                    remote(
                        gx.at[la, i], out.at[xh, my_s], gf_send.at[lay], gf_recv.at[0], lay, home_dp
                    ).start()

                @pl.when((lay == me) & (home_dp == d))
                def _():
                    pltpu.make_async_copy(gx.at[la, i], out.at[xh, my_s], gf_recv.at[0]).start()

        @pl.when(t < pairs)
        def _():
            for i in range(2):
                layer = l0 + i
                xl = x[layer].reshape(2 * rows, feat)
                dyl = dy[layer].reshape(2 * rows, feat)
                gq = mm_tn(xl, e_buf[i].reshape(2 * rows, q3)).astype(BF)
                go = mm_tn(dyl, att[layer].reshape(2 * rows, HEAD)).astype(BF)
                g[layer, :, :, :, :q3] = gq.reshape(n_z, CORES, group, q3)
                g[layer, :, :, :, q3:] = go.reshape(n_z, CORES, group, HEAD)
            remote(
                g.at[layers_of(pair), :, 1 - c], gd.at[pair], gc_send.at[pair], gc_recv.at[pair], me, sibling
            ).start()

        return carry

    lax.fori_loop(0, pairs + 2, backward, 0)

    wait_bytes(out, gf_recv.at[0])
    full = (out[0].astype(F32) + out[1].astype(F32)).reshape(per_block * group, width)
    gq_ref[0] = full[:, :q3]
    go_ref[0] = full[:, q3:].T

    for s in range(per_block):
        uz, uc = spread_to(s)
        for h in range(XH):
            dd = dp_at(h, uz, uc)

            @pl.when((to_pipe != me) | (dd != d))
            def _():
                wait_bytes(wpack.at[pl.ds(s * group, group)], w1_send.at[XH * s + h])

    def drain(la, carry):
        wait_bytes(w.at[layers_of(la), pl.ds(0, n_z - 1), c], wz_send.at[la])
        wait_bytes(w.at[layers_of(la), :, c], wc_send.at[la])
        wait_bytes(gd.at[la], gc_send.at[la])
        wait_bytes(gz.at[la], gz_send.at[la])
        for i in range(2):
            lay = 2 * la + i

            @pl.when((lay != me) | (home_dp != d))
            def _():
                wait_bytes(gx.at[la, i], gf_send.at[lay])

        return carry

    lax.fori_loop(0, pairs, drain, 0)


def per_device(x_down, x_up, cot_down, cot_up, w_qkv, w_out, block_mask):
    n_pipe, n_dp = lax.axis_size("pipe"), lax.axis_size("dp")
    rows, dim = x_down.shape
    block = rows // block_mask.shape[0]
    row = lax.broadcasted_iota(jnp.int32, (rows, rows), 0)
    col = lax.broadcasted_iota(jnp.int32, (rows, rows), 1)
    expanded = jnp.repeat(jnp.repeat(block_mask, block, axis=0), block, axis=1)
    allowed = ((expanded == 1) & (col <= row)).astype(F32)

    feat = dim // n_pipe
    n_z = n_dp // (XH * CORES)
    group = feat // (n_z * CORES)
    per_block = n_pipe // XH
    width = 4 * HEAD
    rb = rows // n_pipe
    layers = n_pipe
    pairs = layers // 2
    any_spec = pl.BlockSpec(memory_space=pl.ANY)
    vmem = pl.BlockSpec(memory_space=pltpu.VMEM)
    dma = pltpu.SemaphoreType.DMA
    return pl.pallas_call(
        functools.partial(kernel, n_pipe, n_dp),
        out_shape=(
            jax.ShapeDtypeStruct(w_qkv.shape, F32),
            jax.ShapeDtypeStruct(w_out.shape, F32),
        ),
        in_specs=[any_spec] * 4 + [vmem] * 3,
        out_specs=(vmem, vmem),
        scratch_shapes=[
            pltpu.VMEM((per_block * group, width), BF),
            pltpu.VMEM((layers, n_z, CORES, group, width), BF),
            pltpu.VMEM((layers, 2, rows, feat), BF),
            pltpu.VMEM((layers, 2, rows, feat), BF),
            pltpu.VMEM((pairs, 2, rows, 2 * width), BF),
            pltpu.VMEM((pairs, 2, rows, 3 * HEAD), BF),
            pltpu.VMEM((layers, 2, rows, rows), BF),
            pltpu.VMEM((layers, 2, rows, HEAD), BF),
            pltpu.VMEM((pairs, 2, rows, HEAD), F32),
            pltpu.VMEM((layers, 2, rows, HEAD), F32),
            pltpu.VMEM((2, 2, rows, 3 * HEAD), BF),
            pltpu.VMEM((2, rows, 2 * width), BF),
            pltpu.VMEM((2, n_pipe - 1, rb, 2 * width), BF),
            pltpu.VMEM((HEAD, width), BF),
            pltpu.VMEM((n_pipe - 1, HEAD // n_pipe, width), BF),
            pltpu.VMEM((pairs, HEAD, width), BF),
            pltpu.VMEM((2, rows, 2 * HEAD), BF),
            pltpu.VMEM((pairs, 2, n_pipe - 1, rows, 2 * HEAD), BF),
            pltpu.VMEM((layers, n_z, CORES, group, width), BF),
            pltpu.VMEM((pairs, 2, n_z, group, width), BF),
            pltpu.VMEM((pairs, n_z - 1, 2, group, width), BF),
            pltpu.VMEM((pairs, 2, group, width), BF),
            pltpu.VMEM((XH, per_block, group, width), BF),
            dma((4,)),
            dma((n_pipe,)), dma((1,)),
            dma((pairs,)), dma((pairs,)),
            dma((pairs,)), dma((pairs,)),
            dma((3,)), dma((3,)), dma((3,)), dma((3,)),
            dma((2,)), dma((pairs, 2)),
            dma((pairs,)), dma((pairs,)),
            dma((pairs,)), dma((pairs,)),
            dma((layers,)), dma((1,)),
        ],
        compiler_params=pltpu.CompilerParams(
            collective_id=0, has_side_effects=True, vmem_limit_bytes=60 * 1024 * 1024
        ),
    )(x_down, x_up, cot_down, cot_up, w_qkv, w_out, allowed)


def solution(mesh):
    placed = (
        P("dp", None),
        P("dp", None),
        P("dp", None),
        P("dp", None),
        P("pipe", "dp", None),
        P("pipe", None, "dp"),
        P(),
    )
    return jax.shard_map(
        per_device,
        mesh=mesh,
        in_specs=placed,
        out_specs=(P("pipe", "dp", None), P("pipe", None, "dp")),
        check_vma=False,
    )
```

```python
import functools

import jax
import jax.numpy as jnp
from jax import lax
from jax.experimental import pallas as pl
from jax.experimental.pallas import tpu as pltpu
from jax.sharding import PartitionSpec as P

BLK = 32
HEAD = 128
XH = 2
CORES = 2
BF = jnp.bfloat16
F32 = jnp.float32

NT = (((1,), (1,)), ((), ()))
TN = (((0,), (0,)), ((), ()))


def mm(a, b):
    return jnp.dot(a, b, preferred_element_type=F32)


def mm_nt(a, b):
    return lax.dot_general(a, b, NT, preferred_element_type=F32)


def mm_tn(a, b):
    return lax.dot_general(a, b, TN, preferred_element_type=F32)


def kernel(
    n_pipe,
    n_dp,
    x_down, x_up, cot_down, cot_up, wq_ref, wo_ref, mask_ref,
    gq_ref, go_ref,
    allowed, wpack, w, x, dy, agb, p1, soft, att, t1, rbuf, e_buf,
    rs_send, rs_recv, gh_send, gh_recv, ghb, ds_send, ds_recv, da0,
    g, gd, gz, gx, out,
    load_sem, w1_send, w1_recv, wz_send, wz_recv, wc_send, wc_recv,
    rs_ssem, rs_rsem, ag_ssem, ag_rsem, gh_ssem, gh_rsem, ha_ssem, ha_rsem, ds_ssem, ds_rsem,
    gc_send, gc_recv, gz_send, gz_recv, gf_send, gf_recv,
):
    pairs = n_pipe // 2
    n_z = n_dp // (XH * CORES)
    n_i = n_dp // n_pipe
    rows = x.shape[2]
    feat = x.shape[3]
    dim = feat * n_pipe
    group = w.shape[3]
    per_block = n_pipe // XH
    rb = rows // n_pipe
    end = pairs - 1
    q3 = 3 * HEAD
    width = 4 * HEAD
    scale = HEAD ** (-0.5)

    me = lax.axis_index("pipe")
    d = lax.axis_index("dp")
    xh = d // (n_z * CORES)
    z = (d // CORES) % n_z
    c = d % CORES

    def dp_at(xh_, z_, c_):
        return xh_ * (n_z * CORES) + z_ * CORES + c_

    def peer(k):
        return lax.rem(me + 1 + k, n_pipe)

    def z_peer(k):
        return dp_at(xh, lax.rem(z + 1 + k, n_z), c)

    sibling = dp_at(xh, z, 1 - c)

    def spread_to(s):
        u = (d % n_i) * per_block + s
        return u // CORES, u % CORES

    to_pipe = d // n_i
    my_u = z * CORES + c
    home_dp = n_i * me + my_u // per_block
    my_s = my_u % per_block
    keeps_one = home_dp == d

    def remote(src, dst, ssem, rsem, pp, dd):
        return pltpu.make_async_remote_copy(
            src_ref=src, dst_ref=dst, send_sem=ssem, recv_sem=rsem,
            device_id={"pipe": pp, "dp": dd}, device_id_type=pl.DeviceIdType.MESH,
        )

    def wait_bytes(ref, sem):
        pltpu.make_async_copy(ref, ref, sem).wait()

    def layers_of(pair):
        return pl.ds(2 * pair, 2)

    barrier = pltpu.get_barrier_semaphore()

    def greet(pp, dd):
        pl.semaphore_signal(
            barrier, inc=1, device_id={"pipe": pp, "dp": dd},
            device_id_type=pl.DeviceIdType.MESH,
        )

    for s in range(per_block):
        uz, uc = spread_to(s)
        for h in range(XH):
            dd = dp_at(h, uz, uc)

            @pl.when((to_pipe != me) | (dd != d))
            def _():
                greet(to_pipe, dd)

    for j in range(n_pipe):

        @pl.when((j != me) | (home_dp != d))
        def _():
            greet(j, home_dp)

    for k in range(n_z - 1):
        greet(me, z_peer(k))
    greet(me, sibling)
    for k in range(n_pipe - 1):
        greet(peer(k), d)

    cols = pl.ds(pl.multiple_of(me * feat, feat), feat)
    top = 2 * pairs - 1
    loads = [
        pltpu.make_async_copy(x_down.at[:, cols], x.at[0, 0], load_sem.at[0]),
        pltpu.make_async_copy(x_up.at[:, cols], x.at[0, 1], load_sem.at[1]),
        pltpu.make_async_copy(cot_down.at[:, cols], dy.at[top, 0], load_sem.at[2]),
        pltpu.make_async_copy(cot_up.at[:, cols], dy.at[top, 1], load_sem.at[3]),
    ]
    for copy in loads:
        copy.start()

    blocks = mask_ref.shape[0]
    row = lax.broadcasted_iota(jnp.int32, (rows, rows), 0)
    col = lax.broadcasted_iota(jnp.int32, (rows, rows), 1)
    read = jnp.zeros((rows, rows), jnp.int32)
    for i in range(blocks):
        for j in range(blocks):
            inside = (row // (rows // blocks) == i) & (col // (rows // blocks) == j)
            read = jnp.where(inside, mask_ref[i, j], read)
    allowed[...] = jnp.where((read == 1) & (col <= row), 1.0, 0.0)

    wpack[:, :q3] = wq_ref[0]
    wpack[:, q3:] = wo_ref[0].astype(F32).T.astype(BF)

    pl.semaphore_wait(barrier, 3 * n_pipe + n_z - 1 - 2 * jnp.where(keeps_one, 1, 0))

    for s in range(per_block):
        uz, uc = spread_to(s)
        src = wpack.at[pl.ds(s * group, group)]
        dst = w.at[me, uz, uc]
        for h in range(XH):
            dd = dp_at(h, uz, uc)

            @pl.when((to_pipe != me) | (dd != d))
            def _():
                remote(src, dst, w1_send.at[XH * s + h], w1_recv.at[0], to_pipe, dd).start()

            @pl.when((to_pipe == me) & (dd == d))
            def _():
                pltpu.make_async_copy(src, dst, w1_recv.at[0]).start()

    wait_bytes(w.at[:, z, c], w1_recv.at[0])

    def start_wz(pair):
        mine = w.at[layers_of(pair), z, c]
        for k in range(n_z - 1):
            remote(mine, mine, wz_send.at[pair], wz_recv.at[pair], me, z_peer(k)).start()

    def start_wc(pair):
        wait_bytes(w.at[layers_of(pair), pl.ds(0, n_z - 1), c], wz_recv.at[pair])
        mine = w.at[layers_of(pair), :, c]
        remote(mine, mine, wc_send.at[pair], wc_recv.at[pair], me, sibling).start()

    def wait_wc(pair):
        wait_bytes(w.at[layers_of(pair), :, 1 - c], wc_recv.at[pair])

    def weight(layer):
        return w[layer].reshape(feat, width)

    start_wz(0)
    for copy in loads:
        copy.wait()

    own = pl.ds(pl.multiple_of(me * rb, rb), rb)

    def scatter(src, dst, ssem, rsem):
        for k in range(n_pipe - 1):
            to = peer(k)
            remote(
                src.at[pl.ds(pl.multiple_of(to * rb, rb), rb)], dst.at[n_pipe - 2 - k], ssem, rsem, to, d
            ).start()

    def gather(ref, ssem, rsem):
        for k in range(n_pipe - 1):
            remote(ref.at[own], ref.at[own], ssem, rsem, peer(k), d).start()

    def wait_gather(ref, ssem, rsem):
        part = ref.at[pl.ds(0, rows - rb)]
        wait_bytes(part, rsem)
        wait_bytes(part, ssem)

    def start_rs(cas, xl, pair):
        xf = xl.astype(F32)
        rs_send[cas, :, :width] = mm(xl, weight(2 * pair)).astype(BF)
        rs_send[cas, :, width : width + q3] = mm(xl, weight(2 * pair + 1)[:, :q3]).astype(BF)
        sq = jnp.sum(xf * xf, axis=-1, keepdims=True)
        rs_send[cas, :, width + q3 :] = jnp.broadcast_to(sq, (rows, HEAD)).astype(BF)
        scatter(rs_send.at[cas], rs_recv.at[cas], rs_ssem.at[cas], rs_rsem.at[cas])

    def start_ag(pair, cas):
        wait_bytes(rs_recv.at[cas], rs_rsem.at[cas])
        wait_bytes(rs_recv.at[cas], rs_ssem.at[cas])
        total = rs_send[cas, own].astype(F32)
        for k in range(n_pipe - 1):
            total = total + rs_recv[cas, k].astype(F32)
        norm = total[:, width + q3 :]
        r = lax.rsqrt(norm * (1.0 / dim) + 1e-6)
        high = norm.astype(BF).astype(F32)
        lane = lax.broadcasted_iota(jnp.int32, norm.shape, 1)
        agb[pair, cas, own, :q3] = (total[:, :q3] * r[:, :1]).astype(BF)
        agb[pair, cas, own, q3 : width + q3] = total[:, q3 : width + q3].astype(BF)
        agb[pair, cas, own, width + q3 :] = jnp.where(lane < HEAD // 2, high, norm - high).astype(BF)
        gather(agb.at[pair, cas], ag_ssem.at[cas], ag_rsem.at[cas])

    def start_rs_gh(pair):
        w0 = weight(2 * pair)[:, q3:]
        gh_send[:, :q3] = mm_tn(w0, weight(2 * pair + 1)[:, :q3]).astype(BF)
        gh_send[:, q3:] = mm_tn(w0, w0).astype(BF)
        for k in range(n_pipe - 1):
            to = peer(k)
            gr = HEAD // n_pipe
            remote(
                gh_send.at[pl.ds(pl.multiple_of(to * gr, gr), gr)], gh_recv.at[pair, n_pipe - 2 - k],
                gh_ssem.at[0], gh_rsem.at[pair], to, d,
            ).start()

    gh_own = pl.ds(pl.multiple_of(me * (HEAD // n_pipe), HEAD // n_pipe), HEAD // n_pipe)

    def start_ag_gh(pair):
        wait_bytes(gh_recv.at[pair], gh_rsem.at[pair])
        wait_bytes(gh_recv.at[pair], gh_ssem.at[0])
        total = gh_send[gh_own].astype(F32)
        for k in range(n_pipe - 1):
            total = total + gh_recv[pair, k].astype(F32)
        ghb[pair, gh_own] = total.astype(BF)
        ref = ghb.at[pair, gh_own]
        for k in range(n_pipe - 1):
            remote(ref, ref, ha_ssem.at[pair], ha_rsem.at[pair], peer(k), d).start()

    def wait_ag_gh(pair):
        part = ghb.at[pair, pl.ds(0, HEAD - HEAD // n_pipe)]
        wait_bytes(part, ha_rsem.at[pair])
        wait_bytes(part, ha_ssem.at[pair])

    def attend(layer, cas, pr):
        s = mm_nt(pr[:, :HEAD], pr[:, HEAD : 2 * HEAD]) * scale
        s = jnp.where(allowed[...] > 0.5, s, -1e30)
        ex = jnp.exp(s - jnp.max(s, axis=-1, keepdims=True))
        sm = (ex / jnp.sum(ex, axis=-1, keepdims=True)).astype(BF)
        soft[layer, cas] = sm
        a = mm(sm, pr[:, 2 * HEAD : q3]).astype(BF)
        att[layer, cas] = a
        return a

    start_wc(0)
    if pairs > 1:
        start_wz(1)
    wait_wc(0)
    for cas in range(2):
        start_rs(cas, x[0, cas], 0)
    start_rs_gh(0)
    start_ag_gh(0)

    def forward(pair, carry):
        l0 = 2 * pair
        l1 = l0 + 1
        for cas in range(2):
            start_ag(pair, cas)

        @pl.when(pair < end)
        def _():
            start_wc(pair + 1)

            @pl.when(pair + 2 < pairs)
            def _():
                start_wz(pair + 2)

            wait_wc(pair + 1)
            start_rs_gh(pair + 1)

        for cas in range(2):
            wait_gather(agb.at[pair, cas], ag_ssem.at[cas], ag_rsem.at[cas])
            a0 = attend(l0, cas, agb[pair, cas, :, :q3])
            n0 = (
                agb[pair, cas, :, width + q3 : width + q3 + 1].astype(F32)
                + agb[pair, cas, :, 2 * width - HEAD // 2 : 2 * width - HEAD // 2 + 1].astype(F32)
            )
            x1 = (x[l0, cas].astype(F32) + mm_nt(a0, weight(l0)[:, q3:])).astype(BF)
            x[l1, cas] = x1
            if cas == 0:
                wait_ag_gh(pair)
            agh = mm(a0, ghb[pair])
            c0 = agb[pair, cas, :, q3:width].astype(F32)
            v = agh[:, q3:]
            n1 = n0 + jnp.sum(a0.astype(F32) * (2.0 * c0 + v), axis=-1, keepdims=True)
            t1[pair, cas] = c0 + v
            r0 = lax.rsqrt(n0 * (1.0 / dim) + 1e-6)
            r1 = lax.rsqrt(jnp.maximum(n1, 0.0) * (1.0 / dim) + 1e-6)
            rbuf[l0, cas] = jnp.broadcast_to(r0, (rows, HEAD))
            rbuf[l1, cas] = jnp.broadcast_to(r1, (rows, HEAD))
            pr1 = ((agb[pair, cas, :, width : width + q3].astype(F32) + agh[:, :q3]) * r1).astype(BF)
            p1[pair, cas] = pr1
            a1 = attend(l1, cas, pr1)

            @pl.when(pair < end)
            def _():
                x2 = (x1.astype(F32) + mm_nt(a1, weight(l1)[:, q3:])).astype(BF)
                x[l1 + 1, cas] = x2
                start_rs(cas, x2, pair + 1)

        @pl.when(pair < end)
        def _():
            start_ag_gh(pair + 1)

        return carry

    lax.fori_loop(0, pairs, forward, 0)

    def start_ds(cas, dyl, pair):
        ds_send[cas, :, :HEAD] = mm(dyl, weight(2 * pair)[:, q3:]).astype(BF)
        ds_send[cas, :, HEAD:] = mm(dyl, weight(2 * pair + 1)[:, q3:]).astype(BF)
        for k in range(n_pipe - 1):
            remote(
                ds_send.at[cas], ds_recv.at[pair, cas, n_pipe - 2 - k],
                ds_ssem.at[cas], ds_rsem.at[pair, cas], peer(k), d,
            ).start()

    def attend_back(layer, cas, slot, pr, da):
        sm = soft[layer, cas]
        smf = sm.astype(F32)
        r = rbuf[layer, cas]
        dv = mm_tn(sm, da)
        dsm = mm_nt(da, pr[:, 2 * HEAD :])
        ds = (smf * (dsm - jnp.sum(dsm * smf, axis=-1, keepdims=True)) * scale).astype(BF)
        dq = mm(ds, pr[:, HEAD : 2 * HEAD])
        dk = mm_tn(ds, pr[:, :HEAD])
        prf = pr.astype(F32)
        dot = jnp.sum(
            dq * prf[:, :HEAD] + dk * prf[:, HEAD : 2 * HEAD] + dv * prf[:, 2 * HEAD :], axis=-1, keepdims=True
        )
        e_buf[slot, cas, :, :HEAD] = (dq * r).astype(BF)
        e_buf[slot, cas, :, HEAD : 2 * HEAD] = (dk * r).astype(BF)
        e_buf[slot, cas, :, 2 * HEAD :] = (dv * r).astype(BF)
        return r[:, :1] * r[:, :1] * dot * (1.0 / dim)

    def weight_grads(layer, i):
        xl = x[layer].reshape(2 * rows, feat)
        dyl = dy[layer].reshape(2 * rows, feat)
        gq = mm_tn(xl, e_buf[i].reshape(2 * rows, q3)).astype(BF)
        go = mm_tn(dyl, att[layer].reshape(2 * rows, HEAD)).astype(BF)
        g[layer, :, :, :, :q3] = gq.reshape(n_z, CORES, group, q3)
        g[layer, :, :, :, q3:] = go.reshape(n_z, CORES, group, HEAD)
        remote(
            g.at[layer, :, 1 - c], gd.at[layer], gc_send.at[layer], gc_recv.at[layer], me, sibling
        ).start()

    for cas in range(2):
        start_ds(cas, dy[top, cas], end)

    def backward(t, carry):
        pair = end - t
        l0 = 2 * pair
        l1 = l0 + 1

        @pl.when(t < pairs)
        def _():
            for cas in range(2):
                wait_bytes(ds_recv.at[pair, cas], ds_rsem.at[pair, cas])
                wait_bytes(ds_recv.at[pair, cas], ds_ssem.at[cas])
                total = ds_send[cas].astype(F32)
                for k in range(n_pipe - 1):
                    total = total + ds_recv[pair, cas, k].astype(F32)
                cc1 = attend_back(l1, cas, 1, p1[pair, cas], total[:, HEAD:].astype(BF))
                e1 = e_buf[1, cas]
                da0[cas] = (total[:, :HEAD] + mm_nt(e1, ghb[pair][:, :q3]) - cc1 * t1[pair, cas]).astype(BF)
                dy[l0, cas] = (
                    dy[l1, cas].astype(F32) + mm_nt(e1, weight(l1)[:, :q3]) - x[l1, cas].astype(F32) * cc1
                ).astype(BF)

                @pl.when(pair > 0)
                def _():
                    cc0 = attend_back(l0, cas, 0, agb[pair, cas, :, :q3], da0[cas])
                    dy_new = (
                        dy[l0, cas].astype(F32)
                        + mm_nt(e_buf[0, cas], weight(l0)[:, :q3])
                        - x[l0, cas].astype(F32) * cc0
                    ).astype(BF)
                    dy[l0 - 1, cas] = dy_new
                    start_ds(cas, dy_new, pair - 1)

            @pl.when(pair == 0)
            def _():
                weight_grads(l1, 1)
                for cas in range(2):
                    attend_back(l0, cas, 0, agb[pair, cas, :, :q3], da0[cas])

        @pl.when((t >= 1) & (t < pairs + 1))
        def _():
            la = pair + 1
            for i in range(2):
                lay = 2 * la + i
                wait_bytes(gd.at[lay], gc_recv.at[lay])
                mine = (lay, slice(None), pl.ds(c, 1))
                g[mine] = (g[mine].astype(F32) + gd[lay][:, None].astype(F32)).astype(BF)
            for k in range(n_z - 1):
                to_z = lax.rem(z + 1 + k, n_z)
                remote(
                    g.at[layers_of(la), to_z, c], gz.at[la, n_z - 2 - k],
                    gz_send.at[la], gz_recv.at[la], me, z_peer(k),
                ).start()

        @pl.when((t >= 2) & (t < pairs + 2))
        def _():
            la = pair + 2
            wait_bytes(gz.at[la], gz_recv.at[la])
            total = g[layers_of(la), z, c].astype(F32)
            for k in range(n_z - 1):
                total = total + gz[la, k].astype(F32)
            gx[la] = total.astype(BF)

        @pl.when((t < pairs) & (pair > 0))
        def _():
            weight_grads(l1, 1)

        @pl.when(t < pairs)
        def _():
            weight_grads(l0, 0)

        return carry

    lax.fori_loop(0, pairs + 2, backward, 0)

    for k in range(n_pipe):
        lay = lax.rem(me + 1 + k, n_pipe)
        src = gx.at[lay // 2, lay % 2]

        @pl.when((lay != me) | (home_dp != d))
        def _():
            remote(src, out.at[xh, my_s], gf_send.at[lay], gf_recv.at[0], lay, home_dp).start()

        @pl.when((lay == me) & (home_dp == d))
        def _():
            pltpu.make_async_copy(src, out.at[xh, my_s], gf_recv.at[0]).start()

    wait_bytes(out, gf_recv.at[0])
    full = (out[0].astype(F32) + out[1].astype(F32)).reshape(per_block * group, width)
    gq_ref[0] = full[:, :q3]
    go_ref[0] = full[:, q3:].T

    for s in range(per_block):
        uz, uc = spread_to(s)
        for h in range(XH):
            dd = dp_at(h, uz, uc)

            @pl.when((to_pipe != me) | (dd != d))
            def _():
                wait_bytes(wpack.at[pl.ds(s * group, group)], w1_send.at[XH * s + h])

    def drain(la, carry):
        wait_bytes(w.at[layers_of(la), pl.ds(0, n_z - 1), c], wz_send.at[la])
        wait_bytes(w.at[layers_of(la), :, c], wc_send.at[la])
        wait_bytes(gz.at[la], gz_send.at[la])
        for i in range(2):
            lay = 2 * la + i
            wait_bytes(gd.at[lay], gc_send.at[lay])

            @pl.when((lay != me) | (home_dp != d))
            def _():
                wait_bytes(gx.at[la, i], gf_send.at[lay])

        return carry

    lax.fori_loop(0, pairs, drain, 0)


def per_device(x_down, x_up, cot_down, cot_up, w_qkv, w_out, block_mask):
    n_pipe, n_dp = lax.axis_size("pipe"), lax.axis_size("dp")
    rows, dim = x_down.shape
    feat = dim // n_pipe
    n_z = n_dp // (XH * CORES)
    group = feat // (n_z * CORES)
    per_block = n_pipe // XH
    width = 4 * HEAD
    rb = rows // n_pipe
    layers = n_pipe
    pairs = layers // 2
    any_spec = pl.BlockSpec(memory_space=pl.ANY)
    vmem = pl.BlockSpec(memory_space=pltpu.VMEM)
    dma = pltpu.SemaphoreType.DMA
    return pl.pallas_call(
        functools.partial(kernel, n_pipe, n_dp),
        out_shape=(
            jax.ShapeDtypeStruct(w_qkv.shape, F32),
            jax.ShapeDtypeStruct(w_out.shape, F32),
        ),
        in_specs=[any_spec] * 4 + [vmem] * 2 + [pl.BlockSpec(memory_space=pltpu.SMEM)],
        out_specs=(vmem, vmem),
        scratch_shapes=[
            pltpu.VMEM((rows, rows), F32),
            pltpu.VMEM((per_block * group, width), BF),
            pltpu.VMEM((layers, n_z, CORES, group, width), BF),
            pltpu.VMEM((layers, 2, rows, feat), BF),
            pltpu.VMEM((layers, 2, rows, feat), BF),
            pltpu.VMEM((pairs, 2, rows, 2 * width), BF),
            pltpu.VMEM((pairs, 2, rows, 3 * HEAD), BF),
            pltpu.VMEM((layers, 2, rows, rows), BF),
            pltpu.VMEM((layers, 2, rows, HEAD), BF),
            pltpu.VMEM((pairs, 2, rows, HEAD), F32),
            pltpu.VMEM((layers, 2, rows, HEAD), F32),
            pltpu.VMEM((2, 2, rows, 3 * HEAD), BF),
            pltpu.VMEM((2, rows, 2 * width), BF),
            pltpu.VMEM((2, n_pipe - 1, rb, 2 * width), BF),
            pltpu.VMEM((HEAD, width), BF),
            pltpu.VMEM((pairs, n_pipe - 1, HEAD // n_pipe, width), BF),
            pltpu.VMEM((pairs, HEAD, width), BF),
            pltpu.VMEM((2, rows, 2 * HEAD), BF),
            pltpu.VMEM((pairs, 2, n_pipe - 1, rows, 2 * HEAD), BF),
            pltpu.VMEM((2, rows, HEAD), BF),
            pltpu.VMEM((layers, n_z, CORES, group, width), BF),
            pltpu.VMEM((layers, n_z, group, width), BF),
            pltpu.VMEM((pairs, n_z - 1, 2, group, width), BF),
            pltpu.VMEM((pairs, 2, group, width), BF),
            pltpu.VMEM((XH, per_block, group, width), BF),
            dma((4,)),
            dma((n_pipe,)), dma((1,)),
            dma((pairs,)), dma((pairs,)),
            dma((pairs,)), dma((pairs,)),
            dma((2,)), dma((2,)), dma((2,)), dma((2,)),
            dma((1,)), dma((pairs,)), dma((pairs,)), dma((pairs,)),
            dma((2,)), dma((pairs, 2)),
            dma((layers,)), dma((layers,)),
            dma((pairs,)), dma((pairs,)),
            dma((layers,)), dma((1,)),
        ],
        compiler_params=pltpu.CompilerParams(
            collective_id=0, has_side_effects=True, vmem_limit_bytes=60 * 1024 * 1024
        ),
    )(x_down, x_up, cot_down, cot_up, w_qkv, w_out, block_mask)


def solution(mesh):
    placed = (
        P("dp", None),
        P("dp", None),
        P("dp", None),
        P("dp", None),
        P("pipe", "dp", None),
        P("pipe", None, "dp"),
        P(),
    )
    return jax.shard_map(
        per_device,
        mesh=mesh,
        in_specs=placed,
        out_specs=(P("pipe", "dp", None), P("pipe", None, "dp")),
        check_vma=False,
    )
```

```python
import functools

import jax
import jax.numpy as jnp
from jax import lax
from jax.experimental import pallas as pl
from jax.experimental.pallas import tpu as pltpu
from jax.sharding import PartitionSpec as P

BLK = 32
HEAD = 128
XH = 2
CORES = 2
BF = jnp.bfloat16
F32 = jnp.float32

NT = (((1,), (1,)), ((), ()))
TN = (((0,), (0,)), ((), ()))


def mm(a, b):
    return jnp.dot(a, b, preferred_element_type=F32)


def mm_nt(a, b):
    return lax.dot_general(a, b, NT, preferred_element_type=F32)


def mm_tn(a, b):
    return lax.dot_general(a, b, TN, preferred_element_type=F32)


def kernel(
    n_pipe,
    n_dp,
    x_down, x_up, cot_down, cot_up, wq_ref, wo_ref, mask_ref,
    gq_ref, go_ref,
    allowed, wpack, w, x, dy, agb, p1, soft, att, t1, rbuf, e_buf,
    rs_send, rs_recv, gh_send, gh_recv, ghb, ds_send, ds_recv, da0,
    g, gd, gz, gx, hp, out,
    load_sem, w1_send, w1_recv, wz_send, wz_recv, wc_send, wc_recv,
    rs_ssem, rs_rsem, ag_ssem, ag_rsem, gh_ssem, gh_rsem, ha_ssem, ha_rsem, ds_ssem, ds_rsem,
    gc_send, gc_recv, gz_send, gz_recv, hp_send, hp_recv, gf_send, gf_recv,
):
    pairs = n_pipe // 2
    n_z = n_dp // (XH * CORES)
    n_i = n_dp // n_pipe
    rows = x.shape[2]
    feat = x.shape[3]
    dim = feat * n_pipe
    group = w.shape[3]
    per_block = n_pipe // XH
    rb = rows // n_pipe
    end = pairs - 1
    q3 = 3 * HEAD
    width = 4 * HEAD
    scale = HEAD ** (-0.5)

    me = lax.axis_index("pipe")
    d = lax.axis_index("dp")
    xh = d // (n_z * CORES)
    z = (d // CORES) % n_z
    c = d % CORES

    def dp_at(xh_, z_, c_):
        return xh_ * (n_z * CORES) + z_ * CORES + c_

    def peer(k):
        return lax.rem(me + 1 + k, n_pipe)

    def z_peer(k):
        return dp_at(xh, lax.rem(z + 1 + k, n_z), c)

    sibling = dp_at(xh, z, 1 - c)

    def spread_to(s):
        u = (d % n_i) * per_block + s
        return u // CORES, u % CORES

    to_pipe = d // n_i
    my_u = z * CORES + c
    home_dp = n_i * me + my_u // per_block
    my_s = my_u % per_block
    keeps_one = home_dp == d

    def remote(src, dst, ssem, rsem, pp, dd):
        return pltpu.make_async_remote_copy(
            src_ref=src, dst_ref=dst, send_sem=ssem, recv_sem=rsem,
            device_id={"pipe": pp, "dp": dd}, device_id_type=pl.DeviceIdType.MESH,
        )

    def wait_bytes(ref, sem):
        pltpu.make_async_copy(ref, ref, sem).wait()

    def layers_of(pair):
        return pl.ds(2 * pair, 2)

    barrier = pltpu.get_barrier_semaphore()

    def greet(pp, dd):
        pl.semaphore_signal(
            barrier, inc=1, device_id={"pipe": pp, "dp": dd},
            device_id_type=pl.DeviceIdType.MESH,
        )

    for s in range(per_block):
        uz, uc = spread_to(s)
        for h in range(XH):
            dd = dp_at(h, uz, uc)

            @pl.when((to_pipe != me) | (dd != d))
            def _():
                greet(to_pipe, dd)

            @pl.when(dd != d)
            def _():
                greet(me, dd)

    for j in range(n_pipe):

        @pl.when((j != me) | (home_dp != d))
        def _():
            greet(j, home_dp)

        @pl.when(n_i * j + my_u // per_block != d)
        def _():
            greet(me, n_i * j + my_u // per_block)

    for k in range(n_z - 1):
        greet(me, z_peer(k))
    greet(me, sibling)
    for k in range(n_pipe - 1):
        greet(peer(k), d)

    cols = pl.ds(pl.multiple_of(me * feat, feat), feat)
    top = 2 * pairs - 1
    loads = [
        pltpu.make_async_copy(x_down.at[:, cols], x.at[0, 0], load_sem.at[0]),
        pltpu.make_async_copy(x_up.at[:, cols], x.at[0, 1], load_sem.at[1]),
        pltpu.make_async_copy(cot_down.at[:, cols], dy.at[top, 0], load_sem.at[2]),
        pltpu.make_async_copy(cot_up.at[:, cols], dy.at[top, 1], load_sem.at[3]),
    ]
    for copy in loads:
        copy.start()

    blocks = mask_ref.shape[0]
    row = lax.broadcasted_iota(jnp.int32, (rows, rows), 0)
    col = lax.broadcasted_iota(jnp.int32, (rows, rows), 1)
    read = jnp.zeros((rows, rows), jnp.int32)
    for i in range(blocks):
        for j in range(blocks):
            inside = (row // (rows // blocks) == i) & (col // (rows // blocks) == j)
            read = jnp.where(inside, mask_ref[i, j], read)
    allowed[...] = jnp.where((read == 1) & (col <= row), 1.0, 0.0)

    wpack[:, :q3] = wq_ref[0]
    wpack[:, q3:] = wo_ref[0].astype(F32).T.astype(BF)

    itself = jnp.where(keeps_one, 1, 0) + jnp.where(my_u // per_block == d % n_i, 1, 0)
    pl.semaphore_wait(barrier, 5 * n_pipe + n_z - 1 - 2 * itself)

    for s in range(per_block):
        uz, uc = spread_to(s)
        src = wpack.at[pl.ds(s * group, group)]
        dst = w.at[me, uz, uc]
        for h in range(XH):
            dd = dp_at(h, uz, uc)

            @pl.when((to_pipe != me) | (dd != d))
            def _():
                remote(src, dst, w1_send.at[XH * s + h], w1_recv.at[0], to_pipe, dd).start()

            @pl.when((to_pipe == me) & (dd == d))
            def _():
                pltpu.make_async_copy(src, dst, w1_recv.at[0]).start()

    wait_bytes(w.at[:, z, c], w1_recv.at[0])

    def start_wz(pair):
        mine = w.at[layers_of(pair), z, c]
        for k in range(n_z - 1):
            remote(mine, mine, wz_send.at[pair], wz_recv.at[pair], me, z_peer(k)).start()

    def start_wc(pair):
        wait_bytes(w.at[layers_of(pair), pl.ds(0, n_z - 1), c], wz_recv.at[pair])
        mine = w.at[layers_of(pair), :, c]
        remote(mine, mine, wc_send.at[pair], wc_recv.at[pair], me, sibling).start()

    def wait_wc(pair):
        wait_bytes(w.at[layers_of(pair), :, 1 - c], wc_recv.at[pair])

    def weight(layer):
        return w[layer].reshape(feat, width)

    start_wz(0)
    for copy in loads:
        copy.wait()

    own = pl.ds(pl.multiple_of(me * rb, rb), rb)

    def scatter(src, dst, ssem, rsem):
        for k in range(n_pipe - 1):
            to = peer(k)
            remote(
                src.at[pl.ds(pl.multiple_of(to * rb, rb), rb)], dst.at[n_pipe - 2 - k], ssem, rsem, to, d
            ).start()

    def gather(ref, ssem, rsem):
        for k in range(n_pipe - 1):
            remote(ref.at[own], ref.at[own], ssem, rsem, peer(k), d).start()

    def wait_gather(ref, ssem, rsem):
        part = ref.at[pl.ds(0, rows - rb)]
        wait_bytes(part, rsem)
        wait_bytes(part, ssem)

    def start_rs(cas, xl, pair):
        xf = xl.astype(F32)
        sq = jnp.sum(xf * xf, axis=-1, keepdims=True)
        first = mm(xl, weight(2 * pair))
        rs_send[cas, 0, :, :q3] = first[:, :q3].astype(BF)
        rs_send[cas, 0, :, q3:] = jnp.broadcast_to(sq, (rows, HEAD)).astype(BF)
        scatter(rs_send.at[cas, 0], rs_recv.at[cas, 0], rs_ssem.at[cas, 0], rs_rsem.at[cas, 0])
        rs_send[cas, 1, :, :HEAD] = first[:, q3:].astype(BF)
        rs_send[cas, 1, :, HEAD:] = mm(xl, weight(2 * pair + 1)[:, :q3]).astype(BF)
        scatter(rs_send.at[cas, 1], rs_recv.at[cas, 1], rs_ssem.at[cas, 1], rs_rsem.at[cas, 1])

    def start_ag(pair, cas, half):
        wait_bytes(rs_recv.at[cas, half], rs_rsem.at[cas, half])
        wait_bytes(rs_recv.at[cas, half], rs_ssem.at[cas, half])
        total = rs_send[cas, half, own].astype(F32)
        for k in range(n_pipe - 1):
            total = total + rs_recv[cas, half, k].astype(F32)
        if half == 0:
            norm = total[:, q3:]
            r = lax.rsqrt(norm * (1.0 / dim) + 1e-6)
            high = norm.astype(BF).astype(F32)
            lane = lax.broadcasted_iota(jnp.int32, norm.shape, 1)
            agb[pair, cas, 0, own, :q3] = (total[:, :q3] * r[:, :1]).astype(BF)
            agb[pair, cas, 0, own, q3:] = jnp.where(lane < HEAD // 2, high, norm - high).astype(BF)
        else:
            agb[pair, cas, 1, own] = total.astype(BF)
        gather(agb.at[pair, cas, half], ag_ssem.at[cas, half], ag_rsem.at[cas, half])

    def start_rs_gh(pair):
        w0 = weight(2 * pair)[:, q3:]
        gh_send[:, :q3] = mm_tn(w0, weight(2 * pair + 1)[:, :q3]).astype(BF)
        gh_send[:, q3:] = mm_tn(w0, w0).astype(BF)
        for k in range(n_pipe - 1):
            to = peer(k)
            gr = HEAD // n_pipe
            remote(
                gh_send.at[pl.ds(pl.multiple_of(to * gr, gr), gr)], gh_recv.at[pair, n_pipe - 2 - k],
                gh_ssem.at[0], gh_rsem.at[pair], to, d,
            ).start()

    gh_own = pl.ds(pl.multiple_of(me * (HEAD // n_pipe), HEAD // n_pipe), HEAD // n_pipe)

    def start_ag_gh(pair):
        wait_bytes(gh_recv.at[pair], gh_rsem.at[pair])
        wait_bytes(gh_recv.at[pair], gh_ssem.at[0])
        total = gh_send[gh_own].astype(F32)
        for k in range(n_pipe - 1):
            total = total + gh_recv[pair, k].astype(F32)
        ghb[pair, gh_own] = total.astype(BF)
        ref = ghb.at[pair, gh_own]
        for k in range(n_pipe - 1):
            remote(ref, ref, ha_ssem.at[pair], ha_rsem.at[pair], peer(k), d).start()

    def wait_ag_gh(pair):
        part = ghb.at[pair, pl.ds(0, HEAD - HEAD // n_pipe)]
        wait_bytes(part, ha_rsem.at[pair])
        wait_bytes(part, ha_ssem.at[pair])

    def attend(layer, cas, pr):
        s = mm_nt(pr[:, :HEAD], pr[:, HEAD : 2 * HEAD]) * scale
        s = jnp.where(allowed[...] > 0.5, s, -1e30)
        ex = jnp.exp(s - jnp.max(s, axis=-1, keepdims=True))
        sm = (ex / jnp.sum(ex, axis=-1, keepdims=True)).astype(BF)
        soft[layer, cas] = sm
        a = mm(sm, pr[:, 2 * HEAD : q3]).astype(BF)
        att[layer, cas] = a
        return a

    start_wc(0)
    if pairs > 1:
        start_wz(1)
    wait_wc(0)
    for cas in range(2):
        start_rs(cas, x[0, cas], 0)
    start_rs_gh(0)
    start_ag_gh(0)

    def start_ds(cas, dyl, pair):
        ds_send[cas, :, :HEAD] = mm(dyl, weight(2 * pair)[:, q3:]).astype(BF)
        ds_send[cas, :, HEAD:] = mm(dyl, weight(2 * pair + 1)[:, q3:]).astype(BF)
        for k in range(n_pipe - 1):
            remote(
                ds_send.at[cas], ds_recv.at[pair, cas, n_pipe - 2 - k],
                ds_ssem.at[cas], ds_rsem.at[pair, cas], peer(k), d,
            ).start()

    def forward(pair, carry):
        l0 = 2 * pair
        l1 = l0 + 1
        for cas in range(2):
            for half in range(2):
                start_ag(pair, cas, half)

        @pl.when(pair == end)
        def _():
            for cas in range(2):
                start_ds(cas, dy[top, cas], end)

        @pl.when(pair < end)
        def _():
            start_wc(pair + 1)

            @pl.when(pair + 2 < pairs)
            def _():
                start_wz(pair + 2)

            wait_wc(pair + 1)
            start_rs_gh(pair + 1)

        for cas in range(2):
            wait_gather(agb.at[pair, cas, 0], ag_ssem.at[cas, 0], ag_rsem.at[cas, 0])
            a0 = attend(l0, cas, agb[pair, cas, 0, :, :q3])
            half_lane = width - HEAD // 2
            n0 = (
                agb[pair, cas, 0, :, q3 : q3 + 1].astype(F32)
                + agb[pair, cas, 0, :, half_lane : half_lane + 1].astype(F32)
            )
            x1 = (x[l0, cas].astype(F32) + mm_nt(a0, weight(l0)[:, q3:])).astype(BF)
            x[l1, cas] = x1
            if cas == 0:
                wait_ag_gh(pair)
            agh = mm(a0, ghb[pair])
            wait_gather(agb.at[pair, cas, 1], ag_ssem.at[cas, 1], ag_rsem.at[cas, 1])
            c0 = agb[pair, cas, 1, :, :HEAD].astype(F32)
            v = agh[:, q3:]
            n1 = n0 + jnp.sum(a0.astype(F32) * (2.0 * c0 + v), axis=-1, keepdims=True)
            t1[pair, cas] = c0 + v
            r0 = lax.rsqrt(n0 * (1.0 / dim) + 1e-6)
            r1 = lax.rsqrt(jnp.maximum(n1, 0.0) * (1.0 / dim) + 1e-6)
            rbuf[l0, cas] = jnp.broadcast_to(r0, (rows, HEAD))
            rbuf[l1, cas] = jnp.broadcast_to(r1, (rows, HEAD))
            pr1 = ((agb[pair, cas, 1, :, HEAD:].astype(F32) + agh[:, :q3]) * r1).astype(BF)
            p1[pair, cas] = pr1
            a1 = attend(l1, cas, pr1)

            @pl.when(pair < end)
            def _():
                x2 = (x1.astype(F32) + mm_nt(a1, weight(l1)[:, q3:])).astype(BF)
                x[l1 + 1, cas] = x2
                start_rs(cas, x2, pair + 1)

        @pl.when(pair < end)
        def _():
            start_ag_gh(pair + 1)

        return carry

    lax.fori_loop(0, pairs, forward, 0)

    def attend_back(layer, cas, slot, pr, da):
        sm = soft[layer, cas]
        smf = sm.astype(F32)
        r = rbuf[layer, cas]
        dv = mm_tn(sm, da)
        dsm = mm_nt(da, pr[:, 2 * HEAD :])
        ds = (smf * (dsm - jnp.sum(dsm * smf, axis=-1, keepdims=True)) * scale).astype(BF)
        dq = mm(ds, pr[:, HEAD : 2 * HEAD])
        dk = mm_tn(ds, pr[:, :HEAD])
        prf = pr.astype(F32)
        dot = jnp.sum(
            dq * prf[:, :HEAD] + dk * prf[:, HEAD : 2 * HEAD] + dv * prf[:, 2 * HEAD :], axis=-1, keepdims=True
        )
        e_buf[slot, cas, :, :HEAD] = (dq * r).astype(BF)
        e_buf[slot, cas, :, HEAD : 2 * HEAD] = (dk * r).astype(BF)
        e_buf[slot, cas, :, 2 * HEAD :] = (dv * r).astype(BF)
        return r[:, :1] * r[:, :1] * dot * (1.0 / dim)

    def weight_grads(layer, i):
        xl = x[layer].reshape(2 * rows, feat)
        dyl = dy[layer].reshape(2 * rows, feat)
        gq = mm_tn(xl, e_buf[i].reshape(2 * rows, q3)).astype(BF)
        go = mm_tn(dyl, att[layer].reshape(2 * rows, HEAD)).astype(BF)
        g[layer, :, :, :, :q3] = gq.reshape(n_z, CORES, group, q3)
        g[layer, :, :, :, q3:] = go.reshape(n_z, CORES, group, HEAD)
        remote(
            g.at[layer, :, 1 - c], gd.at[layer], gc_send.at[layer], gc_recv.at[layer], me, sibling
        ).start()

    def backward(t, carry):
        pair = end - t
        l0 = 2 * pair
        l1 = l0 + 1

        @pl.when((t >= 1) & (t < pairs + 1))
        def _():
            la = pair + 1
            for i in range(2):
                lay = 2 * la + i
                wait_bytes(gd.at[lay], gc_recv.at[lay])
                mine = (lay, slice(None), pl.ds(c, 1))
                g[mine] = (g[mine].astype(F32) + gd[lay][:, None].astype(F32)).astype(BF)
            for k in range(n_z - 1):
                to_z = lax.rem(z + 1 + k, n_z)
                remote(
                    g.at[layers_of(la), to_z, c], gz.at[la, n_z - 2 - k],
                    gz_send.at[la], gz_recv.at[la], me, z_peer(k),
                ).start()

        @pl.when(t < pairs)
        def _():
            for cas in range(2):
                wait_bytes(ds_recv.at[pair, cas], ds_rsem.at[pair, cas])
                wait_bytes(ds_recv.at[pair, cas], ds_ssem.at[cas])
                total = ds_send[cas].astype(F32)
                for k in range(n_pipe - 1):
                    total = total + ds_recv[pair, cas, k].astype(F32)
                cc1 = attend_back(l1, cas, 1, p1[pair, cas], total[:, HEAD:].astype(BF))
                e1 = e_buf[1, cas]
                da0[cas] = (total[:, :HEAD] + mm_nt(e1, ghb[pair][:, :q3]) - cc1 * t1[pair, cas]).astype(BF)
                dy[l0, cas] = (
                    dy[l1, cas].astype(F32) + mm_nt(e1, weight(l1)[:, :q3]) - x[l1, cas].astype(F32) * cc1
                ).astype(BF)

                @pl.when(pair > 0)
                def _():
                    cc0 = attend_back(l0, cas, 0, agb[pair, cas, 0, :, :q3], da0[cas])
                    dy_new = (
                        dy[l0, cas].astype(F32)
                        + mm_nt(e_buf[0, cas], weight(l0)[:, :q3])
                        - x[l0, cas].astype(F32) * cc0
                    ).astype(BF)
                    dy[l0 - 1, cas] = dy_new
                    start_ds(cas, dy_new, pair - 1)

            @pl.when(pair == 0)
            def _():
                weight_grads(l1, 1)
                for cas in range(2):
                    attend_back(l0, cas, 0, agb[pair, cas, 0, :, :q3], da0[cas])

        @pl.when((t >= 2) & (t < pairs + 2))
        def _():
            la = pair + 2
            wait_bytes(gz.at[la], gz_recv.at[la])
            total = g[layers_of(la), z, c].astype(F32)
            for k in range(n_z - 1):
                total = total + gz[la, k].astype(F32)
            gx[la] = total.astype(BF)

        @pl.when((t < pairs) & (pair > 0))
        def _():
            weight_grads(l1, 1)

        @pl.when(t < pairs)
        def _():
            weight_grads(l0, 0)

        return carry

    lax.fori_loop(0, pairs + 2, backward, 0)

    for k in range(n_pipe - 1):
        to = peer(k)
        remote(gx.at[to // 2, to % 2], hp.at[me], hp_send.at[0], hp_recv.at[0], to, d).start()
    hp[pl.ds(me, 1)] = gx[pl.ds(me // 2, 1), pl.ds(me % 2, 1)][0]
    wait_bytes(hp.at[pl.ds(0, n_pipe - 1)], hp_recv.at[0])
    for k in range(n_pipe):
        pp = lax.rem(me + k, n_pipe)
        dd = n_i * pp + my_u // per_block

        @pl.when(dd != d)
        def _():
            remote(hp.at[pp], out.at[xh, my_s], gf_send.at[pp], gf_recv.at[0], me, dd).start()

        @pl.when(dd == d)
        def _():
            pltpu.make_async_copy(hp.at[pp], out.at[xh, my_s], gf_recv.at[0]).start()

    wait_bytes(out, gf_recv.at[0])
    full = (out[0].astype(F32) + out[1].astype(F32)).reshape(per_block * group, width)
    gq_ref[0] = full[:, :q3]
    go_ref[0] = full[:, q3:].T

    for s in range(per_block):
        uz, uc = spread_to(s)
        for h in range(XH):
            dd = dp_at(h, uz, uc)

            @pl.when((to_pipe != me) | (dd != d))
            def _():
                wait_bytes(wpack.at[pl.ds(s * group, group)], w1_send.at[XH * s + h])

    wait_bytes(hp.at[pl.ds(0, n_pipe - 1)], hp_send.at[0])

    def drain(la, carry):
        wait_bytes(w.at[layers_of(la), pl.ds(0, n_z - 1), c], wz_send.at[la])
        wait_bytes(w.at[layers_of(la), :, c], wc_send.at[la])
        wait_bytes(gz.at[la], gz_send.at[la])
        for i in range(2):
            lay = 2 * la + i
            wait_bytes(gd.at[lay], gc_send.at[lay])

            @pl.when(n_i * lay + my_u // per_block != d)
            def _():
                wait_bytes(hp.at[lay], gf_send.at[lay])

        return carry

    lax.fori_loop(0, pairs, drain, 0)


def per_device(x_down, x_up, cot_down, cot_up, w_qkv, w_out, block_mask):
    n_pipe, n_dp = lax.axis_size("pipe"), lax.axis_size("dp")
    rows, dim = x_down.shape
    feat = dim // n_pipe
    n_z = n_dp // (XH * CORES)
    group = feat // (n_z * CORES)
    per_block = n_pipe // XH
    width = 4 * HEAD
    rb = rows // n_pipe
    layers = n_pipe
    pairs = layers // 2
    any_spec = pl.BlockSpec(memory_space=pl.ANY)
    vmem = pl.BlockSpec(memory_space=pltpu.VMEM)
    dma = pltpu.SemaphoreType.DMA
    return pl.pallas_call(
        functools.partial(kernel, n_pipe, n_dp),
        out_shape=(
            jax.ShapeDtypeStruct(w_qkv.shape, F32),
            jax.ShapeDtypeStruct(w_out.shape, F32),
        ),
        in_specs=[any_spec] * 4 + [vmem] * 2 + [pl.BlockSpec(memory_space=pltpu.SMEM)],
        out_specs=(vmem, vmem),
        scratch_shapes=[
            pltpu.VMEM((rows, rows), F32),
            pltpu.VMEM((per_block * group, width), BF),
            pltpu.VMEM((layers, n_z, CORES, group, width), BF),
            pltpu.VMEM((layers, 2, rows, feat), BF),
            pltpu.VMEM((layers, 2, rows, feat), BF),
            pltpu.VMEM((pairs, 2, 2, rows, width), BF),
            pltpu.VMEM((pairs, 2, rows, 3 * HEAD), BF),
            pltpu.VMEM((layers, 2, rows, rows), BF),
            pltpu.VMEM((layers, 2, rows, HEAD), BF),
            pltpu.VMEM((pairs, 2, rows, HEAD), F32),
            pltpu.VMEM((layers, 2, rows, HEAD), F32),
            pltpu.VMEM((2, 2, rows, 3 * HEAD), BF),
            pltpu.VMEM((2, 2, rows, width), BF),
            pltpu.VMEM((2, 2, n_pipe - 1, rb, width), BF),
            pltpu.VMEM((HEAD, width), BF),
            pltpu.VMEM((pairs, n_pipe - 1, HEAD // n_pipe, width), BF),
            pltpu.VMEM((pairs, HEAD, width), BF),
            pltpu.VMEM((2, rows, 2 * HEAD), BF),
            pltpu.VMEM((pairs, 2, n_pipe - 1, rows, 2 * HEAD), BF),
            pltpu.VMEM((2, rows, HEAD), BF),
            pltpu.VMEM((layers, n_z, CORES, group, width), BF),
            pltpu.VMEM((layers, n_z, group, width), BF),
            pltpu.VMEM((pairs, n_z - 1, 2, group, width), BF),
            pltpu.VMEM((pairs, 2, group, width), BF),
            pltpu.VMEM((n_pipe, group, width), BF),
            pltpu.VMEM((XH, per_block, group, width), BF),
            dma((4,)),
            dma((n_pipe,)), dma((1,)),
            dma((pairs,)), dma((pairs,)),
            dma((pairs,)), dma((pairs,)),
            dma((2, 2)), dma((2, 2)), dma((2, 2)), dma((2, 2)),
            dma((1,)), dma((pairs,)), dma((pairs,)), dma((pairs,)),
            dma((2,)), dma((pairs, 2)),
            dma((layers,)), dma((layers,)),
            dma((pairs,)), dma((pairs,)),
            dma((1,)), dma((1,)),
            dma((layers,)), dma((1,)),
        ],
        compiler_params=pltpu.CompilerParams(
            collective_id=0, has_side_effects=True, vmem_limit_bytes=60 * 1024 * 1024
        ),
    )(x_down, x_up, cot_down, cot_up, w_qkv, w_out, block_mask)


def solution(mesh):
    placed = (
        P("dp", None),
        P("dp", None),
        P("dp", None),
        P("dp", None),
        P("pipe", "dp", None),
        P("pipe", None, "dp"),
        P(),
    )
    return jax.shard_map(
        per_device,
        mesh=mesh,
        in_specs=placed,
        out_specs=(P("pipe", "dp", None), P("pipe", None, "dp")),
        check_vma=False,
    )
```

```python
import functools

import jax
import jax.numpy as jnp
from jax import lax
from jax.experimental import pallas as pl
from jax.experimental.pallas import tpu as pltpu
from jax.sharding import PartitionSpec as P

BLK = 32
HEAD = 128
XH = 2
CORES = 2
BF = jnp.bfloat16
F32 = jnp.float32

NT = (((1,), (1,)), ((), ()))
TN = (((0,), (0,)), ((), ()))


def mm(a, b):
    return jnp.dot(a, b, preferred_element_type=F32)


def mm_nt(a, b):
    return lax.dot_general(a, b, NT, preferred_element_type=F32)


def mm_tn(a, b):
    return lax.dot_general(a, b, TN, preferred_element_type=F32)


def kernel(
    n_pipe,
    n_dp,
    x_down, x_up, cot_down, cot_up, wq_ref, wo_ref, mask_ref,
    gq_ref, go_ref,
    allowed, wpack, w, x, dy, agb, p1, soft, att, t1, rbuf, e_buf,
    rs_send, rs_recv, gh_send, gh_recv, ghb, ds_send, ds_recv, da0,
    g, gd, gxr, gz, gx, hp, out,
    load_sem, w1_send, w1_recv, wz_send, wz_recv, wc_send, wc_recv,
    rs_ssem, rs_rsem, ag_ssem, ag_rsem, gh_ssem, gh_rsem, ha_ssem, ha_rsem, ds_ssem, ds_rsem,
    gc_send, gc_recv, gs_send, gs_recv, gz_send, gz_recv, hp_send, hp_recv, gf_send, gf_recv,
):
    pairs = n_pipe // 2
    n_z = n_dp // (XH * CORES)
    n_i = n_dp // n_pipe
    rows = x.shape[2]
    feat = x.shape[3]
    dim = feat * n_pipe
    group = w.shape[3]
    per_block = n_pipe // XH
    rb = rows // n_pipe
    end = pairs - 1
    q3 = 3 * HEAD
    width = 4 * HEAD
    scale = HEAD ** (-0.5)

    me = lax.axis_index("pipe")
    d = lax.axis_index("dp")
    xh = d // (n_z * CORES)
    z = (d // CORES) % n_z
    c = d % CORES

    def dp_at(xh_, z_, c_):
        return xh_ * (n_z * CORES) + z_ * CORES + c_

    def peer(k):
        return lax.rem(me + 1 + k, n_pipe)

    def z_peer(k):
        return dp_at(xh, lax.rem(z + 1 + k, n_z), c)

    sibling = dp_at(xh, z, 1 - c)
    xh_peer = dp_at(1 - xh, z, c)
    piece = group // XH
    my_rows = pl.ds(pl.multiple_of(xh * piece, piece), piece)
    other_rows = pl.ds(pl.multiple_of((1 - xh) * piece, piece), piece)

    def spread_to(s):
        u = (d % n_i) * per_block + s
        return u // CORES, u % CORES

    to_pipe = d // n_i
    my_u = z * CORES + c
    home_dp = n_i * me + my_u // per_block
    my_s = my_u % per_block
    keeps_one = home_dp == d

    def remote(src, dst, ssem, rsem, pp, dd):
        return pltpu.make_async_remote_copy(
            src_ref=src, dst_ref=dst, send_sem=ssem, recv_sem=rsem,
            device_id={"pipe": pp, "dp": dd}, device_id_type=pl.DeviceIdType.MESH,
        )

    def wait_bytes(ref, sem):
        pltpu.make_async_copy(ref, ref, sem).wait()

    def layers_of(pair):
        return pl.ds(2 * pair, 2)

    barrier = pltpu.get_barrier_semaphore()

    def greet(pp, dd):
        pl.semaphore_signal(
            barrier, inc=1, device_id={"pipe": pp, "dp": dd},
            device_id_type=pl.DeviceIdType.MESH,
        )

    for s in range(per_block):
        uz, uc = spread_to(s)
        for h in range(XH):
            dd = dp_at(h, uz, uc)

            @pl.when((to_pipe != me) | (dd != d))
            def _():
                greet(to_pipe, dd)

            @pl.when(dd != d)
            def _():
                greet(me, dd)

    for j in range(n_pipe):

        @pl.when((j != me) | (home_dp != d))
        def _():
            greet(j, home_dp)

        @pl.when(n_i * j + my_u // per_block != d)
        def _():
            greet(me, n_i * j + my_u // per_block)

    for k in range(n_z - 1):
        greet(me, z_peer(k))
    greet(me, sibling)
    greet(me, xh_peer)
    for k in range(n_pipe - 1):
        greet(peer(k), d)

    cols = pl.ds(pl.multiple_of(me * feat, feat), feat)
    top = 2 * pairs - 1
    loads = [
        pltpu.make_async_copy(x_down.at[:, cols], x.at[0, 0], load_sem.at[0]),
        pltpu.make_async_copy(x_up.at[:, cols], x.at[0, 1], load_sem.at[1]),
        pltpu.make_async_copy(cot_down.at[:, cols], dy.at[top, 0], load_sem.at[2]),
        pltpu.make_async_copy(cot_up.at[:, cols], dy.at[top, 1], load_sem.at[3]),
    ]
    for copy in loads:
        copy.start()

    blocks = mask_ref.shape[0]
    row = lax.broadcasted_iota(jnp.int32, (rows, rows), 0)
    col = lax.broadcasted_iota(jnp.int32, (rows, rows), 1)
    read = jnp.zeros((rows, rows), jnp.int32)
    for i in range(blocks):
        for j in range(blocks):
            inside = (row // (rows // blocks) == i) & (col // (rows // blocks) == j)
            read = jnp.where(inside, mask_ref[i, j], read)
    allowed[...] = jnp.where((read == 1) & (col <= row), 1.0, 0.0)

    wpack[:, :q3] = wq_ref[0]
    wpack[:, q3:] = wo_ref[0].astype(F32).T.astype(BF)

    itself = jnp.where(keeps_one, 1, 0) + jnp.where(my_u // per_block == d % n_i, 1, 0)
    pl.semaphore_wait(barrier, 5 * n_pipe + n_z - 2 * itself)

    def spread():
        for s in range(per_block):
            uz, uc = spread_to(s)
            src = wpack.at[pl.ds(s * group, group)]
            dst = w.at[me, uz, uc]
            for h in range(XH):
                dd = dp_at(h, uz, uc)

                @pl.when((to_pipe != me) | (dd != d))
                def _():
                    remote(src, dst, w1_send.at[XH * s + h], w1_recv.at[me // 2], to_pipe, dd).start()

                @pl.when((to_pipe == me) & (dd == d))
                def _():
                    pltpu.make_async_copy(src, dst, w1_recv.at[me // 2]).start()

    def wait_spread(pair):
        wait_bytes(w.at[layers_of(pair), z, c], w1_recv.at[pair])

    def start_wz(layer):
        mine = w.at[layer, z, c]
        for k in range(n_z - 1):
            remote(mine, mine, wz_send.at[layer], wz_recv.at[layer], me, z_peer(k)).start()

    def start_wc(layer):
        wait_bytes(w.at[layer, pl.ds(0, n_z - 1), c], wz_recv.at[layer])
        mine = w.at[layer, :, c]
        remote(mine, mine, wc_send.at[layer], wc_recv.at[layer], me, sibling).start()

    def wait_wc(layer):
        wait_bytes(w.at[layer, :, 1 - c], wc_recv.at[layer])

    @pl.when(me < 2)
    def _():
        spread()

    wait_spread(0)
    start_wz(0)
    start_wz(1)

    @pl.when(me >= 2)
    def _():
        spread()

    def weight(layer):
        return w[layer].reshape(feat, width)

    for copy in loads:
        copy.wait()

    own = pl.ds(pl.multiple_of(me * rb, rb), rb)

    def scatter(src, dst, ssem, rsem):
        for k in range(n_pipe - 1):
            to = peer(k)
            remote(
                src.at[pl.ds(pl.multiple_of(to * rb, rb), rb)], dst.at[n_pipe - 2 - k], ssem, rsem, to, d
            ).start()

    def gather(ref, ssem, rsem):
        for k in range(n_pipe - 1):
            remote(ref.at[own], ref.at[own], ssem, rsem, peer(k), d).start()

    def wait_gather(ref, ssem, rsem):
        part = ref.at[pl.ds(0, rows - rb)]
        wait_bytes(part, rsem)
        wait_bytes(part, ssem)

    def start_rs_first(cas, xl, pair):
        xf = xl.astype(F32)
        sq = jnp.sum(xf * xf, axis=-1, keepdims=True)
        first = mm(xl, weight(2 * pair))
        rs_send[cas, 0, :, :q3] = first[:, :q3].astype(BF)
        rs_send[cas, 0, :, q3:] = jnp.broadcast_to(sq, (rows, HEAD)).astype(BF)
        scatter(rs_send.at[cas, 0], rs_recv.at[cas, 0], rs_ssem.at[cas, 0], rs_rsem.at[cas, 0])
        rs_send[cas, 1, :, :HEAD] = first[:, q3:].astype(BF)

    def start_rs_second(cas, xl, pair):
        rs_send[cas, 1, :, HEAD:] = mm(xl, weight(2 * pair + 1)[:, :q3]).astype(BF)
        scatter(rs_send.at[cas, 1], rs_recv.at[cas, 1], rs_ssem.at[cas, 1], rs_rsem.at[cas, 1])

    def start_ag(pair, cas, half):
        wait_bytes(rs_recv.at[cas, half], rs_rsem.at[cas, half])
        wait_bytes(rs_recv.at[cas, half], rs_ssem.at[cas, half])
        total = rs_send[cas, half, own].astype(F32)
        for k in range(n_pipe - 1):
            total = total + rs_recv[cas, half, k].astype(F32)
        if half == 0:
            norm = total[:, q3:]
            r = lax.rsqrt(norm * (1.0 / dim) + 1e-6)
            high = norm.astype(BF).astype(F32)
            lane = lax.broadcasted_iota(jnp.int32, norm.shape, 1)
            agb[pair, cas, 0, own, :q3] = (total[:, :q3] * r[:, :1]).astype(BF)
            agb[pair, cas, 0, own, q3:] = jnp.where(lane < HEAD // 2, high, norm - high).astype(BF)
        else:
            agb[pair, cas, 1, own] = total.astype(BF)
        gather(agb.at[pair, cas, half], ag_ssem.at[cas, half], ag_rsem.at[cas, half])

    def start_rs_gh(pair):
        w0 = weight(2 * pair)[:, q3:]
        gh_send[:, :q3] = mm_tn(w0, weight(2 * pair + 1)[:, :q3]).astype(BF)
        gh_send[:, q3:] = mm_tn(w0, w0).astype(BF)
        for k in range(n_pipe - 1):
            to = peer(k)
            gr = HEAD // n_pipe
            remote(
                gh_send.at[pl.ds(pl.multiple_of(to * gr, gr), gr)], gh_recv.at[pair, n_pipe - 2 - k],
                gh_ssem.at[0], gh_rsem.at[pair], to, d,
            ).start()

    gh_own = pl.ds(pl.multiple_of(me * (HEAD // n_pipe), HEAD // n_pipe), HEAD // n_pipe)

    def start_ag_gh(pair):
        wait_bytes(gh_recv.at[pair], gh_rsem.at[pair])
        wait_bytes(gh_recv.at[pair], gh_ssem.at[0])
        total = gh_send[gh_own].astype(F32)
        for k in range(n_pipe - 1):
            total = total + gh_recv[pair, k].astype(F32)
        ghb[pair, gh_own] = total.astype(BF)
        ref = ghb.at[pair, gh_own]
        for k in range(n_pipe - 1):
            remote(ref, ref, ha_ssem.at[pair], ha_rsem.at[pair], peer(k), d).start()

    def wait_ag_gh(pair):
        part = ghb.at[pair, pl.ds(0, HEAD - HEAD // n_pipe)]
        wait_bytes(part, ha_rsem.at[pair])
        wait_bytes(part, ha_ssem.at[pair])

    def attend(layer, cas, pr):
        s = mm_nt(pr[:, :HEAD], pr[:, HEAD : 2 * HEAD]) * scale
        s = jnp.where(allowed[...] > 0.5, s, -1e30)
        ex = jnp.exp(s - jnp.max(s, axis=-1, keepdims=True))
        sm = (ex / jnp.sum(ex, axis=-1, keepdims=True)).astype(BF)
        soft[layer, cas] = sm
        a = mm(sm, pr[:, 2 * HEAD : q3]).astype(BF)
        att[layer, cas] = a
        return a

    start_wc(0)
    wait_wc(0)
    for cas in range(2):
        start_rs_first(cas, x[0, cas], 0)
    start_wc(1)
    wait_wc(1)
    for cas in range(2):
        start_rs_second(cas, x[0, cas], 0)
    start_rs_gh(0)
    for pair in range(1, pairs):
        wait_spread(pair)
    if pairs > 1:
        start_wz(2)
        start_wz(3)

    def start_ds(cas, dyl, pair):
        ds_send[cas, :, :HEAD] = mm(dyl, weight(2 * pair)[:, q3:]).astype(BF)
        ds_send[cas, :, HEAD:] = mm(dyl, weight(2 * pair + 1)[:, q3:]).astype(BF)
        for k in range(n_pipe - 1):
            remote(
                ds_send.at[cas], ds_recv.at[pair, cas, n_pipe - 2 - k],
                ds_ssem.at[cas], ds_rsem.at[pair, cas], peer(k), d,
            ).start()

    def forward(pair, carry):
        l0 = 2 * pair
        l1 = l0 + 1
        for cas in range(2):
            for half in range(2):
                start_ag(pair, cas, half)

        @pl.when(pair == 0)
        def _():
            start_ag_gh(0)

        @pl.when(pair == end)
        def _():
            for cas in range(2):
                start_ds(cas, dy[top, cas], end)

        @pl.when(pair < end)
        def _():
            start_wc(l0 + 2)
            start_wc(l1 + 2)

            @pl.when(pair + 2 < pairs)
            def _():
                start_wz(l0 + 4)
                start_wz(l1 + 4)

            wait_wc(l0 + 2)
            wait_wc(l1 + 2)
            start_rs_gh(pair + 1)

        for cas in range(2):
            wait_gather(agb.at[pair, cas, 0], ag_ssem.at[cas, 0], ag_rsem.at[cas, 0])
            a0 = attend(l0, cas, agb[pair, cas, 0, :, :q3])
            half_lane = width - HEAD // 2
            n0 = (
                agb[pair, cas, 0, :, q3 : q3 + 1].astype(F32)
                + agb[pair, cas, 0, :, half_lane : half_lane + 1].astype(F32)
            )
            x1 = (x[l0, cas].astype(F32) + mm_nt(a0, weight(l0)[:, q3:])).astype(BF)
            x[l1, cas] = x1
            if cas == 0:
                wait_ag_gh(pair)
            agh = mm(a0, ghb[pair])
            wait_gather(agb.at[pair, cas, 1], ag_ssem.at[cas, 1], ag_rsem.at[cas, 1])
            c0 = agb[pair, cas, 1, :, :HEAD].astype(F32)
            v = agh[:, q3:]
            n1 = n0 + jnp.sum(a0.astype(F32) * (2.0 * c0 + v), axis=-1, keepdims=True)
            t1[pair, cas] = c0 + v
            r0 = lax.rsqrt(n0 * (1.0 / dim) + 1e-6)
            r1 = lax.rsqrt(jnp.maximum(n1, 0.0) * (1.0 / dim) + 1e-6)
            rbuf[l0, cas] = jnp.broadcast_to(r0, (rows, HEAD))
            rbuf[l1, cas] = jnp.broadcast_to(r1, (rows, HEAD))
            pr1 = ((agb[pair, cas, 1, :, HEAD:].astype(F32) + agh[:, :q3]) * r1).astype(BF)
            p1[pair, cas] = pr1
            a1 = attend(l1, cas, pr1)

            @pl.when(pair < end)
            def _():
                x2 = (x1.astype(F32) + mm_nt(a1, weight(l1)[:, q3:])).astype(BF)
                x[l1 + 1, cas] = x2
                start_rs_first(cas, x2, pair + 1)
                start_rs_second(cas, x2, pair + 1)

        @pl.when(pair < end)
        def _():
            start_ag_gh(pair + 1)

        return carry

    lax.fori_loop(0, pairs, forward, 0)

    def attend_back(layer, cas, slot, pr, da):
        sm = soft[layer, cas]
        smf = sm.astype(F32)
        r = rbuf[layer, cas]
        dv = mm_tn(sm, da)
        dsm = mm_nt(da, pr[:, 2 * HEAD :])
        ds = (smf * (dsm - jnp.sum(dsm * smf, axis=-1, keepdims=True)) * scale).astype(BF)
        dq = mm(ds, pr[:, HEAD : 2 * HEAD])
        dk = mm_tn(ds, pr[:, :HEAD])
        prf = pr.astype(F32)
        dot = jnp.sum(
            dq * prf[:, :HEAD] + dk * prf[:, HEAD : 2 * HEAD] + dv * prf[:, 2 * HEAD :], axis=-1, keepdims=True
        )
        e_buf[slot, cas, :, :HEAD] = (dq * r).astype(BF)
        e_buf[slot, cas, :, HEAD : 2 * HEAD] = (dk * r).astype(BF)
        e_buf[slot, cas, :, 2 * HEAD :] = (dv * r).astype(BF)
        return r[:, :1] * r[:, :1] * dot * (1.0 / dim)

    def weight_grads(layer, i):
        xl = x[layer].reshape(2 * rows, feat)
        dyl = dy[layer].reshape(2 * rows, feat)
        gq = mm_tn(xl, e_buf[i].reshape(2 * rows, q3)).astype(BF)
        go = mm_tn(dyl, att[layer].reshape(2 * rows, HEAD)).astype(BF)
        g[layer, :, :, :, :q3] = gq.reshape(n_z, CORES, group, q3)
        g[layer, :, :, :, q3:] = go.reshape(n_z, CORES, group, HEAD)
        remote(
            g.at[layer, :, 1 - c], gd.at[layer], gc_send.at[layer], gc_recv.at[layer], me, sibling
        ).start()

    def backward(t, carry):
        pair = end - t
        l0 = 2 * pair
        l1 = l0 + 1

        @pl.when((t >= 1) & (t < pairs + 1))
        def _():
            for i in (1, 0):
                lay = 2 * (pair + 1) + i
                wait_bytes(gd.at[lay], gc_recv.at[lay])
                mine = (lay, slice(None), pl.ds(c, 1))
                g[mine] = (g[mine].astype(F32) + gd[lay][:, None].astype(F32)).astype(BF)
                remote(
                    g.at[lay, :, c, other_rows], gxr.at[lay], gs_send.at[lay], gs_recv.at[lay], me, xh_peer
                ).start()

        @pl.when(t < pairs)
        def _():
            for cas in range(2):
                wait_bytes(ds_recv.at[pair, cas], ds_rsem.at[pair, cas])
                wait_bytes(ds_recv.at[pair, cas], ds_ssem.at[cas])
                total = ds_send[cas].astype(F32)
                for k in range(n_pipe - 1):
                    total = total + ds_recv[pair, cas, k].astype(F32)
                cc1 = attend_back(l1, cas, 1, p1[pair, cas], total[:, HEAD:].astype(BF))
                e1 = e_buf[1, cas]
                da0[cas] = (total[:, :HEAD] + mm_nt(e1, ghb[pair][:, :q3]) - cc1 * t1[pair, cas]).astype(BF)
                dy[l0, cas] = (
                    dy[l1, cas].astype(F32) + mm_nt(e1, weight(l1)[:, :q3]) - x[l1, cas].astype(F32) * cc1
                ).astype(BF)

                @pl.when(pair > 0)
                def _():
                    cc0 = attend_back(l0, cas, 0, agb[pair, cas, 0, :, :q3], da0[cas])
                    dy_new = (
                        dy[l0, cas].astype(F32)
                        + mm_nt(e_buf[0, cas], weight(l0)[:, :q3])
                        - x[l0, cas].astype(F32) * cc0
                    ).astype(BF)
                    dy[l0 - 1, cas] = dy_new
                    start_ds(cas, dy_new, pair - 1)

            @pl.when(pair == 0)
            def _():
                weight_grads(l1, 1)
                for cas in range(2):
                    attend_back(l0, cas, 0, agb[pair, cas, 0, :, :q3], da0[cas])

        @pl.when((t >= 1) & (t < pairs + 1))
        def _():
            for i in (1, 0):
                lay = 2 * (pair + 1) + i
                wait_bytes(gxr.at[lay], gs_recv.at[lay])
                mine = (lay, slice(None), pl.ds(c, 1), my_rows)
                g[mine] = (g[mine].astype(F32) + gxr[lay][:, None].astype(F32)).astype(BF)
                for k in range(n_z - 1):
                    to_z = lax.rem(z + 1 + k, n_z)
                    remote(
                        g.at[lay, to_z, c, my_rows], gz.at[lay, n_z - 2 - k],
                        gz_send.at[lay], gz_recv.at[lay], me, z_peer(k),
                    ).start()

        @pl.when((t >= 2) & (t < pairs + 2))
        def _():
            for i in (1, 0):
                lay = 2 * (pair + 2) + i
                wait_bytes(gz.at[lay], gz_recv.at[lay])
                total = g[lay, z, c, my_rows].astype(F32)
                for k in range(n_z - 1):
                    total = total + gz[lay, k].astype(F32)
                gx[lay] = total.astype(BF)

        @pl.when((t < pairs) & (pair > 0))
        def _():
            weight_grads(l1, 1)

        @pl.when(t < pairs)
        def _():
            weight_grads(l0, 0)

        return carry

    lax.fori_loop(0, pairs + 2, backward, 0)

    for k in range(n_pipe - 1):
        to = peer(k)
        remote(gx.at[to], hp.at[me], hp_send.at[0], hp_recv.at[0], to, d).start()
    hp[pl.ds(me, 1)] = gx[pl.ds(me, 1)]
    wait_bytes(hp.at[pl.ds(0, n_pipe - 1)], hp_recv.at[0])
    for k in range(n_pipe):
        pp = lax.rem(me + k, n_pipe)
        dd = n_i * pp + my_u // per_block

        @pl.when(dd != d)
        def _():
            remote(hp.at[pp], out.at[my_s, xh], gf_send.at[pp], gf_recv.at[0], me, dd).start()

        @pl.when(dd == d)
        def _():
            pltpu.make_async_copy(hp.at[pp], out.at[my_s, xh], gf_recv.at[0]).start()

    wait_bytes(out, gf_recv.at[0])
    full = out[...].astype(F32).reshape(per_block * group, width)
    gq_ref[0] = full[:, :q3]
    go_ref[0] = full[:, q3:].T

    for s in range(per_block):
        uz, uc = spread_to(s)
        for h in range(XH):
            dd = dp_at(h, uz, uc)

            @pl.when((to_pipe != me) | (dd != d))
            def _():
                wait_bytes(wpack.at[pl.ds(s * group, group)], w1_send.at[XH * s + h])

    wait_bytes(hp.at[pl.ds(0, n_pipe - 1)], hp_send.at[0])

    def drain(lay, carry):
        wait_bytes(w.at[lay, pl.ds(0, n_z - 1), c], wz_send.at[lay])
        wait_bytes(w.at[lay, :, c], wc_send.at[lay])
        wait_bytes(gd.at[lay], gc_send.at[lay])
        wait_bytes(gxr.at[lay], gs_send.at[lay])
        wait_bytes(gz.at[lay], gz_send.at[lay])

        @pl.when(n_i * lay + my_u // per_block != d)
        def _():
            wait_bytes(hp.at[lay], gf_send.at[lay])

        return carry

    lax.fori_loop(0, n_pipe, drain, 0)


def per_device(x_down, x_up, cot_down, cot_up, w_qkv, w_out, block_mask):
    n_pipe, n_dp = lax.axis_size("pipe"), lax.axis_size("dp")
    rows, dim = x_down.shape
    feat = dim // n_pipe
    n_z = n_dp // (XH * CORES)
    group = feat // (n_z * CORES)
    per_block = n_pipe // XH
    width = 4 * HEAD
    rb = rows // n_pipe
    layers = n_pipe
    pairs = layers // 2
    any_spec = pl.BlockSpec(memory_space=pl.ANY)
    vmem = pl.BlockSpec(memory_space=pltpu.VMEM)
    dma = pltpu.SemaphoreType.DMA
    return pl.pallas_call(
        functools.partial(kernel, n_pipe, n_dp),
        out_shape=(
            jax.ShapeDtypeStruct(w_qkv.shape, F32),
            jax.ShapeDtypeStruct(w_out.shape, F32),
        ),
        in_specs=[any_spec] * 4 + [vmem] * 2 + [pl.BlockSpec(memory_space=pltpu.SMEM)],
        out_specs=(vmem, vmem),
        scratch_shapes=[
            pltpu.VMEM((rows, rows), F32),
            pltpu.VMEM((per_block * group, width), BF),
            pltpu.VMEM((layers, n_z, CORES, group, width), BF),
            pltpu.VMEM((layers, 2, rows, feat), BF),
            pltpu.VMEM((layers, 2, rows, feat), BF),
            pltpu.VMEM((pairs, 2, 2, rows, width), BF),
            pltpu.VMEM((pairs, 2, rows, 3 * HEAD), BF),
            pltpu.VMEM((layers, 2, rows, rows), BF),
            pltpu.VMEM((layers, 2, rows, HEAD), BF),
            pltpu.VMEM((pairs, 2, rows, HEAD), F32),
            pltpu.VMEM((layers, 2, rows, HEAD), F32),
            pltpu.VMEM((2, 2, rows, 3 * HEAD), BF),
            pltpu.VMEM((2, 2, rows, width), BF),
            pltpu.VMEM((2, 2, n_pipe - 1, rb, width), BF),
            pltpu.VMEM((HEAD, width), BF),
            pltpu.VMEM((pairs, n_pipe - 1, HEAD // n_pipe, width), BF),
            pltpu.VMEM((pairs, HEAD, width), BF),
            pltpu.VMEM((2, rows, 2 * HEAD), BF),
            pltpu.VMEM((pairs, 2, n_pipe - 1, rows, 2 * HEAD), BF),
            pltpu.VMEM((2, rows, HEAD), BF),
            pltpu.VMEM((layers, n_z, CORES, group, width), BF),
            pltpu.VMEM((layers, n_z, group, width), BF),
            pltpu.VMEM((layers, n_z, group // XH, width), BF),
            pltpu.VMEM((layers, n_z - 1, group // XH, width), BF),
            pltpu.VMEM((layers, group // XH, width), BF),
            pltpu.VMEM((layers, group // XH, width), BF),
            pltpu.VMEM((per_block, XH, group // XH, width), BF),
            dma((4,)),
            dma((n_pipe,)), dma((pairs,)),
            dma((layers,)), dma((layers,)),
            dma((layers,)), dma((layers,)),
            dma((2, 2)), dma((2, 2)), dma((2, 2)), dma((2, 2)),
            dma((1,)), dma((pairs,)), dma((pairs,)), dma((pairs,)),
            dma((2,)), dma((pairs, 2)),
            dma((layers,)), dma((layers,)),
            dma((layers,)), dma((layers,)),
            dma((layers,)), dma((layers,)),
            dma((1,)), dma((1,)),
            dma((layers,)), dma((1,)),
        ],
        compiler_params=pltpu.CompilerParams(
            collective_id=0, has_side_effects=True, vmem_limit_bytes=60 * 1024 * 1024
        ),
    )(x_down, x_up, cot_down, cot_up, w_qkv, w_out, block_mask)


def solution(mesh):
    placed = (
        P("dp", None),
        P("dp", None),
        P("dp", None),
        P("dp", None),
        P("pipe", "dp", None),
        P("pipe", None, "dp"),
        P(),
    )
    return jax.shard_map(
        per_device,
        mesh=mesh,
        in_specs=placed,
        out_specs=(P("pipe", "dp", None), P("pipe", None, "dp")),
        check_vma=False,
    )
```

```python
import functools

import jax
import jax.numpy as jnp
from jax import lax
from jax.experimental import pallas as pl
from jax.experimental.pallas import tpu as pltpu
from jax.sharding import PartitionSpec as P

BLK = 32
HEAD = 128
XH = 2
CORES = 2
BF = jnp.bfloat16
F32 = jnp.float32

NT = (((1,), (1,)), ((), ()))
TN = (((0,), (0,)), ((), ()))


def mm(a, b):
    return jnp.dot(a, b, preferred_element_type=F32)


def mm_nt(a, b):
    return lax.dot_general(a, b, NT, preferred_element_type=F32)


def mm_tn(a, b):
    return lax.dot_general(a, b, TN, preferred_element_type=F32)


def kernel(
    n_pipe,
    n_dp,
    x_down, x_up, cot_down, cot_up, wq_ref, wo_ref, mask_ref,
    gq_ref, go_ref,
    allowed, wpack, w1b, w, x, dy, agb, p1, soft, att, t1, rbuf, e_buf,
    rs_send, rs_recv, gh_send, gh_recv, ghb, ds_send, ds_recv, da, da0,
    g, gd, gxr, gz, gx, hp, out,
    load_sem, w1_send, w1_recv, w2_send, w2_recv, wz_send, wz_recv, wc_send, wc_recv,
    rs_ssem, rs_rsem, ag_ssem, ag_rsem, gh_ssem, gh_rsem, ha_ssem, ha_rsem, ds_ssem, ds_rsem, da_ssem, da_rsem,
    gc_send, gc_recv, gs_send, gs_recv, gz_send, gz_recv, hp_send, hp_recv, gf_send, gf_recv,
):
    pairs = n_pipe // 2
    n_z = n_dp // (XH * CORES)
    n_i = n_dp // n_pipe
    rows = x.shape[2]
    feat = x.shape[3]
    dim = feat * n_pipe
    group = w.shape[3]
    per_block = n_pipe // XH
    rb = rows // n_pipe
    end = pairs - 1
    q3 = 3 * HEAD
    width = 4 * HEAD
    scale = HEAD ** (-0.5)

    me = lax.axis_index("pipe")
    d = lax.axis_index("dp")
    xh = d // (n_z * CORES)
    z = (d // CORES) % n_z
    c = d % CORES

    def dp_at(xh_, z_, c_):
        return xh_ * (n_z * CORES) + z_ * CORES + c_

    def peer(k):
        return lax.rem(me + 1 + k, n_pipe)

    def z_peer(k):
        return dp_at(xh, lax.rem(z + 1 + k, n_z), c)

    sibling = dp_at(xh, z, 1 - c)
    xh_peer = dp_at(1 - xh, z, c)
    piece = group // XH
    my_rows = pl.ds(pl.multiple_of(xh * piece, piece), piece)
    other_rows = pl.ds(pl.multiple_of((1 - xh) * piece, piece), piece)

    def spread_to(s):
        u = (d % n_i) * per_block + s
        return u // CORES, u % CORES

    to_pipe = d // n_i
    my_u = z * CORES + c
    my_s = my_u % per_block

    def remote(src, dst, ssem, rsem, pp, dd):
        return pltpu.make_async_remote_copy(
            src_ref=src, dst_ref=dst, send_sem=ssem, recv_sem=rsem,
            device_id={"pipe": pp, "dp": dd}, device_id_type=pl.DeviceIdType.MESH,
        )

    def wait_bytes(ref, sem):
        pltpu.make_async_copy(ref, ref, sem).wait()

    def layers_of(pair):
        return pl.ds(2 * pair, 2)

    barrier = pltpu.get_barrier_semaphore()

    def greet(pp, dd):
        pl.semaphore_signal(
            barrier, inc=1, device_id={"pipe": pp, "dp": dd},
            device_id_type=pl.DeviceIdType.MESH,
        )

    for s in range(per_block):
        uz, uc = spread_to(s)
        for h in range(XH):
            dd = dp_at(h, uz, uc)

            @pl.when(dd != d)
            def _():
                greet(me, dd)

    for j in range(n_pipe):

        @pl.when(n_i * j + my_u // per_block != d)
        def _():
            greet(me, n_i * j + my_u // per_block)

    for k in range(n_z - 1):
        greet(me, z_peer(k))
    greet(me, sibling)
    greet(me, xh_peer)
    for k in range(n_pipe - 1):
        greet(peer(k), d)
        greet(peer(k), xh_peer)

    cols = pl.ds(pl.multiple_of(me * feat, feat), feat)
    top = 2 * pairs - 1
    loads = [
        pltpu.make_async_copy(x_down.at[:, cols], x.at[0, 0], load_sem.at[0]),
        pltpu.make_async_copy(x_up.at[:, cols], x.at[0, 1], load_sem.at[1]),
        pltpu.make_async_copy(cot_down.at[:, cols], dy.at[top, 0], load_sem.at[2]),
        pltpu.make_async_copy(cot_up.at[:, cols], dy.at[top, 1], load_sem.at[3]),
    ]
    for copy in loads:
        copy.start()

    blocks = mask_ref.shape[0]
    row = lax.broadcasted_iota(jnp.int32, (rows, rows), 0)
    col = lax.broadcasted_iota(jnp.int32, (rows, rows), 1)
    read = jnp.zeros((rows, rows), jnp.int32)
    for i in range(blocks):
        for j in range(blocks):
            inside = (row // (rows // blocks) == i) & (col // (rows // blocks) == j)
            read = jnp.where(inside, mask_ref[i, j], read)
    allowed[...] = jnp.where((read == 1) & (col <= row), 1.0, 0.0)

    wpack[:, :q3] = wq_ref[0]
    wpack[:, q3:] = wo_ref[0].astype(F32).T.astype(BF)

    itself = jnp.where(my_u // per_block == d % n_i, 1, 0)
    pl.semaphore_wait(barrier, 4 * n_pipe + n_z - 1 - 2 * itself)

    for s in range(per_block):
        uz, uc = spread_to(s)
        for h in range(XH):
            dd = dp_at(h, uz, uc)
            src = wpack.at[pl.ds((XH * s + h) * piece, piece)]

            @pl.when(dd != d)
            def _():
                remote(src, w1b.at[to_pipe], w1_send.at[XH * s + h], w1_recv.at[0], me, dd).start()

            @pl.when(dd == d)
            def _():
                pltpu.make_async_copy(src, w1b.at[to_pipe], w1_recv.at[0]).start()

    wait_bytes(w1b, w1_recv.at[0])
    held = w.at[me, z, c, my_rows]
    for k in range(n_pipe - 1):
        to = peer(k)
        remote(w1b.at[to], held, w2_send.at[0], w2_recv.at[0], to, d).start()
        remote(w1b.at[to], held, w2_send.at[1], w2_recv.at[0], to, xh_peer).start()
    remote(w1b.at[me], held, w2_send.at[1], w2_recv.at[0], me, xh_peer).start()
    pltpu.make_async_copy(w1b.at[me], held, w2_recv.at[0]).start()
    wait_bytes(w.at[:, z, c], w2_recv.at[0])

    def start_wz(layer):
        mine = w.at[layer, z, c]
        for k in range(n_z - 1):
            remote(mine, mine, wz_send.at[layer], wz_recv.at[layer], me, z_peer(k)).start()

    def start_wc(layer):
        wait_bytes(w.at[layer, pl.ds(0, n_z - 1), c], wz_recv.at[layer])
        mine = w.at[layer, :, c]
        remote(mine, mine, wc_send.at[layer], wc_recv.at[layer], me, sibling).start()

    def wait_wc(layer):
        wait_bytes(w.at[layer, :, 1 - c], wc_recv.at[layer])

    start_wz(0)
    start_wz(1)

    def weight(layer):
        return w[layer].reshape(feat, width)

    for copy in loads:
        copy.wait()

    own = pl.ds(pl.multiple_of(me * rb, rb), rb)

    def scatter(src, dst, ssem, rsem):
        for k in range(n_pipe - 1):
            to = peer(k)
            remote(
                src.at[pl.ds(pl.multiple_of(to * rb, rb), rb)], dst.at[n_pipe - 2 - k], ssem, rsem, to, d
            ).start()

    def gather(ref, ssem, rsem):
        for k in range(n_pipe - 1):
            remote(ref.at[own], ref.at[own], ssem, rsem, peer(k), d).start()

    def wait_gather(ref, ssem, rsem):
        part = ref.at[pl.ds(0, rows - rb)]
        wait_bytes(part, rsem)
        wait_bytes(part, ssem)

    def start_rs_first(cas, xl, pair):
        xf = xl.astype(F32)
        sq = jnp.sum(xf * xf, axis=-1, keepdims=True)
        first = mm(xl, weight(2 * pair))
        rs_send[cas, 0, :, :q3] = first[:, :q3].astype(BF)
        rs_send[cas, 0, :, q3:] = jnp.broadcast_to(sq, (rows, HEAD)).astype(BF)
        scatter(rs_send.at[cas, 0], rs_recv.at[cas, 0], rs_ssem.at[cas, 0], rs_rsem.at[cas, 0])
        rs_send[cas, 1, :, :HEAD] = first[:, q3:].astype(BF)

    def start_rs_second(cas, xl, pair):
        rs_send[cas, 1, :, HEAD:] = mm(xl, weight(2 * pair + 1)[:, :q3]).astype(BF)
        scatter(rs_send.at[cas, 1], rs_recv.at[cas, 1], rs_ssem.at[cas, 1], rs_rsem.at[cas, 1])

    def start_ag(pair, cas, half):
        wait_bytes(rs_recv.at[cas, half], rs_rsem.at[cas, half])
        wait_bytes(rs_recv.at[cas, half], rs_ssem.at[cas, half])
        total = rs_send[cas, half, own].astype(F32)
        for k in range(n_pipe - 1):
            total = total + rs_recv[cas, half, k].astype(F32)
        if half == 0:
            norm = total[:, q3:]
            r = lax.rsqrt(norm * (1.0 / dim) + 1e-6)
            high = norm.astype(BF).astype(F32)
            lane = lax.broadcasted_iota(jnp.int32, norm.shape, 1)
            agb[pair, cas, 0, own, :q3] = (total[:, :q3] * r[:, :1]).astype(BF)
            agb[pair, cas, 0, own, q3:] = jnp.where(lane < HEAD // 2, high, norm - high).astype(BF)
        else:
            agb[pair, cas, 1, own] = total.astype(BF)
        gather(agb.at[pair, cas, half], ag_ssem.at[cas, half], ag_rsem.at[cas, half])

    def start_rs_gh(pair):
        w0 = weight(2 * pair)[:, q3:]
        gh_send[:, :q3] = mm_tn(w0, weight(2 * pair + 1)[:, :q3]).astype(BF)
        gh_send[:, q3:] = mm_tn(w0, w0).astype(BF)
        for k in range(n_pipe - 1):
            to = peer(k)
            gr = HEAD // n_pipe
            remote(
                gh_send.at[pl.ds(pl.multiple_of(to * gr, gr), gr)], gh_recv.at[pair, n_pipe - 2 - k],
                gh_ssem.at[0], gh_rsem.at[pair], to, d,
            ).start()

    gh_own = pl.ds(pl.multiple_of(me * (HEAD // n_pipe), HEAD // n_pipe), HEAD // n_pipe)

    def start_ag_gh(pair):
        wait_bytes(gh_recv.at[pair], gh_rsem.at[pair])
        wait_bytes(gh_recv.at[pair], gh_ssem.at[0])
        total = gh_send[gh_own].astype(F32)
        for k in range(n_pipe - 1):
            total = total + gh_recv[pair, k].astype(F32)
        ghb[pair, gh_own] = total.astype(BF)
        ref = ghb.at[pair, gh_own]
        for k in range(n_pipe - 1):
            remote(ref, ref, ha_ssem.at[pair], ha_rsem.at[pair], peer(k), d).start()

    def wait_ag_gh(pair):
        part = ghb.at[pair, pl.ds(0, HEAD - HEAD // n_pipe)]
        wait_bytes(part, ha_rsem.at[pair])
        wait_bytes(part, ha_ssem.at[pair])

    def attend(layer, cas, pr):
        s = mm_nt(pr[:, :HEAD], pr[:, HEAD : 2 * HEAD]) * scale
        s = jnp.where(allowed[...] > 0.5, s, -1e30)
        ex = jnp.exp(s - jnp.max(s, axis=-1, keepdims=True))
        sm = (ex / jnp.sum(ex, axis=-1, keepdims=True)).astype(BF)
        soft[layer, cas] = sm
        a = mm(sm, pr[:, 2 * HEAD : q3]).astype(BF)
        att[layer, cas] = a
        return a

    start_wc(0)
    wait_wc(0)
    for cas in range(2):
        start_rs_first(cas, x[0, cas], 0)
    start_wc(1)
    if pairs > 1:
        start_wz(2)
        start_wz(3)
    wait_wc(1)
    for cas in range(2):
        start_rs_second(cas, x[0, cas], 0)
    start_rs_gh(0)

    def start_ds(cas, dyl, pair):
        ds_send[cas, :, :HEAD] = mm(dyl, weight(2 * pair)[:, q3:]).astype(BF)
        ds_send[cas, :, HEAD:] = mm(dyl, weight(2 * pair + 1)[:, q3:]).astype(BF)
        scatter(ds_send.at[cas], ds_recv.at[cas], ds_ssem.at[cas], ds_rsem.at[cas])

    def start_da(cas):
        wait_bytes(ds_recv.at[cas], ds_rsem.at[cas])
        wait_bytes(ds_recv.at[cas], ds_ssem.at[cas])
        total = ds_send[cas, own].astype(F32)
        for k in range(n_pipe - 1):
            total = total + ds_recv[cas, k].astype(F32)
        da[cas, own] = total.astype(BF)
        gather(da.at[cas], da_ssem.at[cas], da_rsem.at[cas])

    def forward(pair, carry):
        l0 = 2 * pair
        l1 = l0 + 1
        for cas in range(2):
            for half in range(2):
                start_ag(pair, cas, half)

        @pl.when(pair == 0)
        def _():
            start_ag_gh(0)

        @pl.when(pair == end)
        def _():
            for cas in range(2):
                start_ds(cas, dy[top, cas], end)

        @pl.when(pair < end)
        def _():
            start_wc(l0 + 2)
            start_wc(l1 + 2)

            @pl.when(pair + 2 < pairs)
            def _():
                start_wz(l0 + 4)
                start_wz(l1 + 4)

            wait_wc(l0 + 2)
            wait_wc(l1 + 2)
            start_rs_gh(pair + 1)

        for cas in range(2):
            wait_gather(agb.at[pair, cas, 0], ag_ssem.at[cas, 0], ag_rsem.at[cas, 0])
            a0 = attend(l0, cas, agb[pair, cas, 0, :, :q3])
            half_lane = width - HEAD // 2
            n0 = (
                agb[pair, cas, 0, :, q3 : q3 + 1].astype(F32)
                + agb[pair, cas, 0, :, half_lane : half_lane + 1].astype(F32)
            )
            x1 = (x[l0, cas].astype(F32) + mm_nt(a0, weight(l0)[:, q3:])).astype(BF)
            x[l1, cas] = x1
            if cas == 0:
                wait_ag_gh(pair)
            agh = mm(a0, ghb[pair])
            wait_gather(agb.at[pair, cas, 1], ag_ssem.at[cas, 1], ag_rsem.at[cas, 1])
            c0 = agb[pair, cas, 1, :, :HEAD].astype(F32)
            v = agh[:, q3:]
            n1 = n0 + jnp.sum(a0.astype(F32) * (2.0 * c0 + v), axis=-1, keepdims=True)
            t1[pair, cas] = c0 + v
            r0 = lax.rsqrt(n0 * (1.0 / dim) + 1e-6)
            r1 = lax.rsqrt(jnp.maximum(n1, 0.0) * (1.0 / dim) + 1e-6)
            rbuf[l0, cas] = jnp.broadcast_to(r0, (rows, HEAD))
            rbuf[l1, cas] = jnp.broadcast_to(r1, (rows, HEAD))
            pr1 = ((agb[pair, cas, 1, :, HEAD:].astype(F32) + agh[:, :q3]) * r1).astype(BF)
            p1[pair, cas] = pr1
            a1 = attend(l1, cas, pr1)

            @pl.when(pair < end)
            def _():
                x2 = (x1.astype(F32) + mm_nt(a1, weight(l1)[:, q3:])).astype(BF)
                x[l1 + 1, cas] = x2
                start_rs_first(cas, x2, pair + 1)
                start_rs_second(cas, x2, pair + 1)

        @pl.when(pair < end)
        def _():
            start_ag_gh(pair + 1)

        return carry

    lax.fori_loop(0, pairs, forward, 0)

    def attend_back(layer, cas, slot, pr, da):
        sm = soft[layer, cas]
        smf = sm.astype(F32)
        r = rbuf[layer, cas]
        dv = mm_tn(sm, da)
        dsm = mm_nt(da, pr[:, 2 * HEAD :])
        ds = (smf * (dsm - jnp.sum(dsm * smf, axis=-1, keepdims=True)) * scale).astype(BF)
        dq = mm(ds, pr[:, HEAD : 2 * HEAD])
        dk = mm_tn(ds, pr[:, :HEAD])
        prf = pr.astype(F32)
        dot = jnp.sum(
            dq * prf[:, :HEAD] + dk * prf[:, HEAD : 2 * HEAD] + dv * prf[:, 2 * HEAD :], axis=-1, keepdims=True
        )
        e_buf[slot, cas, :, :HEAD] = (dq * r).astype(BF)
        e_buf[slot, cas, :, HEAD : 2 * HEAD] = (dk * r).astype(BF)
        e_buf[slot, cas, :, 2 * HEAD :] = (dv * r).astype(BF)
        return r[:, :1] * r[:, :1] * dot * (1.0 / dim)

    def weight_grads(layer, i):
        xl = x[layer].reshape(2 * rows, feat)
        dyl = dy[layer].reshape(2 * rows, feat)
        gq = mm_tn(xl, e_buf[i].reshape(2 * rows, q3)).astype(BF)
        go = mm_tn(dyl, att[layer].reshape(2 * rows, HEAD)).astype(BF)
        g[layer, :, :, :, :q3] = gq.reshape(n_z, CORES, group, q3)
        g[layer, :, :, :, q3:] = go.reshape(n_z, CORES, group, HEAD)
        remote(
            g.at[layer, :, 1 - c], gd.at[layer], gc_send.at[layer], gc_recv.at[layer], me, sibling
        ).start()

    def backward(t, carry):
        pair = end - t
        l0 = 2 * pair
        l1 = l0 + 1

        @pl.when(t < pairs)
        def _():
            for cas in range(2):
                start_da(cas)

        @pl.when((t >= 1) & (t < pairs + 1))
        def _():
            for i in (1, 0):
                lay = 2 * (pair + 1) + i
                wait_bytes(gd.at[lay], gc_recv.at[lay])
                mine = (lay, slice(None), pl.ds(c, 1))
                g[mine] = (g[mine].astype(F32) + gd[lay][:, None].astype(F32)).astype(BF)
                remote(
                    g.at[lay, :, c, other_rows], gxr.at[lay], gs_send.at[lay], gs_recv.at[lay], me, xh_peer
                ).start()

        @pl.when(t < pairs)
        def _():
            for cas in range(2):
                wait_gather(da.at[cas], da_ssem.at[cas], da_rsem.at[cas])
                cc1 = attend_back(l1, cas, 1, p1[pair, cas], da[cas, :, HEAD:])
                e1 = e_buf[1, cas]
                da0[cas] = (da[cas, :, :HEAD].astype(F32) + mm_nt(e1, ghb[pair][:, :q3]) - cc1 * t1[pair, cas]).astype(BF)
                dy[l0, cas] = (
                    dy[l1, cas].astype(F32) + mm_nt(e1, weight(l1)[:, :q3]) - x[l1, cas].astype(F32) * cc1
                ).astype(BF)

                @pl.when(pair > 0)
                def _():
                    cc0 = attend_back(l0, cas, 0, agb[pair, cas, 0, :, :q3], da0[cas])
                    dy_new = (
                        dy[l0, cas].astype(F32)
                        + mm_nt(e_buf[0, cas], weight(l0)[:, :q3])
                        - x[l0, cas].astype(F32) * cc0
                    ).astype(BF)
                    dy[l0 - 1, cas] = dy_new
                    start_ds(cas, dy_new, pair - 1)

            @pl.when(pair == 0)
            def _():
                weight_grads(l1, 1)
                for cas in range(2):
                    attend_back(l0, cas, 0, agb[pair, cas, 0, :, :q3], da0[cas])

        @pl.when((t >= 1) & (t < pairs + 1))
        def _():
            for i in (1, 0):
                lay = 2 * (pair + 1) + i
                wait_bytes(gxr.at[lay], gs_recv.at[lay])
                mine = (lay, slice(None), pl.ds(c, 1), my_rows)
                g[mine] = (g[mine].astype(F32) + gxr[lay][:, None].astype(F32)).astype(BF)
                for k in range(n_z - 1):
                    to_z = lax.rem(z + 1 + k, n_z)
                    remote(
                        g.at[lay, to_z, c, my_rows], gz.at[lay, n_z - 2 - k],
                        gz_send.at[lay], gz_recv.at[lay], me, z_peer(k),
                    ).start()

        @pl.when((t >= 2) & (t < pairs + 2))
        def _():
            for i in (1, 0):
                lay = 2 * (pair + 2) + i
                wait_bytes(gz.at[lay], gz_recv.at[lay])
                total = g[lay, z, c, my_rows].astype(F32)
                for k in range(n_z - 1):
                    total = total + gz[lay, k].astype(F32)
                gx[lay] = total.astype(BF)

        @pl.when((t < pairs) & (pair > 0))
        def _():
            weight_grads(l1, 1)

        @pl.when(t < pairs)
        def _():
            weight_grads(l0, 0)

        return carry

    lax.fori_loop(0, pairs + 2, backward, 0)

    for k in range(n_pipe - 1):
        to = peer(k)
        remote(gx.at[to], hp.at[me], hp_send.at[0], hp_recv.at[0], to, d).start()
    hp[pl.ds(me, 1)] = gx[pl.ds(me, 1)]
    wait_bytes(hp.at[pl.ds(0, n_pipe - 1)], hp_recv.at[0])
    for k in range(n_pipe):
        pp = lax.rem(me + k, n_pipe)
        dd = n_i * pp + my_u // per_block

        @pl.when(dd != d)
        def _():
            remote(hp.at[pp], out.at[my_s, xh], gf_send.at[pp], gf_recv.at[0], me, dd).start()

        @pl.when(dd == d)
        def _():
            pltpu.make_async_copy(hp.at[pp], out.at[my_s, xh], gf_recv.at[0]).start()

    wait_bytes(out, gf_recv.at[0])
    full = out[...].astype(F32).reshape(per_block * group, width)
    gq_ref[0] = full[:, :q3]
    go_ref[0] = full[:, q3:].T

    for s in range(per_block):
        uz, uc = spread_to(s)
        for h in range(XH):
            dd = dp_at(h, uz, uc)

            @pl.when(dd != d)
            def _():
                wait_bytes(wpack.at[pl.ds((XH * s + h) * piece, piece)], w1_send.at[XH * s + h])

    wait_bytes(w1b.at[pl.ds(0, n_pipe - 1)], w2_send.at[0])
    wait_bytes(w1b, w2_send.at[1])
    wait_bytes(hp.at[pl.ds(0, n_pipe - 1)], hp_send.at[0])

    def drain(lay, carry):
        wait_bytes(w.at[lay, pl.ds(0, n_z - 1), c], wz_send.at[lay])
        wait_bytes(w.at[lay, :, c], wc_send.at[lay])
        wait_bytes(gd.at[lay], gc_send.at[lay])
        wait_bytes(gxr.at[lay], gs_send.at[lay])
        wait_bytes(gz.at[lay], gz_send.at[lay])

        @pl.when(n_i * lay + my_u // per_block != d)
        def _():
            wait_bytes(hp.at[lay], gf_send.at[lay])

        return carry

    lax.fori_loop(0, n_pipe, drain, 0)


def per_device(x_down, x_up, cot_down, cot_up, w_qkv, w_out, block_mask):
    n_pipe, n_dp = lax.axis_size("pipe"), lax.axis_size("dp")
    rows, dim = x_down.shape
    feat = dim // n_pipe
    n_z = n_dp // (XH * CORES)
    group = feat // (n_z * CORES)
    per_block = n_pipe // XH
    width = 4 * HEAD
    rb = rows // n_pipe
    layers = n_pipe
    pairs = layers // 2
    any_spec = pl.BlockSpec(memory_space=pl.ANY)
    vmem = pl.BlockSpec(memory_space=pltpu.VMEM)
    dma = pltpu.SemaphoreType.DMA
    return pl.pallas_call(
        functools.partial(kernel, n_pipe, n_dp),
        out_shape=(
            jax.ShapeDtypeStruct(w_qkv.shape, F32),
            jax.ShapeDtypeStruct(w_out.shape, F32),
        ),
        in_specs=[any_spec] * 4 + [vmem] * 2 + [pl.BlockSpec(memory_space=pltpu.SMEM)],
        out_specs=(vmem, vmem),
        scratch_shapes=[
            pltpu.VMEM((rows, rows), F32),
            pltpu.VMEM((per_block * group, width), BF),
            pltpu.VMEM((n_pipe, group // XH, width), BF),
            pltpu.VMEM((layers, n_z, CORES, group, width), BF),
            pltpu.VMEM((layers, 2, rows, feat), BF),
            pltpu.VMEM((layers, 2, rows, feat), BF),
            pltpu.VMEM((pairs, 2, 2, rows, width), BF),
            pltpu.VMEM((pairs, 2, rows, 3 * HEAD), BF),
            pltpu.VMEM((layers, 2, rows, rows), BF),
            pltpu.VMEM((layers, 2, rows, HEAD), BF),
            pltpu.VMEM((pairs, 2, rows, HEAD), F32),
            pltpu.VMEM((layers, 2, rows, HEAD), F32),
            pltpu.VMEM((2, 2, rows, 3 * HEAD), BF),
            pltpu.VMEM((2, 2, rows, width), BF),
            pltpu.VMEM((2, 2, n_pipe - 1, rb, width), BF),
            pltpu.VMEM((HEAD, width), BF),
            pltpu.VMEM((pairs, n_pipe - 1, HEAD // n_pipe, width), BF),
            pltpu.VMEM((pairs, HEAD, width), BF),
            pltpu.VMEM((2, rows, 2 * HEAD), BF),
            pltpu.VMEM((2, n_pipe - 1, rb, 2 * HEAD), BF),
            pltpu.VMEM((2, rows, 2 * HEAD), BF),
            pltpu.VMEM((2, rows, HEAD), BF),
            pltpu.VMEM((layers, n_z, CORES, group, width), BF),
            pltpu.VMEM((layers, n_z, group, width), BF),
            pltpu.VMEM((layers, n_z, group // XH, width), BF),
            pltpu.VMEM((layers, n_z - 1, group // XH, width), BF),
            pltpu.VMEM((layers, group // XH, width), BF),
            pltpu.VMEM((layers, group // XH, width), BF),
            pltpu.VMEM((per_block, XH, group // XH, width), BF),
            dma((4,)),
            dma((n_pipe,)), dma((1,)),
            dma((2,)), dma((1,)),
            dma((layers,)), dma((layers,)),
            dma((layers,)), dma((layers,)),
            dma((2, 2)), dma((2, 2)), dma((2, 2)), dma((2, 2)),
            dma((1,)), dma((pairs,)), dma((pairs,)), dma((pairs,)),
            dma((2,)), dma((2,)), dma((2,)), dma((2,)),
            dma((layers,)), dma((layers,)),
            dma((layers,)), dma((layers,)),
            dma((layers,)), dma((layers,)),
            dma((1,)), dma((1,)),
            dma((layers,)), dma((1,)),
        ],
        compiler_params=pltpu.CompilerParams(
            collective_id=0, has_side_effects=True, vmem_limit_bytes=60 * 1024 * 1024
        ),
    )(x_down, x_up, cot_down, cot_up, w_qkv, w_out, block_mask)


def solution(mesh):
    placed = (
        P("dp", None),
        P("dp", None),
        P("dp", None),
        P("dp", None),
        P("pipe", "dp", None),
        P("pipe", None, "dp"),
        P(),
    )
    return jax.shard_map(
        per_device,
        mesh=mesh,
        in_specs=placed,
        out_specs=(P("pipe", "dp", None), P("pipe", None, "dp")),
        check_vma=False,
    )
```

```python
import functools

import jax
import jax.numpy as jnp
from jax import lax
from jax.experimental import pallas as pl
from jax.experimental.pallas import tpu as pltpu
from jax.sharding import PartitionSpec as P

BLK = 32
HEAD = 128
XH = 2
CORES = 2
BF = jnp.bfloat16
F32 = jnp.float32

NT = (((1,), (1,)), ((), ()))
TN = (((0,), (0,)), ((), ()))


def mm(a, b):
    return jnp.dot(a, b, preferred_element_type=F32)


def mm_nt(a, b):
    return lax.dot_general(a, b, NT, preferred_element_type=F32)


def mm_tn(a, b):
    return lax.dot_general(a, b, TN, preferred_element_type=F32)


def kernel(
    n_pipe,
    n_dp,
    x_down, x_up, cot_down, cot_up, wq_ref, wo_ref, mask_ref,
    gq_ref, go_ref,
    allowed, wpack, w1b, w, x, dy, agb, p1, soft, att, t1, rbuf, e_buf,
    rs_send, rs_recv, gh_send, gh_recv, ghb, ds_send, ds_recv, da, da0,
    g, gd, gxr, gz, gx, hp, out,
    load_sem, w1_send, w1_recv, w2_send, w2_recv, wz_send, wz_recv, wx_send, wx_recv, wc_send, wc_recv,
    rs_ssem, rs_rsem, ag_ssem, ag_rsem, gh_ssem, gh_rsem, ha_ssem, ha_rsem, ds_ssem, ds_rsem, da_ssem, da_rsem,
    gc_send, gc_recv, gs_send, gs_recv, gz_send, gz_recv, hp_send, hp_recv, gf_send, gf_recv,
):
    pairs = n_pipe // 2
    n_z = n_dp // (XH * CORES)
    n_i = n_dp // n_pipe
    rows = x.shape[2]
    feat = x.shape[3]
    dim = feat * n_pipe
    group = w.shape[3]
    per_block = n_pipe // XH
    rb = rows // n_pipe
    end = pairs - 1
    q3 = 3 * HEAD
    width = 4 * HEAD
    scale = HEAD ** (-0.5)

    me = lax.axis_index("pipe")
    d = lax.axis_index("dp")
    xh = d // (n_z * CORES)
    z = (d // CORES) % n_z
    c = d % CORES

    def dp_at(xh_, z_, c_):
        return xh_ * (n_z * CORES) + z_ * CORES + c_

    def peer(k):
        return lax.rem(me + 1 + k, n_pipe)

    def z_peer(k):
        return dp_at(xh, lax.rem(z + 1 + k, n_z), c)

    sibling = dp_at(xh, z, 1 - c)
    xh_peer = dp_at(1 - xh, z, c)
    piece = group // XH
    my_rows = pl.ds(pl.multiple_of(xh * piece, piece), piece)
    other_rows = pl.ds(pl.multiple_of((1 - xh) * piece, piece), piece)

    def spread_to(s):
        u = (d % n_i) * per_block + s
        return u // CORES, u % CORES

    to_pipe = d // n_i
    my_u = z * CORES + c
    my_s = my_u % per_block

    def remote(src, dst, ssem, rsem, pp, dd):
        return pltpu.make_async_remote_copy(
            src_ref=src, dst_ref=dst, send_sem=ssem, recv_sem=rsem,
            device_id={"pipe": pp, "dp": dd}, device_id_type=pl.DeviceIdType.MESH,
        )

    def wait_bytes(ref, sem):
        pltpu.make_async_copy(ref, ref, sem).wait()

    def layers_of(pair):
        return pl.ds(2 * pair, 2)

    barrier = pltpu.get_barrier_semaphore()

    def greet(pp, dd):
        pl.semaphore_signal(
            barrier, inc=1, device_id={"pipe": pp, "dp": dd},
            device_id_type=pl.DeviceIdType.MESH,
        )

    for s in range(per_block):
        uz, uc = spread_to(s)
        for h in range(XH):
            dd = dp_at(h, uz, uc)

            @pl.when(dd != d)
            def _():
                greet(me, dd)

    for j in range(n_pipe):

        @pl.when(n_i * j + my_u // per_block != d)
        def _():
            greet(me, n_i * j + my_u // per_block)

    for k in range(n_z - 1):
        greet(me, z_peer(k))
    greet(me, sibling)
    greet(me, xh_peer)
    for k in range(n_pipe - 1):
        greet(peer(k), d)

    cols = pl.ds(pl.multiple_of(me * feat, feat), feat)
    top = 2 * pairs - 1
    loads = [
        pltpu.make_async_copy(x_down.at[:, cols], x.at[0, 0], load_sem.at[0]),
        pltpu.make_async_copy(x_up.at[:, cols], x.at[0, 1], load_sem.at[1]),
        pltpu.make_async_copy(cot_down.at[:, cols], dy.at[top, 0], load_sem.at[2]),
        pltpu.make_async_copy(cot_up.at[:, cols], dy.at[top, 1], load_sem.at[3]),
    ]
    for copy in loads:
        copy.start()

    blocks = mask_ref.shape[0]
    row = lax.broadcasted_iota(jnp.int32, (rows, rows), 0)
    col = lax.broadcasted_iota(jnp.int32, (rows, rows), 1)
    read = jnp.zeros((rows, rows), jnp.int32)
    for i in range(blocks):
        for j in range(blocks):
            inside = (row // (rows // blocks) == i) & (col // (rows // blocks) == j)
            read = jnp.where(inside, mask_ref[i, j], read)
    allowed[...] = jnp.where((read == 1) & (col <= row), 1.0, 0.0)

    wpack[:, :q3] = wq_ref[0]
    wpack[:, q3:] = wo_ref[0].astype(F32).T.astype(BF)

    itself = jnp.where(my_u // per_block == d % n_i, 1, 0)
    pl.semaphore_wait(barrier, 3 * n_pipe + n_z - 2 * itself)

    for s in range(per_block):
        uz, uc = spread_to(s)
        for h in range(XH):
            dd = dp_at(h, uz, uc)
            src = wpack.at[pl.ds((XH * s + h) * piece, piece)]

            @pl.when(dd != d)
            def _():
                remote(src, w1b.at[to_pipe], w1_send.at[XH * s + h], w1_recv.at[0], me, dd).start()

            @pl.when(dd == d)
            def _():
                pltpu.make_async_copy(src, w1b.at[to_pipe], w1_recv.at[0]).start()

    wait_bytes(w1b, w1_recv.at[0])
    held = w.at[me, z, c, my_rows]
    for k in range(n_pipe - 1):
        to = peer(k)
        remote(w1b.at[to], held, w2_send.at[0], w2_recv.at[0], to, d).start()
    pltpu.make_async_copy(w1b.at[me], held, w2_recv.at[0]).start()
    wait_bytes(w.at[:, z, c, my_rows], w2_recv.at[0])

    def start_wz(layer):
        mine = w.at[layer, z, c, my_rows]
        for k in range(n_z - 1):
            remote(mine, mine, wz_send.at[layer], wz_recv.at[layer], me, z_peer(k)).start()

    def start_wx(layer):
        wait_bytes(w.at[layer, pl.ds(0, n_z - 1), c, my_rows], wz_recv.at[layer])
        mine = w.at[layer, :, c, my_rows]
        remote(mine, mine, wx_send.at[layer], wx_recv.at[layer], me, xh_peer).start()

    def start_wc(layer):
        wait_bytes(w.at[layer, :, c, other_rows], wx_recv.at[layer])
        mine = w.at[layer, :, c]
        remote(mine, mine, wc_send.at[layer], wc_recv.at[layer], me, sibling).start()

    def wait_wc(layer):
        wait_bytes(w.at[layer, :, 1 - c], wc_recv.at[layer])

    start_wz(0)
    start_wz(1)

    def weight(layer):
        return w[layer].reshape(feat, width)

    for copy in loads:
        copy.wait()

    own = pl.ds(pl.multiple_of(me * rb, rb), rb)

    def scatter(src, dst, ssem, rsem):
        for k in range(n_pipe - 1):
            to = peer(k)
            remote(
                src.at[pl.ds(pl.multiple_of(to * rb, rb), rb)], dst.at[n_pipe - 2 - k], ssem, rsem, to, d
            ).start()

    def gather(ref, ssem, rsem):
        for k in range(n_pipe - 1):
            remote(ref.at[own], ref.at[own], ssem, rsem, peer(k), d).start()

    def wait_gather(ref, ssem, rsem):
        part = ref.at[pl.ds(0, rows - rb)]
        wait_bytes(part, rsem)
        wait_bytes(part, ssem)

    def start_rs_first(cas, xl, pair):
        xf = xl.astype(F32)
        sq = jnp.sum(xf * xf, axis=-1, keepdims=True)
        first = mm(xl, weight(2 * pair))
        rs_send[cas, 0, :, :q3] = first[:, :q3].astype(BF)
        rs_send[cas, 0, :, q3:] = jnp.broadcast_to(sq, (rows, HEAD)).astype(BF)
        scatter(rs_send.at[cas, 0], rs_recv.at[cas, 0], rs_ssem.at[cas, 0], rs_rsem.at[cas, 0])
        rs_send[cas, 1, :, :HEAD] = first[:, q3:].astype(BF)

    def start_rs_second(cas, xl, pair):
        rs_send[cas, 1, :, HEAD:] = mm(xl, weight(2 * pair + 1)[:, :q3]).astype(BF)
        scatter(rs_send.at[cas, 1], rs_recv.at[cas, 1], rs_ssem.at[cas, 1], rs_rsem.at[cas, 1])

    def start_ag(pair, cas, half):
        wait_bytes(rs_recv.at[cas, half], rs_rsem.at[cas, half])
        wait_bytes(rs_recv.at[cas, half], rs_ssem.at[cas, half])
        total = rs_send[cas, half, own].astype(F32)
        for k in range(n_pipe - 1):
            total = total + rs_recv[cas, half, k].astype(F32)
        if half == 0:
            norm = total[:, q3:]
            r = lax.rsqrt(norm * (1.0 / dim) + 1e-6)
            high = norm.astype(BF).astype(F32)
            lane = lax.broadcasted_iota(jnp.int32, norm.shape, 1)
            agb[pair, cas, 0, own, :q3] = (total[:, :q3] * r[:, :1]).astype(BF)
            agb[pair, cas, 0, own, q3:] = jnp.where(lane < HEAD // 2, high, norm - high).astype(BF)
        else:
            agb[pair, cas, 1, own] = total.astype(BF)
        gather(agb.at[pair, cas, half], ag_ssem.at[cas, half], ag_rsem.at[cas, half])

    def start_rs_gh(pair):
        w0 = weight(2 * pair)[:, q3:]
        gh_send[:, :q3] = mm_tn(w0, weight(2 * pair + 1)[:, :q3]).astype(BF)
        gh_send[:, q3:] = mm_tn(w0, w0).astype(BF)
        for k in range(n_pipe - 1):
            to = peer(k)
            gr = HEAD // n_pipe
            remote(
                gh_send.at[pl.ds(pl.multiple_of(to * gr, gr), gr)], gh_recv.at[pair, n_pipe - 2 - k],
                gh_ssem.at[0], gh_rsem.at[pair], to, d,
            ).start()

    gh_own = pl.ds(pl.multiple_of(me * (HEAD // n_pipe), HEAD // n_pipe), HEAD // n_pipe)

    def start_ag_gh(pair):
        wait_bytes(gh_recv.at[pair], gh_rsem.at[pair])
        wait_bytes(gh_recv.at[pair], gh_ssem.at[0])
        total = gh_send[gh_own].astype(F32)
        for k in range(n_pipe - 1):
            total = total + gh_recv[pair, k].astype(F32)
        ghb[pair, gh_own] = total.astype(BF)
        ref = ghb.at[pair, gh_own]
        for k in range(n_pipe - 1):
            remote(ref, ref, ha_ssem.at[pair], ha_rsem.at[pair], peer(k), d).start()

    def wait_ag_gh(pair):
        part = ghb.at[pair, pl.ds(0, HEAD - HEAD // n_pipe)]
        wait_bytes(part, ha_rsem.at[pair])
        wait_bytes(part, ha_ssem.at[pair])

    def attend(layer, cas, pr):
        s = mm_nt(pr[:, :HEAD], pr[:, HEAD : 2 * HEAD]) * scale
        s = jnp.where(allowed[...] > 0.5, s, -1e30)
        ex = jnp.exp(s - jnp.max(s, axis=-1, keepdims=True))
        sm = (ex / jnp.sum(ex, axis=-1, keepdims=True)).astype(BF)
        soft[layer, cas] = sm
        a = mm(sm, pr[:, 2 * HEAD : q3]).astype(BF)
        att[layer, cas] = a
        return a

    start_wx(0)
    if pairs > 1:
        start_wz(2)
        start_wz(3)
    start_wx(1)
    start_wc(0)
    wait_wc(0)
    for cas in range(2):
        start_rs_first(cas, x[0, cas], 0)
    start_wc(1)
    if pairs > 1:
        start_wx(2)
        start_wx(3)
    if pairs > 2:
        start_wz(4)
        start_wz(5)
    wait_wc(1)
    for cas in range(2):
        start_rs_second(cas, x[0, cas], 0)
    start_rs_gh(0)

    def start_ds(cas, dyl, pair):
        ds_send[cas, :, :HEAD] = mm(dyl, weight(2 * pair)[:, q3:]).astype(BF)
        ds_send[cas, :, HEAD:] = mm(dyl, weight(2 * pair + 1)[:, q3:]).astype(BF)
        scatter(ds_send.at[cas], ds_recv.at[cas], ds_ssem.at[cas], ds_rsem.at[cas])

    def start_da(cas):
        wait_bytes(ds_recv.at[cas], ds_rsem.at[cas])
        wait_bytes(ds_recv.at[cas], ds_ssem.at[cas])
        total = ds_send[cas, own].astype(F32)
        for k in range(n_pipe - 1):
            total = total + ds_recv[cas, k].astype(F32)
        da[cas, own] = total.astype(BF)
        gather(da.at[cas], da_ssem.at[cas], da_rsem.at[cas])

    def forward(pair, carry):
        l0 = 2 * pair
        l1 = l0 + 1
        for cas in range(2):
            for half in range(2):
                start_ag(pair, cas, half)

        @pl.when(pair == 0)
        def _():
            start_ag_gh(0)

        @pl.when(pair == end)
        def _():
            for cas in range(2):
                start_ds(cas, dy[top, cas], end)

        @pl.when(pair < end)
        def _():
            start_wc(l0 + 2)
            start_wc(l1 + 2)

            @pl.when(pair + 2 < pairs)
            def _():
                start_wx(l0 + 4)
                start_wx(l1 + 4)

            @pl.when(pair + 3 < pairs)
            def _():
                start_wz(l0 + 6)
                start_wz(l1 + 6)

            wait_wc(l0 + 2)
            wait_wc(l1 + 2)
            start_rs_gh(pair + 1)

        for cas in range(2):
            wait_gather(agb.at[pair, cas, 0], ag_ssem.at[cas, 0], ag_rsem.at[cas, 0])
            a0 = attend(l0, cas, agb[pair, cas, 0, :, :q3])
            half_lane = width - HEAD // 2
            n0 = (
                agb[pair, cas, 0, :, q3 : q3 + 1].astype(F32)
                + agb[pair, cas, 0, :, half_lane : half_lane + 1].astype(F32)
            )
            x1 = (x[l0, cas].astype(F32) + mm_nt(a0, weight(l0)[:, q3:])).astype(BF)
            x[l1, cas] = x1
            if cas == 0:
                wait_ag_gh(pair)
            agh = mm(a0, ghb[pair])
            wait_gather(agb.at[pair, cas, 1], ag_ssem.at[cas, 1], ag_rsem.at[cas, 1])
            c0 = agb[pair, cas, 1, :, :HEAD].astype(F32)
            v = agh[:, q3:]
            n1 = n0 + jnp.sum(a0.astype(F32) * (2.0 * c0 + v), axis=-1, keepdims=True)
            t1[pair, cas] = c0 + v
            r0 = lax.rsqrt(n0 * (1.0 / dim) + 1e-6)
            r1 = lax.rsqrt(jnp.maximum(n1, 0.0) * (1.0 / dim) + 1e-6)
            rbuf[l0, cas] = jnp.broadcast_to(r0, (rows, HEAD))
            rbuf[l1, cas] = jnp.broadcast_to(r1, (rows, HEAD))
            pr1 = ((agb[pair, cas, 1, :, HEAD:].astype(F32) + agh[:, :q3]) * r1).astype(BF)
            p1[pair, cas] = pr1
            a1 = attend(l1, cas, pr1)

            @pl.when(pair < end)
            def _():
                x2 = (x1.astype(F32) + mm_nt(a1, weight(l1)[:, q3:])).astype(BF)
                x[l1 + 1, cas] = x2
                start_rs_first(cas, x2, pair + 1)
                start_rs_second(cas, x2, pair + 1)

        @pl.when(pair < end)
        def _():
            start_ag_gh(pair + 1)

        return carry

    lax.fori_loop(0, pairs, forward, 0)

    def attend_back(layer, cas, slot, pr, da):
        sm = soft[layer, cas]
        smf = sm.astype(F32)
        r = rbuf[layer, cas]
        dv = mm_tn(sm, da)
        dsm = mm_nt(da, pr[:, 2 * HEAD :])
        ds = (smf * (dsm - jnp.sum(dsm * smf, axis=-1, keepdims=True)) * scale).astype(BF)
        dq = mm(ds, pr[:, HEAD : 2 * HEAD])
        dk = mm_tn(ds, pr[:, :HEAD])
        prf = pr.astype(F32)
        dot = jnp.sum(
            dq * prf[:, :HEAD] + dk * prf[:, HEAD : 2 * HEAD] + dv * prf[:, 2 * HEAD :], axis=-1, keepdims=True
        )
        e_buf[slot, cas, :, :HEAD] = (dq * r).astype(BF)
        e_buf[slot, cas, :, HEAD : 2 * HEAD] = (dk * r).astype(BF)
        e_buf[slot, cas, :, 2 * HEAD :] = (dv * r).astype(BF)
        return r[:, :1] * r[:, :1] * dot * (1.0 / dim)

    def weight_grads(layer, i):
        xl = x[layer].reshape(2 * rows, feat)
        dyl = dy[layer].reshape(2 * rows, feat)
        gq = mm_tn(xl, e_buf[i].reshape(2 * rows, q3)).astype(BF)
        go = mm_tn(dyl, att[layer].reshape(2 * rows, HEAD)).astype(BF)
        g[layer, :, :, :, :q3] = gq.reshape(n_z, CORES, group, q3)
        g[layer, :, :, :, q3:] = go.reshape(n_z, CORES, group, HEAD)
        remote(
            g.at[layer, :, 1 - c], gd.at[layer], gc_send.at[layer], gc_recv.at[layer], me, sibling
        ).start()

    start_da(0)

    def start_gz(la):
        for i in (1, 0):
            lay = 2 * la + i
            wait_bytes(gxr.at[lay], gs_recv.at[lay])
            mine = (lay, slice(None), pl.ds(c, 1), my_rows)
            g[mine] = (g[mine].astype(F32) + gxr[lay][:, None].astype(F32)).astype(BF)
            for k in range(n_z - 1):
                to_z = lax.rem(z + 1 + k, n_z)
                remote(
                    g.at[lay, to_z, c, my_rows], gz.at[lay, n_z - 2 - k],
                    gz_send.at[lay], gz_recv.at[lay], me, z_peer(k),
                ).start()

    def backward(t, carry):
        pair = end - t
        l0 = 2 * pair
        l1 = l0 + 1

        @pl.when(t < pairs)
        def _():
            start_da(1)

        @pl.when((t >= 1) & (t < pairs + 1))
        def _():
            for i in (1, 0):
                lay = 2 * (pair + 1) + i
                wait_bytes(gd.at[lay], gc_recv.at[lay])
                mine = (lay, slice(None), pl.ds(c, 1))
                g[mine] = (g[mine].astype(F32) + gd[lay][:, None].astype(F32)).astype(BF)
                remote(
                    g.at[lay, :, c, other_rows], gxr.at[lay], gs_send.at[lay], gs_recv.at[lay], me, xh_peer
                ).start()

        @pl.when(t < pairs)
        def _():
            for cas in range(2):
                wait_gather(da.at[cas], da_ssem.at[cas], da_rsem.at[cas])
                cc1 = attend_back(l1, cas, 1, p1[pair, cas], da[cas, :, HEAD:])
                e1 = e_buf[1, cas]
                da0[cas] = (da[cas, :, :HEAD].astype(F32) + mm_nt(e1, ghb[pair][:, :q3]) - cc1 * t1[pair, cas]).astype(BF)
                dy[l0, cas] = (
                    dy[l1, cas].astype(F32) + mm_nt(e1, weight(l1)[:, :q3]) - x[l1, cas].astype(F32) * cc1
                ).astype(BF)

                @pl.when(pair > 0)
                def _():
                    cc0 = attend_back(l0, cas, 0, agb[pair, cas, 0, :, :q3], da0[cas])
                    dy_new = (
                        dy[l0, cas].astype(F32)
                        + mm_nt(e_buf[0, cas], weight(l0)[:, :q3])
                        - x[l0, cas].astype(F32) * cc0
                    ).astype(BF)
                    dy[l0 - 1, cas] = dy_new
                    start_ds(cas, dy_new, pair - 1)

                if cas == 0:

                    @pl.when(t >= 1)
                    def _():
                        start_gz(pair + 1)

            @pl.when(pair == 0)
            def _():
                weight_grads(l1, 1)
                for cas in range(2):
                    attend_back(l0, cas, 0, agb[pair, cas, 0, :, :q3], da0[cas])

        @pl.when(t == pairs)
        def _():
            start_gz(0)

        @pl.when(t < end)
        def _():
            start_da(0)

        @pl.when((t >= 2) & (t < pairs + 2))
        def _():
            for i in (1, 0):
                lay = 2 * (pair + 2) + i
                wait_bytes(gz.at[lay], gz_recv.at[lay])
                total = g[lay, z, c, my_rows].astype(F32)
                for k in range(n_z - 1):
                    total = total + gz[lay, k].astype(F32)
                gx[lay] = total.astype(BF)

        @pl.when((t < pairs) & (pair > 0))
        def _():
            weight_grads(l1, 1)

        @pl.when(t < pairs)
        def _():
            weight_grads(l0, 0)

        return carry

    lax.fori_loop(0, pairs + 2, backward, 0)

    for k in range(n_pipe - 1):
        to = peer(k)
        remote(gx.at[to], hp.at[me], hp_send.at[0], hp_recv.at[0], to, d).start()
    hp[pl.ds(me, 1)] = gx[pl.ds(me, 1)]
    wait_bytes(hp.at[pl.ds(0, n_pipe - 1)], hp_recv.at[0])
    for k in range(n_pipe):
        pp = lax.rem(me + k, n_pipe)
        dd = n_i * pp + my_u // per_block

        @pl.when(dd != d)
        def _():
            remote(hp.at[pp], out.at[my_s, xh], gf_send.at[pp], gf_recv.at[0], me, dd).start()

        @pl.when(dd == d)
        def _():
            pltpu.make_async_copy(hp.at[pp], out.at[my_s, xh], gf_recv.at[0]).start()

    wait_bytes(out, gf_recv.at[0])
    full = out[...].astype(F32).reshape(per_block * group, width)
    gq_ref[0] = full[:, :q3]
    go_ref[0] = full[:, q3:].T

    for s in range(per_block):
        uz, uc = spread_to(s)
        for h in range(XH):
            dd = dp_at(h, uz, uc)

            @pl.when(dd != d)
            def _():
                wait_bytes(wpack.at[pl.ds((XH * s + h) * piece, piece)], w1_send.at[XH * s + h])

    wait_bytes(w1b.at[pl.ds(0, n_pipe - 1)], w2_send.at[0])
    wait_bytes(hp.at[pl.ds(0, n_pipe - 1)], hp_send.at[0])

    def drain(lay, carry):
        wait_bytes(w.at[lay, pl.ds(0, n_z - 1), c, my_rows], wz_send.at[lay])
        wait_bytes(w.at[lay, :, c, my_rows], wx_send.at[lay])
        wait_bytes(w.at[lay, :, c], wc_send.at[lay])
        wait_bytes(gd.at[lay], gc_send.at[lay])
        wait_bytes(gxr.at[lay], gs_send.at[lay])
        wait_bytes(gz.at[lay], gz_send.at[lay])

        @pl.when(n_i * lay + my_u // per_block != d)
        def _():
            wait_bytes(hp.at[lay], gf_send.at[lay])

        return carry

    lax.fori_loop(0, n_pipe, drain, 0)


def per_device(x_down, x_up, cot_down, cot_up, w_qkv, w_out, block_mask):
    n_pipe, n_dp = lax.axis_size("pipe"), lax.axis_size("dp")
    rows, dim = x_down.shape
    feat = dim // n_pipe
    n_z = n_dp // (XH * CORES)
    group = feat // (n_z * CORES)
    per_block = n_pipe // XH
    width = 4 * HEAD
    rb = rows // n_pipe
    layers = n_pipe
    pairs = layers // 2
    any_spec = pl.BlockSpec(memory_space=pl.ANY)
    vmem = pl.BlockSpec(memory_space=pltpu.VMEM)
    dma = pltpu.SemaphoreType.DMA
    return pl.pallas_call(
        functools.partial(kernel, n_pipe, n_dp),
        out_shape=(
            jax.ShapeDtypeStruct(w_qkv.shape, F32),
            jax.ShapeDtypeStruct(w_out.shape, F32),
        ),
        in_specs=[any_spec] * 4 + [vmem] * 2 + [pl.BlockSpec(memory_space=pltpu.SMEM)],
        out_specs=(vmem, vmem),
        scratch_shapes=[
            pltpu.VMEM((rows, rows), F32),
            pltpu.VMEM((per_block * group, width), BF),
            pltpu.VMEM((n_pipe, group // XH, width), BF),
            pltpu.VMEM((layers, n_z, CORES, group, width), BF),
            pltpu.VMEM((layers, 2, rows, feat), BF),
            pltpu.VMEM((layers, 2, rows, feat), BF),
            pltpu.VMEM((pairs, 2, 2, rows, width), BF),
            pltpu.VMEM((pairs, 2, rows, 3 * HEAD), BF),
            pltpu.VMEM((layers, 2, rows, rows), BF),
            pltpu.VMEM((layers, 2, rows, HEAD), BF),
            pltpu.VMEM((pairs, 2, rows, HEAD), F32),
            pltpu.VMEM((layers, 2, rows, HEAD), F32),
            pltpu.VMEM((2, 2, rows, 3 * HEAD), BF),
            pltpu.VMEM((2, 2, rows, width), BF),
            pltpu.VMEM((2, 2, n_pipe - 1, rb, width), BF),
            pltpu.VMEM((HEAD, width), BF),
            pltpu.VMEM((pairs, n_pipe - 1, HEAD // n_pipe, width), BF),
            pltpu.VMEM((pairs, HEAD, width), BF),
            pltpu.VMEM((2, rows, 2 * HEAD), BF),
            pltpu.VMEM((2, n_pipe - 1, rb, 2 * HEAD), BF),
            pltpu.VMEM((2, rows, 2 * HEAD), BF),
            pltpu.VMEM((2, rows, HEAD), BF),
            pltpu.VMEM((layers, n_z, CORES, group, width), BF),
            pltpu.VMEM((layers, n_z, group, width), BF),
            pltpu.VMEM((layers, n_z, group // XH, width), BF),
            pltpu.VMEM((layers, n_z - 1, group // XH, width), BF),
            pltpu.VMEM((layers, group // XH, width), BF),
            pltpu.VMEM((layers, group // XH, width), BF),
            pltpu.VMEM((per_block, XH, group // XH, width), BF),
            dma((4,)),
            dma((n_pipe,)), dma((1,)),
            dma((1,)), dma((1,)),
            dma((layers,)), dma((layers,)),
            dma((layers,)), dma((layers,)),
            dma((layers,)), dma((layers,)),
            dma((2, 2)), dma((2, 2)), dma((2, 2)), dma((2, 2)),
            dma((1,)), dma((pairs,)), dma((pairs,)), dma((pairs,)),
            dma((2,)), dma((2,)), dma((2,)), dma((2,)),
            dma((layers,)), dma((layers,)),
            dma((layers,)), dma((layers,)),
            dma((layers,)), dma((layers,)),
            dma((1,)), dma((1,)),
            dma((layers,)), dma((1,)),
        ],
        compiler_params=pltpu.CompilerParams(
            collective_id=0, has_side_effects=True, vmem_limit_bytes=60 * 1024 * 1024
        ),
    )(x_down, x_up, cot_down, cot_up, w_qkv, w_out, block_mask)


def solution(mesh):
    placed = (
        P("dp", None),
        P("dp", None),
        P("dp", None),
        P("dp", None),
        P("pipe", "dp", None),
        P("pipe", None, "dp"),
        P(),
    )
    return jax.shard_map(
        per_device,
        mesh=mesh,
        in_specs=placed,
        out_specs=(P("pipe", "dp", None), P("pipe", None, "dp")),
        check_vma=False,
    )
```

```python
import functools

import jax
import jax.numpy as jnp
from jax import lax
from jax.experimental import pallas as pl
from jax.experimental.pallas import tpu as pltpu
from jax.sharding import PartitionSpec as P

BLK = 32
HEAD = 128
XH = 2
CORES = 2
BF = jnp.bfloat16
F32 = jnp.float32

NT = (((1,), (1,)), ((), ()))
TN = (((0,), (0,)), ((), ()))


def mm(a, b):
    return jnp.dot(a, b, preferred_element_type=F32)


def mm_nt(a, b):
    return lax.dot_general(a, b, NT, preferred_element_type=F32)


def mm_tn(a, b):
    return lax.dot_general(a, b, TN, preferred_element_type=F32)


def kernel(
    n_pipe,
    n_dp,
    x_down, x_up, cot_down, cot_up, wq_ref, wo_ref, mask_ref,
    gq_ref, go_ref,
    allowed, wpack, w1b, w, x, dy, agb, p1, soft, att, t1, rbuf, e_buf,
    rs_send, rs_recv, gh_send, gh_recv, ghb, ds_send, ds_recv, da, da0,
    g, gd, gxr, gz, gx, gyr, gf, hp, out,
    load_sem, w1_send, w1_recv, w2_send, w2_recv, wz_send, wz_recv, wc_send, wc_recv,
    rs_ssem, rs_rsem, ag_ssem, ag_rsem, gh_ssem, gh_rsem, ha_ssem, ha_rsem, ds_ssem, ds_rsem, da_ssem, da_rsem,
    gc_send, gc_recv, gs_send, gs_recv, gy_send, gy_recv, gz_send, gz_recv, hp_send, hp_recv, gf_send, gf_recv,
):
    pairs = n_pipe // 2
    n_z = n_dp // (XH * CORES)
    n_i = n_dp // n_pipe
    rows = x.shape[2]
    feat = x.shape[3]
    dim = feat * n_pipe
    group = w.shape[3]
    per_block = n_pipe // XH
    rb = rows // n_pipe
    end = pairs - 1
    q3 = 3 * HEAD
    width = 4 * HEAD
    scale = HEAD ** (-0.5)

    me = lax.axis_index("pipe")
    d = lax.axis_index("dp")
    xh = d // (n_z * CORES)
    z = (d // CORES) % n_z
    c = d % CORES

    def dp_at(xh_, z_, c_):
        return xh_ * (n_z * CORES) + z_ * CORES + c_

    def peer(k):
        return lax.rem(me + 1 + k, n_pipe)

    def z_peer(k):
        return dp_at(xh, lax.rem(z + 1 + k, n_z), c)

    sibling = dp_at(xh, z, 1 - c)
    xh_peer = dp_at(1 - xh, z, c)
    piece = group // XH
    my_rows = pl.ds(pl.multiple_of(xh * piece, piece), piece)
    other_rows = pl.ds(pl.multiple_of((1 - xh) * piece, piece), piece)

    def spread_to(s):
        u = (d % n_i) * per_block + s
        return u // CORES, u % CORES

    to_pipe = d // n_i
    my_u = z * CORES + c
    my_s = my_u % per_block

    def remote(src, dst, ssem, rsem, pp, dd):
        return pltpu.make_async_remote_copy(
            src_ref=src, dst_ref=dst, send_sem=ssem, recv_sem=rsem,
            device_id={"pipe": pp, "dp": dd}, device_id_type=pl.DeviceIdType.MESH,
        )

    def wait_bytes(ref, sem):
        pltpu.make_async_copy(ref, ref, sem).wait()

    def layers_of(pair):
        return pl.ds(2 * pair, 2)

    barrier = pltpu.get_barrier_semaphore()

    def greet(pp, dd):
        pl.semaphore_signal(
            barrier, inc=1, device_id={"pipe": pp, "dp": dd},
            device_id_type=pl.DeviceIdType.MESH,
        )

    for s in range(per_block):
        uz, uc = spread_to(s)
        for h in range(XH):
            dd = dp_at(h, uz, uc)

            @pl.when(dd != d)
            def _():
                greet(me, dd)

    for j in range(n_pipe):

        @pl.when(n_i * j + my_u // per_block != d)
        def _():
            greet(me, n_i * j + my_u // per_block)

    for k in range(n_z - 1):
        greet(me, z_peer(k))
    greet(me, sibling)
    greet(me, xh_peer)
    for k in range(n_pipe - 1):
        greet(peer(k), d)
        greet(peer(k), xh_peer)

    cols = pl.ds(pl.multiple_of(me * feat, feat), feat)
    top = 2 * pairs - 1
    loads = [
        pltpu.make_async_copy(x_down.at[:, cols], x.at[0, 0], load_sem.at[0]),
        pltpu.make_async_copy(x_up.at[:, cols], x.at[0, 1], load_sem.at[1]),
        pltpu.make_async_copy(cot_down.at[:, cols], dy.at[top, 0], load_sem.at[2]),
        pltpu.make_async_copy(cot_up.at[:, cols], dy.at[top, 1], load_sem.at[3]),
    ]
    for copy in loads:
        copy.start()

    blocks = mask_ref.shape[0]
    row = lax.broadcasted_iota(jnp.int32, (rows, rows), 0)
    col = lax.broadcasted_iota(jnp.int32, (rows, rows), 1)
    read = jnp.zeros((rows, rows), jnp.int32)
    for i in range(blocks):
        for j in range(blocks):
            inside = (row // (rows // blocks) == i) & (col // (rows // blocks) == j)
            read = jnp.where(inside, mask_ref[i, j], read)
    allowed[...] = jnp.where((read == 1) & (col <= row), 1.0, 0.0)

    wpack[:, :q3] = wq_ref[0]
    wpack[:, q3:] = wo_ref[0].astype(F32).T.astype(BF)

    itself = jnp.where(my_u // per_block == d % n_i, 1, 0)
    pl.semaphore_wait(barrier, 4 * n_pipe + n_z - 1 - 2 * itself)

    for s in range(per_block):
        uz, uc = spread_to(s)
        for h in range(XH):
            dd = dp_at(h, uz, uc)
            src = wpack.at[pl.ds((XH * s + h) * piece, piece)]

            @pl.when(dd != d)
            def _():
                remote(src, w1b.at[to_pipe], w1_send.at[XH * s + h], w1_recv.at[0], me, dd).start()

            @pl.when(dd == d)
            def _():
                pltpu.make_async_copy(src, w1b.at[to_pipe], w1_recv.at[0]).start()

    wait_bytes(w1b, w1_recv.at[0])
    held = w.at[me, z, c, my_rows]
    for k in range(n_pipe - 1):
        to = peer(k)
        remote(w1b.at[to], held, w2_send.at[0], w2_recv.at[0], to, d).start()
        remote(w1b.at[to], held, w2_send.at[1], w2_recv.at[0], to, xh_peer).start()
    remote(w1b.at[me], held, w2_send.at[1], w2_recv.at[0], me, xh_peer).start()
    pltpu.make_async_copy(w1b.at[me], held, w2_recv.at[0]).start()
    wait_bytes(w.at[:, z, c], w2_recv.at[0])

    def start_wz(layer):
        mine = w.at[layer, z, c]
        for k in range(n_z - 1):
            remote(mine, mine, wz_send.at[layer], wz_recv.at[layer], me, z_peer(k)).start()

    def start_wc(layer):
        wait_bytes(w.at[layer, pl.ds(0, n_z - 1), c], wz_recv.at[layer])
        mine = w.at[layer, :, c]
        remote(mine, mine, wc_send.at[layer], wc_recv.at[layer], me, sibling).start()

    def wait_wc(layer):
        wait_bytes(w.at[layer, :, 1 - c], wc_recv.at[layer])

    start_wz(0)
    start_wz(1)

    def weight(layer):
        return w[layer].reshape(feat, width)

    for copy in loads:
        copy.wait()

    own = pl.ds(pl.multiple_of(me * rb, rb), rb)

    def scatter(src, dst, ssem, rsem):
        for k in range(n_pipe - 1):
            to = peer(k)
            remote(
                src.at[pl.ds(pl.multiple_of(to * rb, rb), rb)], dst.at[n_pipe - 2 - k], ssem, rsem, to, d
            ).start()

    def gather(ref, ssem, rsem):
        for k in range(n_pipe - 1):
            remote(ref.at[own], ref.at[own], ssem, rsem, peer(k), d).start()

    def wait_gather(ref, ssem, rsem):
        part = ref.at[pl.ds(0, rows - rb)]
        wait_bytes(part, rsem)
        wait_bytes(part, ssem)

    def start_rs_first(cas, xl, pair):
        xf = xl.astype(F32)
        sq = jnp.sum(xf * xf, axis=-1, keepdims=True)
        first = mm(xl, weight(2 * pair))
        rs_send[cas, 0, :, :q3] = first[:, :q3].astype(BF)
        rs_send[cas, 0, :, q3:] = jnp.broadcast_to(sq, (rows, HEAD)).astype(BF)
        scatter(rs_send.at[cas, 0], rs_recv.at[cas, 0], rs_ssem.at[cas, 0], rs_rsem.at[cas, 0])
        rs_send[cas, 1, :, :HEAD] = first[:, q3:].astype(BF)

    def start_rs_second(cas, xl, pair):
        rs_send[cas, 1, :, HEAD:] = mm(xl, weight(2 * pair + 1)[:, :q3]).astype(BF)
        scatter(rs_send.at[cas, 1], rs_recv.at[cas, 1], rs_ssem.at[cas, 1], rs_rsem.at[cas, 1])

    def start_ag(pair, cas, half):
        wait_bytes(rs_recv.at[cas, half], rs_rsem.at[cas, half])
        wait_bytes(rs_recv.at[cas, half], rs_ssem.at[cas, half])
        total = rs_send[cas, half, own].astype(F32)
        for k in range(n_pipe - 1):
            total = total + rs_recv[cas, half, k].astype(F32)
        if half == 0:
            norm = total[:, q3:]
            r = lax.rsqrt(norm * (1.0 / dim) + 1e-6)
            high = norm.astype(BF).astype(F32)
            lane = lax.broadcasted_iota(jnp.int32, norm.shape, 1)
            agb[pair, cas, 0, own, :q3] = (total[:, :q3] * r[:, :1]).astype(BF)
            agb[pair, cas, 0, own, q3:] = jnp.where(lane < HEAD // 2, high, norm - high).astype(BF)
        else:
            agb[pair, cas, 1, own] = total.astype(BF)
        gather(agb.at[pair, cas, half], ag_ssem.at[cas, half], ag_rsem.at[cas, half])

    def start_rs_gh(pair):
        w0 = weight(2 * pair)[:, q3:]
        gh_send[:, :q3] = mm_tn(w0, weight(2 * pair + 1)[:, :q3]).astype(BF)
        gh_send[:, q3:] = mm_tn(w0, w0).astype(BF)
        for k in range(n_pipe - 1):
            to = peer(k)
            gr = HEAD // n_pipe
            remote(
                gh_send.at[pl.ds(pl.multiple_of(to * gr, gr), gr)], gh_recv.at[pair, n_pipe - 2 - k],
                gh_ssem.at[0], gh_rsem.at[pair], to, d,
            ).start()

    gh_own = pl.ds(pl.multiple_of(me * (HEAD // n_pipe), HEAD // n_pipe), HEAD // n_pipe)

    def start_ag_gh(pair):
        wait_bytes(gh_recv.at[pair], gh_rsem.at[pair])
        wait_bytes(gh_recv.at[pair], gh_ssem.at[0])
        total = gh_send[gh_own].astype(F32)
        for k in range(n_pipe - 1):
            total = total + gh_recv[pair, k].astype(F32)
        ghb[pair, gh_own] = total.astype(BF)
        ref = ghb.at[pair, gh_own]
        for k in range(n_pipe - 1):
            remote(ref, ref, ha_ssem.at[pair], ha_rsem.at[pair], peer(k), d).start()

    def wait_ag_gh(pair):
        part = ghb.at[pair, pl.ds(0, HEAD - HEAD // n_pipe)]
        wait_bytes(part, ha_rsem.at[pair])
        wait_bytes(part, ha_ssem.at[pair])

    def attend(layer, cas, pr):
        s = mm_nt(pr[:, :HEAD], pr[:, HEAD : 2 * HEAD]) * scale
        s = jnp.where(allowed[...] > 0.5, s, -1e30)
        ex = jnp.exp(s - jnp.max(s, axis=-1, keepdims=True))
        sm = (ex / jnp.sum(ex, axis=-1, keepdims=True)).astype(BF)
        soft[layer, cas] = sm
        a = mm(sm, pr[:, 2 * HEAD : q3]).astype(BF)
        att[layer, cas] = a
        return a

    start_wc(0)
    if pairs > 1:
        start_wz(2)
        start_wz(3)
    wait_wc(0)
    for cas in range(2):
        start_rs_first(cas, x[0, cas], 0)
    start_wc(1)
    wait_wc(1)
    for cas in range(2):
        start_rs_second(cas, x[0, cas], 0)
    start_rs_gh(0)

    def start_ds(cas, dyl, pair):
        ds_send[cas, :, :HEAD] = mm(dyl, weight(2 * pair)[:, q3:]).astype(BF)
        ds_send[cas, :, HEAD:] = mm(dyl, weight(2 * pair + 1)[:, q3:]).astype(BF)
        scatter(ds_send.at[cas], ds_recv.at[cas], ds_ssem.at[cas], ds_rsem.at[cas])

    def start_da(cas):
        wait_bytes(ds_recv.at[cas], ds_rsem.at[cas])
        wait_bytes(ds_recv.at[cas], ds_ssem.at[cas])
        total = ds_send[cas, own].astype(F32)
        for k in range(n_pipe - 1):
            total = total + ds_recv[cas, k].astype(F32)
        da[cas, own] = total.astype(BF)
        gather(da.at[cas], da_ssem.at[cas], da_rsem.at[cas])

    def forward(pair, carry):
        l0 = 2 * pair
        l1 = l0 + 1
        for cas in range(2):
            for half in range(2):
                start_ag(pair, cas, half)

        @pl.when(pair == 0)
        def _():
            start_ag_gh(0)

        @pl.when(pair == end)
        def _():
            for cas in range(2):
                start_ds(cas, dy[top, cas], end)

        @pl.when(pair < end)
        def _():
            start_wc(l0 + 2)

            @pl.when(pair + 2 < pairs)
            def _():
                start_wz(l0 + 4)

            start_wc(l1 + 2)

            @pl.when(pair + 2 < pairs)
            def _():
                start_wz(l1 + 4)

            wait_wc(l0 + 2)
            wait_wc(l1 + 2)
            start_rs_gh(pair + 1)

        for cas in range(2):
            wait_gather(agb.at[pair, cas, 0], ag_ssem.at[cas, 0], ag_rsem.at[cas, 0])
            a0 = attend(l0, cas, agb[pair, cas, 0, :, :q3])
            half_lane = width - HEAD // 2
            n0 = (
                agb[pair, cas, 0, :, q3 : q3 + 1].astype(F32)
                + agb[pair, cas, 0, :, half_lane : half_lane + 1].astype(F32)
            )
            x1 = (x[l0, cas].astype(F32) + mm_nt(a0, weight(l0)[:, q3:])).astype(BF)
            x[l1, cas] = x1
            if cas == 0:
                wait_ag_gh(pair)
            agh = mm(a0, ghb[pair])
            wait_gather(agb.at[pair, cas, 1], ag_ssem.at[cas, 1], ag_rsem.at[cas, 1])
            c0 = agb[pair, cas, 1, :, :HEAD].astype(F32)
            v = agh[:, q3:]
            n1 = n0 + jnp.sum(a0.astype(F32) * (2.0 * c0 + v), axis=-1, keepdims=True)
            t1[pair, cas] = c0 + v
            r0 = lax.rsqrt(n0 * (1.0 / dim) + 1e-6)
            r1 = lax.rsqrt(jnp.maximum(n1, 0.0) * (1.0 / dim) + 1e-6)
            rbuf[l0, cas] = jnp.broadcast_to(r0, (rows, HEAD))
            rbuf[l1, cas] = jnp.broadcast_to(r1, (rows, HEAD))
            pr1 = ((agb[pair, cas, 1, :, HEAD:].astype(F32) + agh[:, :q3]) * r1).astype(BF)
            p1[pair, cas] = pr1
            a1 = attend(l1, cas, pr1)

            @pl.when(pair < end)
            def _():
                x2 = (x1.astype(F32) + mm_nt(a1, weight(l1)[:, q3:])).astype(BF)
                x[l1 + 1, cas] = x2
                start_rs_first(cas, x2, pair + 1)
                start_rs_second(cas, x2, pair + 1)

        @pl.when(pair < end)
        def _():
            start_ag_gh(pair + 1)

        return carry

    lax.fori_loop(0, pairs, forward, 0)

    def attend_back(layer, cas, slot, pr, da):
        sm = soft[layer, cas]
        smf = sm.astype(F32)
        r = rbuf[layer, cas]
        dv = mm_tn(sm, da)
        dsm = mm_nt(da, pr[:, 2 * HEAD :])
        ds = (smf * (dsm - jnp.sum(dsm * smf, axis=-1, keepdims=True)) * scale).astype(BF)
        dq = mm(ds, pr[:, HEAD : 2 * HEAD])
        dk = mm_tn(ds, pr[:, :HEAD])
        prf = pr.astype(F32)
        dot = jnp.sum(
            dq * prf[:, :HEAD] + dk * prf[:, HEAD : 2 * HEAD] + dv * prf[:, 2 * HEAD :], axis=-1, keepdims=True
        )
        e_buf[slot, cas, :, :HEAD] = (dq * r).astype(BF)
        e_buf[slot, cas, :, HEAD : 2 * HEAD] = (dk * r).astype(BF)
        e_buf[slot, cas, :, 2 * HEAD :] = (dv * r).astype(BF)
        return r[:, :1] * r[:, :1] * dot * (1.0 / dim)

    def weight_grads(layer, i):
        xl = x[layer].reshape(2 * rows, feat)
        dyl = dy[layer].reshape(2 * rows, feat)
        gq = mm_tn(xl, e_buf[i].reshape(2 * rows, q3)).astype(BF)
        go = mm_tn(dyl, att[layer].reshape(2 * rows, HEAD)).astype(BF)
        g[layer, :, :, :, :q3] = gq.reshape(n_z, CORES, group, q3)
        g[layer, :, :, :, q3:] = go.reshape(n_z, CORES, group, HEAD)
        remote(
            g.at[layer, :, 1 - c], gd.at[layer], gc_send.at[layer], gc_recv.at[layer], me, sibling
        ).start()

    start_da(0)

    def add_cores(lay):
        wait_bytes(gd.at[lay], gc_recv.at[lay])
        mine = (lay, slice(None), pl.ds(c, 1))
        g[mine] = (g[mine].astype(F32) + gd[lay][:, None].astype(F32)).astype(BF)

    def start_gz(lay, src_rows, slot_rows):
        for k in range(n_z - 1):
            to_z = lax.rem(z + 1 + k, n_z)
            remote(
                g.at[lay, to_z, c, src_rows], gz.at[lay, n_z - 2 - k, slot_rows],
                gz_send.at[lay], gz_recv.at[lay], me, z_peer(k),
            ).start()

    def sum_z(pair):
        for i in (1, 0):
            lay = 2 * pair + i
            wait_bytes(gz.at[lay], gz_recv.at[lay])
            total = g[lay, z, c].astype(F32)
            for k in range(n_z - 1):
                total = total + gz[lay, k].astype(F32)
            gx[lay] = total.astype(BF)

    def backward(t, carry):
        pair = end - t
        l0 = 2 * pair
        l1 = l0 + 1

        start_da(1)

        @pl.when(t >= 1)
        def _():
            for i in (1, 0):
                lay = l0 + 2 + i
                add_cores(lay)
                start_gz(lay, pl.ds(0, group), pl.ds(0, group))

        for cas in range(2):
            wait_gather(da.at[cas], da_ssem.at[cas], da_rsem.at[cas])
            cc1 = attend_back(l1, cas, 1, p1[pair, cas], da[cas, :, HEAD:])
            e1 = e_buf[1, cas]
            da0[cas] = (da[cas, :, :HEAD].astype(F32) + mm_nt(e1, ghb[pair][:, :q3]) - cc1 * t1[pair, cas]).astype(BF)
            dy[l0, cas] = (
                dy[l1, cas].astype(F32) + mm_nt(e1, weight(l1)[:, :q3]) - x[l1, cas].astype(F32) * cc1
            ).astype(BF)

            @pl.when(pair > 0)
            def _():
                cc0 = attend_back(l0, cas, 0, agb[pair, cas, 0, :, :q3], da0[cas])
                dy_new = (
                    dy[l0, cas].astype(F32)
                    + mm_nt(e_buf[0, cas], weight(l0)[:, :q3])
                    - x[l0, cas].astype(F32) * cc0
                ).astype(BF)
                dy[l0 - 1, cas] = dy_new
                start_ds(cas, dy_new, pair - 1)

        @pl.when(pair == 0)
        def _():
            weight_grads(l1, 1)
            for cas in range(2):
                attend_back(l0, cas, 0, agb[pair, cas, 0, :, :q3], da0[cas])

        @pl.when(t < end)
        def _():
            start_da(0)

        @pl.when(t >= 2)
        def _():
            sum_z(pair + 2)

        @pl.when(pair > 0)
        def _():
            weight_grads(l1, 1)

        weight_grads(l0, 0)
        return carry

    lax.fori_loop(0, pairs, backward, 0)

    for lay in (1, 0):
        add_cores(lay)
        remote(
            g.at[lay, :, c, other_rows], gxr.at[lay], gs_send.at[lay], gs_recv.at[lay], me, xh_peer
        ).start()
    rest = pl.ds(2, n_pipe - 2)
    if pairs > 1:
        sum_z(1)
        remote(
            gx.at[rest, other_rows], gyr.at[rest], gy_send.at[0], gy_recv.at[0], me, xh_peer
        ).start()
    for lay in (1, 0):
        wait_bytes(gxr.at[lay], gs_recv.at[lay])
        mine = (lay, slice(None), pl.ds(c, 1), my_rows)
        g[mine] = (g[mine].astype(F32) + gxr[lay][:, None].astype(F32)).astype(BF)
        start_gz(lay, my_rows, pl.ds(0, piece))
    if pairs > 1:
        wait_bytes(gyr.at[rest], gy_recv.at[0])
        gf[rest] = (gx[rest, my_rows].astype(F32) + gyr[rest].astype(F32)).astype(BF)
    for lay in (1, 0):
        wait_bytes(gz.at[lay, :, pl.ds(0, piece)], gz_recv.at[lay])
        total = g[lay, z, c, my_rows].astype(F32)
        for k in range(n_z - 1):
            total = total + gz[lay, k, :piece].astype(F32)
        gf[lay] = total.astype(BF)

    for k in range(n_pipe - 1):
        to = peer(k)
        remote(gf.at[to], hp.at[me], hp_send.at[0], hp_recv.at[0], to, d).start()
    hp[pl.ds(me, 1)] = gf[pl.ds(me, 1)]
    wait_bytes(hp.at[pl.ds(0, n_pipe - 1)], hp_recv.at[0])
    for k in range(n_pipe):
        pp = lax.rem(me + k, n_pipe)
        dd = n_i * pp + my_u // per_block

        @pl.when(dd != d)
        def _():
            remote(hp.at[pp], out.at[my_s, xh], gf_send.at[pp], gf_recv.at[0], me, dd).start()

        @pl.when(dd == d)
        def _():
            pltpu.make_async_copy(hp.at[pp], out.at[my_s, xh], gf_recv.at[0]).start()

    wait_bytes(out, gf_recv.at[0])
    full = out[...].astype(F32).reshape(per_block * group, width)
    gq_ref[0] = full[:, :q3]
    go_ref[0] = full[:, q3:].T

    for s in range(per_block):
        uz, uc = spread_to(s)
        for h in range(XH):
            dd = dp_at(h, uz, uc)

            @pl.when(dd != d)
            def _():
                wait_bytes(wpack.at[pl.ds((XH * s + h) * piece, piece)], w1_send.at[XH * s + h])

    wait_bytes(w1b.at[pl.ds(0, n_pipe - 1)], w2_send.at[0])
    wait_bytes(w1b, w2_send.at[1])
    wait_bytes(hp.at[pl.ds(0, n_pipe - 1)], hp_send.at[0])

    def drain(lay, carry):
        wait_bytes(w.at[lay, pl.ds(0, n_z - 1), c], wz_send.at[lay])
        wait_bytes(w.at[lay, :, c], wc_send.at[lay])
        wait_bytes(gd.at[lay], gc_send.at[lay])

        @pl.when(n_i * lay + my_u // per_block != d)
        def _():
            wait_bytes(hp.at[lay], gf_send.at[lay])

        return carry

    lax.fori_loop(0, n_pipe, drain, 0)
    for lay in range(2):
        wait_bytes(gxr.at[lay], gs_send.at[lay])
        wait_bytes(gz.at[lay, :, pl.ds(0, piece)], gz_send.at[lay])
    if pairs > 1:
        wait_bytes(gyr.at[rest], gy_send.at[0])

    def drain_z(lay, carry):
        wait_bytes(gz.at[lay], gz_send.at[lay])
        return carry

    lax.fori_loop(2, n_pipe, drain_z, 0)


def per_device(x_down, x_up, cot_down, cot_up, w_qkv, w_out, block_mask):
    n_pipe, n_dp = lax.axis_size("pipe"), lax.axis_size("dp")
    rows, dim = x_down.shape
    feat = dim // n_pipe
    n_z = n_dp // (XH * CORES)
    group = feat // (n_z * CORES)
    per_block = n_pipe // XH
    width = 4 * HEAD
    rb = rows // n_pipe
    layers = n_pipe
    pairs = layers // 2
    any_spec = pl.BlockSpec(memory_space=pl.ANY)
    vmem = pl.BlockSpec(memory_space=pltpu.VMEM)
    dma = pltpu.SemaphoreType.DMA
    return pl.pallas_call(
        functools.partial(kernel, n_pipe, n_dp),
        out_shape=(
            jax.ShapeDtypeStruct(w_qkv.shape, F32),
            jax.ShapeDtypeStruct(w_out.shape, F32),
        ),
        in_specs=[any_spec] * 4 + [vmem] * 2 + [pl.BlockSpec(memory_space=pltpu.SMEM)],
        out_specs=(vmem, vmem),
        scratch_shapes=[
            pltpu.VMEM((rows, rows), F32),
            pltpu.VMEM((per_block * group, width), BF),
            pltpu.VMEM((n_pipe, group // XH, width), BF),
            pltpu.VMEM((layers, n_z, CORES, group, width), BF),
            pltpu.VMEM((layers, 2, rows, feat), BF),
            pltpu.VMEM((layers, 2, rows, feat), BF),
            pltpu.VMEM((pairs, 2, 2, rows, width), BF),
            pltpu.VMEM((pairs, 2, rows, 3 * HEAD), BF),
            pltpu.VMEM((layers, 2, rows, rows), BF),
            pltpu.VMEM((layers, 2, rows, HEAD), BF),
            pltpu.VMEM((pairs, 2, rows, HEAD), F32),
            pltpu.VMEM((layers, 2, rows, HEAD), F32),
            pltpu.VMEM((2, 2, rows, 3 * HEAD), BF),
            pltpu.VMEM((2, 2, rows, width), BF),
            pltpu.VMEM((2, 2, n_pipe - 1, rb, width), BF),
            pltpu.VMEM((HEAD, width), BF),
            pltpu.VMEM((pairs, n_pipe - 1, HEAD // n_pipe, width), BF),
            pltpu.VMEM((pairs, HEAD, width), BF),
            pltpu.VMEM((2, rows, 2 * HEAD), BF),
            pltpu.VMEM((2, n_pipe - 1, rb, 2 * HEAD), BF),
            pltpu.VMEM((2, rows, 2 * HEAD), BF),
            pltpu.VMEM((2, rows, HEAD), BF),
            pltpu.VMEM((layers, n_z, CORES, group, width), BF),
            pltpu.VMEM((layers, n_z, group, width), BF),
            pltpu.VMEM((2, n_z, group // XH, width), BF),
            pltpu.VMEM((layers, n_z - 1, group, width), BF),
            pltpu.VMEM((layers, group, width), BF),
            pltpu.VMEM((layers, group // XH, width), BF),
            pltpu.VMEM((layers, group // XH, width), BF),
            pltpu.VMEM((layers, group // XH, width), BF),
            pltpu.VMEM((per_block, XH, group // XH, width), BF),
            dma((4,)),
            dma((n_pipe,)), dma((1,)),
            dma((2,)), dma((1,)),
            dma((layers,)), dma((layers,)),
            dma((layers,)), dma((layers,)),
            dma((2, 2)), dma((2, 2)), dma((2, 2)), dma((2, 2)),
            dma((1,)), dma((pairs,)), dma((pairs,)), dma((pairs,)),
            dma((2,)), dma((2,)), dma((2,)), dma((2,)),
            dma((layers,)), dma((layers,)),
            dma((2,)), dma((2,)),
            dma((1,)), dma((1,)),
            dma((layers,)), dma((layers,)),
            dma((1,)), dma((1,)),
            dma((layers,)), dma((1,)),
        ],
        compiler_params=pltpu.CompilerParams(
            collective_id=0, has_side_effects=True, vmem_limit_bytes=60 * 1024 * 1024
        ),
    )(x_down, x_up, cot_down, cot_up, w_qkv, w_out, block_mask)


def solution(mesh):
    placed = (
        P("dp", None),
        P("dp", None),
        P("dp", None),
        P("dp", None),
        P("pipe", "dp", None),
        P("pipe", None, "dp"),
        P(),
    )
    return jax.shard_map(
        per_device,
        mesh=mesh,
        in_specs=placed,
        out_specs=(P("pipe", "dp", None), P("pipe", None, "dp")),
        check_vma=False,
    )
```

```python
import functools

import jax
import jax.numpy as jnp
from jax import lax
from jax.experimental import pallas as pl
from jax.experimental.pallas import tpu as pltpu
from jax.sharding import PartitionSpec as P

BLK = 32
HEAD = 128
XH = 2
CORES = 2
BF = jnp.bfloat16
F32 = jnp.float32

NT = (((1,), (1,)), ((), ()))
TN = (((0,), (0,)), ((), ()))


def mm(a, b):
    return jnp.dot(a, b, preferred_element_type=F32)


def mm_nt(a, b):
    return lax.dot_general(a, b, NT, preferred_element_type=F32)


def mm_tn(a, b):
    return lax.dot_general(a, b, TN, preferred_element_type=F32)


def kernel(
    n_pipe,
    n_dp,
    x_down, x_up, cot_down, cot_up, wq_ref, wo_ref, mask_ref,
    gq_ref, go_ref,
    allowed, wpack, w1b, w, x, dy, agb, p1, soft, att, t1, rbuf, e_buf,
    rs_send, rs_recv, gh_send, gh_recv, ghb, ds_send, ds_recv, da, da0,
    g, gd, gxr, gz, gx, hp, out,
    load_sem, w1_send, w1_recv, w2_send, w2_recv, wz_send, wz_recv, wc_send, wc_recv,
    rs_ssem, rs_rsem, ag_ssem, ag_rsem, gh_ssem, gh_rsem, ha_ssem, ha_rsem, ds_ssem, ds_rsem, da_ssem, da_rsem,
    gc_send, gc_recv, gs_send, gs_recv, gz_send, gz_recv, hp_send, hp_recv, gf_send, gf_recv,
):
    pairs = n_pipe // 2
    n_z = n_dp // (XH * CORES)
    n_i = n_dp // n_pipe
    rows = x.shape[2]
    feat = x.shape[3]
    dim = feat * n_pipe
    group = w.shape[3]
    per_block = n_pipe // XH
    rb = rows // n_pipe
    end = pairs - 1
    q3 = 3 * HEAD
    width = 4 * HEAD
    scale = HEAD ** (-0.5)

    me = lax.axis_index("pipe")
    d = lax.axis_index("dp")
    xh = d // (n_z * CORES)
    z = (d // CORES) % n_z
    c = d % CORES

    def dp_at(xh_, z_, c_):
        return xh_ * (n_z * CORES) + z_ * CORES + c_

    def peer(k):
        return lax.rem(me + 1 + k, n_pipe)

    def z_peer(k):
        return dp_at(xh, lax.rem(z + 1 + k, n_z), c)

    sibling = dp_at(xh, z, 1 - c)
    xh_peer = dp_at(1 - xh, z, c)
    piece = group // XH
    my_rows = pl.ds(pl.multiple_of(xh * piece, piece), piece)
    other_rows = pl.ds(pl.multiple_of((1 - xh) * piece, piece), piece)

    def spread_to(s):
        u = (d % n_i) * per_block + s
        return u // CORES, u % CORES

    to_pipe = d // n_i
    my_u = z * CORES + c
    my_s = my_u % per_block

    def remote(src, dst, ssem, rsem, pp, dd):
        return pltpu.make_async_remote_copy(
            src_ref=src, dst_ref=dst, send_sem=ssem, recv_sem=rsem,
            device_id={"pipe": pp, "dp": dd}, device_id_type=pl.DeviceIdType.MESH,
        )

    def wait_bytes(ref, sem):
        pltpu.make_async_copy(ref, ref, sem).wait()

    def layers_of(pair):
        return pl.ds(2 * pair, 2)

    barrier = pltpu.get_barrier_semaphore()

    def greet(pp, dd):
        pl.semaphore_signal(
            barrier, inc=1, device_id={"pipe": pp, "dp": dd},
            device_id_type=pl.DeviceIdType.MESH,
        )

    for s in range(per_block):
        uz, uc = spread_to(s)
        for h in range(XH):
            dd = dp_at(h, uz, uc)

            @pl.when(dd != d)
            def _():
                greet(me, dd)

    for j in range(n_pipe):

        @pl.when(n_i * j + my_u // per_block != d)
        def _():
            greet(me, n_i * j + my_u // per_block)

    for k in range(n_z - 1):
        greet(me, z_peer(k))
    greet(me, sibling)
    greet(me, xh_peer)
    for k in range(n_pipe - 1):
        greet(peer(k), d)
        greet(peer(k), xh_peer)

    cols = pl.ds(pl.multiple_of(me * feat, feat), feat)
    top = 2 * pairs - 1
    loads = [
        pltpu.make_async_copy(x_down.at[:, cols], x.at[0, 0], load_sem.at[0]),
        pltpu.make_async_copy(x_up.at[:, cols], x.at[0, 1], load_sem.at[1]),
        pltpu.make_async_copy(cot_down.at[:, cols], dy.at[top, 0], load_sem.at[2]),
        pltpu.make_async_copy(cot_up.at[:, cols], dy.at[top, 1], load_sem.at[3]),
    ]
    for copy in loads:
        copy.start()

    blocks = mask_ref.shape[0]
    row = lax.broadcasted_iota(jnp.int32, (rows, rows), 0)
    col = lax.broadcasted_iota(jnp.int32, (rows, rows), 1)
    read = jnp.zeros((rows, rows), jnp.int32)
    for i in range(blocks):
        for j in range(blocks):
            inside = (row // (rows // blocks) == i) & (col // (rows // blocks) == j)
            read = jnp.where(inside, mask_ref[i, j], read)
    allowed[...] = jnp.where((read == 1) & (col <= row), 1.0, 0.0)

    wpack[:, :q3] = wq_ref[0]
    wpack[:, q3:] = wo_ref[0].astype(F32).T.astype(BF)

    itself = jnp.where(my_u // per_block == d % n_i, 1, 0)
    pl.semaphore_wait(barrier, 4 * n_pipe + n_z - 1 - 2 * itself)

    for s in range(per_block):
        uz, uc = spread_to(s)
        for h in range(XH):
            dd = dp_at(h, uz, uc)
            src = wpack.at[pl.ds((XH * s + h) * piece, piece)]

            @pl.when(dd != d)
            def _():
                remote(src, w1b.at[to_pipe], w1_send.at[XH * s + h], w1_recv.at[0], me, dd).start()

            @pl.when(dd == d)
            def _():
                pltpu.make_async_copy(src, w1b.at[to_pipe], w1_recv.at[0]).start()

    wait_bytes(w1b, w1_recv.at[0])
    held = w.at[me, z, c, my_rows]
    for k in range(n_pipe - 1):
        to = peer(k)
        remote(w1b.at[to], held, w2_send.at[0], w2_recv.at[0], to, d).start()
        remote(w1b.at[to], held, w2_send.at[1], w2_recv.at[0], to, xh_peer).start()
    remote(w1b.at[me], held, w2_send.at[1], w2_recv.at[0], me, xh_peer).start()
    pltpu.make_async_copy(w1b.at[me], held, w2_recv.at[0]).start()
    wait_bytes(w.at[:, z, c], w2_recv.at[0])

    two_steps = n_z == 8

    def z_at(step):
        return lax.rem(z + step + n_z, n_z)

    def start_wz(layer):
        mine = w.at[layer, z, c]
        steps = ((1, 0), (-1, 0), (2, 2), (-2, 1)) if two_steps else [(k + 1, 0) for k in range(n_z - 1)]
        for step, sem in steps:
            remote(
                mine, mine, wz_send.at[layer], wz_recv.at[layer, sem], me, dp_at(xh, z_at(step), c)
            ).start()

    def pass_wz(layer):
        if two_steps:
            for side, sem in ((1, 1), (-1, 2)):
                far = w.at[layer, z_at(2 * side), c]
                half = w.at[layer, z_at(2 * side), c, pl.ds(0 if side == 1 else piece, piece)]
                wait_bytes(far, wz_recv.at[layer, sem])
                for ref, step in ((far, -side), (half, -2 * side)):
                    remote(
                        ref, ref, wz_send.at[layer], wz_recv.at[layer, 3], me, dp_at(xh, z_at(step), c)
                    ).start()

    def start_wc(layer):
        if two_steps:
            wait_bytes(w.at[layer, pl.ds(0, 2), c], wz_recv.at[layer, 0])
            wait_bytes(w.at[layer, pl.ds(0, 3), c], wz_recv.at[layer, 3])
        else:
            wait_bytes(w.at[layer, pl.ds(0, n_z - 1), c], wz_recv.at[layer, 0])
        mine = w.at[layer, :, c]
        remote(mine, mine, wc_send.at[layer], wc_recv.at[layer], me, sibling).start()

    def wait_wc(layer):
        wait_bytes(w.at[layer, :, 1 - c], wc_recv.at[layer])

    start_wz(0)
    start_wz(1)

    def weight(layer):
        return w[layer].reshape(feat, width)

    for copy in loads:
        copy.wait()

    own = pl.ds(pl.multiple_of(me * rb, rb), rb)

    def scatter(src, dst, ssem, rsem):
        for k in range(n_pipe - 1):
            to = peer(k)
            remote(
                src.at[pl.ds(pl.multiple_of(to * rb, rb), rb)], dst.at[n_pipe - 2 - k], ssem, rsem, to, d
            ).start()

    def gather(ref, ssem, rsem):
        for k in range(n_pipe - 1):
            remote(ref.at[own], ref.at[own], ssem, rsem, peer(k), d).start()

    def wait_gather(ref, ssem, rsem):
        part = ref.at[pl.ds(0, rows - rb)]
        wait_bytes(part, rsem)
        wait_bytes(part, ssem)

    def start_rs_first(cas, xl, pair):
        xf = xl.astype(F32)
        sq = jnp.sum(xf * xf, axis=-1, keepdims=True)
        first = mm(xl, weight(2 * pair))
        rs_send[cas, 0, :, :q3] = first[:, :q3].astype(BF)
        rs_send[cas, 0, :, q3:] = jnp.broadcast_to(sq, (rows, HEAD)).astype(BF)
        scatter(rs_send.at[cas, 0], rs_recv.at[cas, 0], rs_ssem.at[cas, 0], rs_rsem.at[cas, 0])
        rs_send[cas, 1, :, :HEAD] = first[:, q3:].astype(BF)

    def start_rs_second(cas, xl, pair):
        rs_send[cas, 1, :, HEAD:] = mm(xl, weight(2 * pair + 1)[:, :q3]).astype(BF)
        scatter(rs_send.at[cas, 1], rs_recv.at[cas, 1], rs_ssem.at[cas, 1], rs_rsem.at[cas, 1])

    def start_ag(pair, cas, half):
        wait_bytes(rs_recv.at[cas, half], rs_rsem.at[cas, half])
        wait_bytes(rs_recv.at[cas, half], rs_ssem.at[cas, half])
        total = rs_send[cas, half, own].astype(F32)
        for k in range(n_pipe - 1):
            total = total + rs_recv[cas, half, k].astype(F32)
        if half == 0:
            norm = total[:, q3:]
            r = lax.rsqrt(norm * (1.0 / dim) + 1e-6)
            high = norm.astype(BF).astype(F32)
            lane = lax.broadcasted_iota(jnp.int32, norm.shape, 1)
            agb[pair, cas, 0, own, :q3] = (total[:, :q3] * r[:, :1]).astype(BF)
            agb[pair, cas, 0, own, q3:] = jnp.where(lane < HEAD // 2, high, norm - high).astype(BF)
        else:
            agb[pair, cas, 1, own] = total.astype(BF)
        gather(agb.at[pair, cas, half], ag_ssem.at[cas, half], ag_rsem.at[cas, half])

    def start_rs_gh(pair):
        w0 = weight(2 * pair)[:, q3:]
        gh_send[:, :q3] = mm_tn(w0, weight(2 * pair + 1)[:, :q3]).astype(BF)
        gh_send[:, q3:] = mm_tn(w0, w0).astype(BF)
        for k in range(n_pipe - 1):
            to = peer(k)
            gr = HEAD // n_pipe
            remote(
                gh_send.at[pl.ds(pl.multiple_of(to * gr, gr), gr)], gh_recv.at[pair, n_pipe - 2 - k],
                gh_ssem.at[0], gh_rsem.at[pair], to, d,
            ).start()

    gh_own = pl.ds(pl.multiple_of(me * (HEAD // n_pipe), HEAD // n_pipe), HEAD // n_pipe)

    def start_ag_gh(pair):
        wait_bytes(gh_recv.at[pair], gh_rsem.at[pair])
        wait_bytes(gh_recv.at[pair], gh_ssem.at[0])
        total = gh_send[gh_own].astype(F32)
        for k in range(n_pipe - 1):
            total = total + gh_recv[pair, k].astype(F32)
        ghb[pair, gh_own] = total.astype(BF)
        ref = ghb.at[pair, gh_own]
        for k in range(n_pipe - 1):
            remote(ref, ref, ha_ssem.at[pair], ha_rsem.at[pair], peer(k), d).start()

    def wait_ag_gh(pair):
        part = ghb.at[pair, pl.ds(0, HEAD - HEAD // n_pipe)]
        wait_bytes(part, ha_rsem.at[pair])
        wait_bytes(part, ha_ssem.at[pair])

    def attend(layer, cas, pr):
        s = mm_nt(pr[:, :HEAD], pr[:, HEAD : 2 * HEAD]) * scale
        s = jnp.where(allowed[...] > 0.5, s, -1e30)
        ex = jnp.exp(s - jnp.max(s, axis=-1, keepdims=True))
        sm = (ex / jnp.sum(ex, axis=-1, keepdims=True)).astype(BF)
        soft[layer, cas] = sm
        a = mm(sm, pr[:, 2 * HEAD : q3]).astype(BF)
        att[layer, cas] = a
        return a

    pass_wz(0)
    pass_wz(1)
    if pairs > 1:
        start_wz(2)
        start_wz(3)
    start_wc(0)
    wait_wc(0)
    for cas in range(2):
        start_rs_first(cas, x[0, cas], 0)
    start_wc(1)
    if pairs > 1:
        pass_wz(2)
        pass_wz(3)
    wait_wc(1)
    for cas in range(2):
        start_rs_second(cas, x[0, cas], 0)
    start_rs_gh(0)
    if pairs > 2:
        start_wz(4)
        start_wz(5)

    def start_ds(cas, dyl, pair):
        ds_send[cas, :, :HEAD] = mm(dyl, weight(2 * pair)[:, q3:]).astype(BF)
        ds_send[cas, :, HEAD:] = mm(dyl, weight(2 * pair + 1)[:, q3:]).astype(BF)
        scatter(ds_send.at[cas], ds_recv.at[cas], ds_ssem.at[cas], ds_rsem.at[cas])

    def start_da(cas):
        wait_bytes(ds_recv.at[cas], ds_rsem.at[cas])
        wait_bytes(ds_recv.at[cas], ds_ssem.at[cas])
        total = ds_send[cas, own].astype(F32)
        for k in range(n_pipe - 1):
            total = total + ds_recv[cas, k].astype(F32)
        da[cas, own] = total.astype(BF)
        gather(da.at[cas], da_ssem.at[cas], da_rsem.at[cas])

    def forward(pair, carry):
        l0 = 2 * pair
        l1 = l0 + 1
        for cas in range(2):
            for half in range(2):
                start_ag(pair, cas, half)

        @pl.when(pair == 0)
        def _():
            start_ag_gh(0)

        @pl.when(pair == end)
        def _():
            for cas in range(2):
                start_ds(cas, dy[top, cas], end)

        @pl.when(pair < end)
        def _():
            start_wc(l0 + 2)
            start_wc(l1 + 2)

            @pl.when(pair + 2 < pairs)
            def _():
                pass_wz(l0 + 4)
                pass_wz(l1 + 4)

            @pl.when(pair + 3 < pairs)
            def _():
                start_wz(l0 + 6)
                start_wz(l1 + 6)

            wait_wc(l0 + 2)
            wait_wc(l1 + 2)
            start_rs_gh(pair + 1)

        for cas in range(2):
            wait_gather(agb.at[pair, cas, 0], ag_ssem.at[cas, 0], ag_rsem.at[cas, 0])
            a0 = attend(l0, cas, agb[pair, cas, 0, :, :q3])
            half_lane = width - HEAD // 2
            n0 = (
                agb[pair, cas, 0, :, q3 : q3 + 1].astype(F32)
                + agb[pair, cas, 0, :, half_lane : half_lane + 1].astype(F32)
            )
            x1 = (x[l0, cas].astype(F32) + mm_nt(a0, weight(l0)[:, q3:])).astype(BF)
            x[l1, cas] = x1
            if cas == 0:
                wait_ag_gh(pair)
            agh = mm(a0, ghb[pair])
            wait_gather(agb.at[pair, cas, 1], ag_ssem.at[cas, 1], ag_rsem.at[cas, 1])
            c0 = agb[pair, cas, 1, :, :HEAD].astype(F32)
            v = agh[:, q3:]
            n1 = n0 + jnp.sum(a0.astype(F32) * (2.0 * c0 + v), axis=-1, keepdims=True)
            t1[pair, cas] = c0 + v
            r0 = lax.rsqrt(n0 * (1.0 / dim) + 1e-6)
            r1 = lax.rsqrt(jnp.maximum(n1, 0.0) * (1.0 / dim) + 1e-6)
            rbuf[l0, cas] = jnp.broadcast_to(r0, (rows, HEAD))
            rbuf[l1, cas] = jnp.broadcast_to(r1, (rows, HEAD))
            pr1 = ((agb[pair, cas, 1, :, HEAD:].astype(F32) + agh[:, :q3]) * r1).astype(BF)
            p1[pair, cas] = pr1
            a1 = attend(l1, cas, pr1)

            @pl.when(pair < end)
            def _():
                x2 = (x1.astype(F32) + mm_nt(a1, weight(l1)[:, q3:])).astype(BF)
                x[l1 + 1, cas] = x2
                start_rs_first(cas, x2, pair + 1)
                start_rs_second(cas, x2, pair + 1)

        @pl.when(pair < end)
        def _():
            start_ag_gh(pair + 1)

        return carry

    lax.fori_loop(0, pairs, forward, 0)

    def attend_back(layer, cas, slot, pr, da):
        sm = soft[layer, cas]
        smf = sm.astype(F32)
        r = rbuf[layer, cas]
        dv = mm_tn(sm, da)
        dsm = mm_nt(da, pr[:, 2 * HEAD :])
        ds = (smf * (dsm - jnp.sum(dsm * smf, axis=-1, keepdims=True)) * scale).astype(BF)
        dq = mm(ds, pr[:, HEAD : 2 * HEAD])
        dk = mm_tn(ds, pr[:, :HEAD])
        prf = pr.astype(F32)
        dot = jnp.sum(
            dq * prf[:, :HEAD] + dk * prf[:, HEAD : 2 * HEAD] + dv * prf[:, 2 * HEAD :], axis=-1, keepdims=True
        )
        e_buf[slot, cas, :, :HEAD] = (dq * r).astype(BF)
        e_buf[slot, cas, :, HEAD : 2 * HEAD] = (dk * r).astype(BF)
        e_buf[slot, cas, :, 2 * HEAD :] = (dv * r).astype(BF)
        return r[:, :1] * r[:, :1] * dot * (1.0 / dim)

    def weight_grads(layer, i):
        xl = x[layer].reshape(2 * rows, feat)
        dyl = dy[layer].reshape(2 * rows, feat)
        gq = mm_tn(xl, e_buf[i].reshape(2 * rows, q3)).astype(BF)
        go = mm_tn(dyl, att[layer].reshape(2 * rows, HEAD)).astype(BF)
        g[layer, :, :, :, :q3] = gq.reshape(n_z, CORES, group, q3)
        g[layer, :, :, :, q3:] = go.reshape(n_z, CORES, group, HEAD)
        remote(
            g.at[layer, :, 1 - c], gd.at[layer], gc_send.at[layer], gc_recv.at[layer], me, sibling
        ).start()

    start_da(0)

    def backward(t, carry):
        pair = end - t
        l0 = 2 * pair
        l1 = l0 + 1

        @pl.when(t < pairs)
        def _():
            start_da(1)

        @pl.when((t >= 1) & (t < pairs + 1))
        def _():
            for i in (1, 0):
                lay = 2 * (pair + 1) + i
                wait_bytes(gd.at[lay], gc_recv.at[lay])
                mine = (lay, slice(None), pl.ds(c, 1))
                g[mine] = (g[mine].astype(F32) + gd[lay][:, None].astype(F32)).astype(BF)
                remote(
                    g.at[lay, :, c, other_rows], gxr.at[lay], gs_send.at[lay], gs_recv.at[lay], me, xh_peer
                ).start()

        @pl.when(t < pairs)
        def _():
            for cas in range(2):
                wait_gather(da.at[cas], da_ssem.at[cas], da_rsem.at[cas])
                cc1 = attend_back(l1, cas, 1, p1[pair, cas], da[cas, :, HEAD:])
                e1 = e_buf[1, cas]
                da0[cas] = (da[cas, :, :HEAD].astype(F32) + mm_nt(e1, ghb[pair][:, :q3]) - cc1 * t1[pair, cas]).astype(BF)
                dy[l0, cas] = (
                    dy[l1, cas].astype(F32) + mm_nt(e1, weight(l1)[:, :q3]) - x[l1, cas].astype(F32) * cc1
                ).astype(BF)

                @pl.when(pair > 0)
                def _():
                    cc0 = attend_back(l0, cas, 0, agb[pair, cas, 0, :, :q3], da0[cas])
                    dy_new = (
                        dy[l0, cas].astype(F32)
                        + mm_nt(e_buf[0, cas], weight(l0)[:, :q3])
                        - x[l0, cas].astype(F32) * cc0
                    ).astype(BF)
                    dy[l0 - 1, cas] = dy_new
                    start_ds(cas, dy_new, pair - 1)

            @pl.when(pair == 0)
            def _():
                weight_grads(l1, 1)
                for cas in range(2):
                    attend_back(l0, cas, 0, agb[pair, cas, 0, :, :q3], da0[cas])

        @pl.when(t < end)
        def _():
            start_da(0)

        @pl.when((t >= 1) & (t < pairs + 1))
        def _():
            for i in (1, 0):
                lay = 2 * (pair + 1) + i
                wait_bytes(gxr.at[lay], gs_recv.at[lay])
                mine = (lay, slice(None), pl.ds(c, 1), my_rows)
                g[mine] = (g[mine].astype(F32) + gxr[lay][:, None].astype(F32)).astype(BF)
                for k in range(n_z - 1):
                    to_z = lax.rem(z + 1 + k, n_z)
                    remote(
                        g.at[lay, to_z, c, my_rows], gz.at[lay, n_z - 2 - k],
                        gz_send.at[lay], gz_recv.at[lay], me, z_peer(k),
                    ).start()

        @pl.when((t >= 2) & (t < pairs + 2))
        def _():
            for i in (1, 0):
                lay = 2 * (pair + 2) + i
                wait_bytes(gz.at[lay], gz_recv.at[lay])
                total = g[lay, z, c, my_rows].astype(F32)
                for k in range(n_z - 1):
                    total = total + gz[lay, k].astype(F32)
                gx[lay] = total.astype(BF)

        @pl.when((t < pairs) & (pair > 0))
        def _():
            weight_grads(l1, 1)

        @pl.when(t < pairs)
        def _():
            weight_grads(l0, 0)

        return carry

    lax.fori_loop(0, pairs + 2, backward, 0)

    for k in range(n_pipe - 1):
        to = peer(k)
        remote(gx.at[to], hp.at[me], hp_send.at[0], hp_recv.at[0], to, d).start()
    hp[pl.ds(me, 1)] = gx[pl.ds(me, 1)]
    wait_bytes(hp.at[pl.ds(0, n_pipe - 1)], hp_recv.at[0])
    for k in range(n_pipe):
        pp = lax.rem(me + k, n_pipe)
        dd = n_i * pp + my_u // per_block

        @pl.when(dd != d)
        def _():
            remote(hp.at[pp], out.at[my_s, xh], gf_send.at[pp], gf_recv.at[0], me, dd).start()

        @pl.when(dd == d)
        def _():
            pltpu.make_async_copy(hp.at[pp], out.at[my_s, xh], gf_recv.at[0]).start()

    wait_bytes(out, gf_recv.at[0])
    full = out[...].astype(F32).reshape(per_block * group, width)
    gq_ref[0] = full[:, :q3]
    go_ref[0] = full[:, q3:].T

    for s in range(per_block):
        uz, uc = spread_to(s)
        for h in range(XH):
            dd = dp_at(h, uz, uc)

            @pl.when(dd != d)
            def _():
                wait_bytes(wpack.at[pl.ds((XH * s + h) * piece, piece)], w1_send.at[XH * s + h])

    wait_bytes(w1b.at[pl.ds(0, n_pipe - 1)], w2_send.at[0])
    wait_bytes(w1b, w2_send.at[1])
    wait_bytes(hp.at[pl.ds(0, n_pipe - 1)], hp_send.at[0])

    def drain(lay, carry):
        wait_bytes(w.at[lay, pl.ds(0, n_z - 1), c], wz_send.at[lay])
        wait_bytes(w.at[lay, :, c], wc_send.at[lay])
        wait_bytes(gd.at[lay], gc_send.at[lay])
        wait_bytes(gxr.at[lay], gs_send.at[lay])
        wait_bytes(gz.at[lay], gz_send.at[lay])

        @pl.when(n_i * lay + my_u // per_block != d)
        def _():
            wait_bytes(hp.at[lay], gf_send.at[lay])

        return carry

    lax.fori_loop(0, n_pipe, drain, 0)


def per_device(x_down, x_up, cot_down, cot_up, w_qkv, w_out, block_mask):
    n_pipe, n_dp = lax.axis_size("pipe"), lax.axis_size("dp")
    rows, dim = x_down.shape
    feat = dim // n_pipe
    n_z = n_dp // (XH * CORES)
    group = feat // (n_z * CORES)
    per_block = n_pipe // XH
    width = 4 * HEAD
    rb = rows // n_pipe
    layers = n_pipe
    pairs = layers // 2
    any_spec = pl.BlockSpec(memory_space=pl.ANY)
    vmem = pl.BlockSpec(memory_space=pltpu.VMEM)
    dma = pltpu.SemaphoreType.DMA
    return pl.pallas_call(
        functools.partial(kernel, n_pipe, n_dp),
        out_shape=(
            jax.ShapeDtypeStruct(w_qkv.shape, F32),
            jax.ShapeDtypeStruct(w_out.shape, F32),
        ),
        in_specs=[any_spec] * 4 + [vmem] * 2 + [pl.BlockSpec(memory_space=pltpu.SMEM)],
        out_specs=(vmem, vmem),
        scratch_shapes=[
            pltpu.VMEM((rows, rows), F32),
            pltpu.VMEM((per_block * group, width), BF),
            pltpu.VMEM((n_pipe, group // XH, width), BF),
            pltpu.VMEM((layers, n_z, CORES, group, width), BF),
            pltpu.VMEM((layers, 2, rows, feat), BF),
            pltpu.VMEM((layers, 2, rows, feat), BF),
            pltpu.VMEM((pairs, 2, 2, rows, width), BF),
            pltpu.VMEM((pairs, 2, rows, 3 * HEAD), BF),
            pltpu.VMEM((layers, 2, rows, rows), BF),
            pltpu.VMEM((layers, 2, rows, HEAD), BF),
            pltpu.VMEM((pairs, 2, rows, HEAD), F32),
            pltpu.VMEM((layers, 2, rows, HEAD), F32),
            pltpu.VMEM((2, 2, rows, 3 * HEAD), BF),
            pltpu.VMEM((2, 2, rows, width), BF),
            pltpu.VMEM((2, 2, n_pipe - 1, rb, width), BF),
            pltpu.VMEM((HEAD, width), BF),
            pltpu.VMEM((pairs, n_pipe - 1, HEAD // n_pipe, width), BF),
            pltpu.VMEM((pairs, HEAD, width), BF),
            pltpu.VMEM((2, rows, 2 * HEAD), BF),
            pltpu.VMEM((2, n_pipe - 1, rb, 2 * HEAD), BF),
            pltpu.VMEM((2, rows, 2 * HEAD), BF),
            pltpu.VMEM((2, rows, HEAD), BF),
            pltpu.VMEM((layers, n_z, CORES, group, width), BF),
            pltpu.VMEM((layers, n_z, group, width), BF),
            pltpu.VMEM((layers, n_z, group // XH, width), BF),
            pltpu.VMEM((layers, n_z - 1, group // XH, width), BF),
            pltpu.VMEM((layers, group // XH, width), BF),
            pltpu.VMEM((layers, group // XH, width), BF),
            pltpu.VMEM((per_block, XH, group // XH, width), BF),
            dma((4,)),
            dma((n_pipe,)), dma((1,)),
            dma((2,)), dma((1,)),
            dma((layers,)), dma((layers, 4)),
            dma((layers,)), dma((layers,)),
            dma((2, 2)), dma((2, 2)), dma((2, 2)), dma((2, 2)),
            dma((1,)), dma((pairs,)), dma((pairs,)), dma((pairs,)),
            dma((2,)), dma((2,)), dma((2,)), dma((2,)),
            dma((layers,)), dma((layers,)),
            dma((layers,)), dma((layers,)),
            dma((layers,)), dma((layers,)),
            dma((1,)), dma((1,)),
            dma((layers,)), dma((1,)),
        ],
        compiler_params=pltpu.CompilerParams(
            collective_id=0, has_side_effects=True, vmem_limit_bytes=60 * 1024 * 1024
        ),
    )(x_down, x_up, cot_down, cot_up, w_qkv, w_out, block_mask)


def solution(mesh):
    placed = (
        P("dp", None),
        P("dp", None),
        P("dp", None),
        P("dp", None),
        P("pipe", "dp", None),
        P("pipe", None, "dp"),
        P(),
    )
    return jax.shard_map(
        per_device,
        mesh=mesh,
        in_specs=placed,
        out_specs=(P("pipe", "dp", None), P("pipe", None, "dp")),
        check_vma=False,
    )
```

```python
import functools

import jax
import jax.numpy as jnp
from jax import lax
from jax.experimental import pallas as pl
from jax.experimental.pallas import tpu as pltpu
from jax.sharding import PartitionSpec as P

BLK = 32
HEAD = 128
XH = 2
CORES = 2
BF = jnp.bfloat16
F32 = jnp.float32

NT = (((1,), (1,)), ((), ()))
TN = (((0,), (0,)), ((), ()))


def mm(a, b):
    return jnp.dot(a, b, preferred_element_type=F32)


def mm_nt(a, b):
    return lax.dot_general(a, b, NT, preferred_element_type=F32)


def mm_tn(a, b):
    return lax.dot_general(a, b, TN, preferred_element_type=F32)


def kernel(
    n_pipe,
    n_dp,
    x_down, x_up, cot_down, cot_up, wq_ref, wo_ref, mask_ref,
    gq_ref, go_ref,
    allowed, wpack, w1b, w, x, dy, agb, p1, soft, att, t1, rbuf, e_buf,
    rs_send, rs_recv, gh_send, gh_recv, ghb, ds_send, ds_recv, da, da0,
    g, gd, gxr, gz, gx, gyr, gf, hp, out,
    load_sem, w1_send, w1_recv, w2_send, w2_recv, wz_send, wz_recv, wc_send, wc_recv,
    rs_ssem, rs_rsem, ag_ssem, ag_rsem, gh_ssem, gh_rsem, ha_ssem, ha_rsem, ds_ssem, ds_rsem, da_ssem, da_rsem,
    gc_send, gc_recv, gs_send, gs_recv, gy_send, gy_recv, gz_send, gz_recv, hp_send, hp_recv, gf_send, gf_recv,
):
    pairs = n_pipe // 2
    n_z = n_dp // (XH * CORES)
    n_i = n_dp // n_pipe
    rows = x.shape[2]
    feat = x.shape[3]
    dim = feat * n_pipe
    group = w.shape[3]
    per_block = n_pipe // XH
    rb = rows // n_pipe
    end = pairs - 1
    q3 = 3 * HEAD
    width = 4 * HEAD
    scale = HEAD ** (-0.5)

    me = lax.axis_index("pipe")
    d = lax.axis_index("dp")
    xh = d // (n_z * CORES)
    z = (d // CORES) % n_z
    c = d % CORES

    def dp_at(xh_, z_, c_):
        return xh_ * (n_z * CORES) + z_ * CORES + c_

    def peer(k):
        return lax.rem(me + 1 + k, n_pipe)

    def z_peer(k):
        return dp_at(xh, lax.rem(z + 1 + k, n_z), c)

    sibling = dp_at(xh, z, 1 - c)
    xh_peer = dp_at(1 - xh, z, c)
    piece = group // XH
    my_rows = pl.ds(pl.multiple_of(xh * piece, piece), piece)
    other_rows = pl.ds(pl.multiple_of((1 - xh) * piece, piece), piece)

    def spread_to(s):
        u = (d % n_i) * per_block + s
        return u // CORES, u % CORES

    to_pipe = d // n_i
    my_u = z * CORES + c
    my_s = my_u % per_block

    def remote(src, dst, ssem, rsem, pp, dd):
        return pltpu.make_async_remote_copy(
            src_ref=src, dst_ref=dst, send_sem=ssem, recv_sem=rsem,
            device_id={"pipe": pp, "dp": dd}, device_id_type=pl.DeviceIdType.MESH,
        )

    def wait_bytes(ref, sem):
        pltpu.make_async_copy(ref, ref, sem).wait()

    def layers_of(pair):
        return pl.ds(2 * pair, 2)

    barrier = pltpu.get_barrier_semaphore()

    def greet(pp, dd):
        pl.semaphore_signal(
            barrier, inc=1, device_id={"pipe": pp, "dp": dd},
            device_id_type=pl.DeviceIdType.MESH,
        )

    for s in range(per_block):
        uz, uc = spread_to(s)
        for h in range(XH):
            dd = dp_at(h, uz, uc)

            @pl.when(dd != d)
            def _():
                greet(me, dd)

    for j in range(n_pipe):

        @pl.when(n_i * j + my_u // per_block != d)
        def _():
            greet(me, n_i * j + my_u // per_block)

    for k in range(n_z - 1):
        greet(me, z_peer(k))
    greet(me, sibling)
    greet(me, xh_peer)
    for k in range(n_pipe - 1):
        greet(peer(k), d)
        greet(peer(k), xh_peer)

    cols = pl.ds(pl.multiple_of(me * feat, feat), feat)
    top = 2 * pairs - 1
    loads = [
        pltpu.make_async_copy(x_down.at[:, cols], x.at[0, 0], load_sem.at[0]),
        pltpu.make_async_copy(x_up.at[:, cols], x.at[0, 1], load_sem.at[1]),
        pltpu.make_async_copy(cot_down.at[:, cols], dy.at[top, 0], load_sem.at[2]),
        pltpu.make_async_copy(cot_up.at[:, cols], dy.at[top, 1], load_sem.at[3]),
    ]
    for copy in loads:
        copy.start()

    blocks = mask_ref.shape[0]
    row = lax.broadcasted_iota(jnp.int32, (rows, rows), 0)
    col = lax.broadcasted_iota(jnp.int32, (rows, rows), 1)
    read = jnp.zeros((rows, rows), jnp.int32)
    for i in range(blocks):
        for j in range(blocks):
            inside = (row // (rows // blocks) == i) & (col // (rows // blocks) == j)
            read = jnp.where(inside, mask_ref[i, j], read)
    allowed[...] = jnp.where((read == 1) & (col <= row), 1.0, 0.0)

    wpack[:, :q3] = wq_ref[0]
    wpack[:, q3:] = wo_ref[0].astype(F32).T.astype(BF)

    itself = jnp.where(my_u // per_block == d % n_i, 1, 0)
    pl.semaphore_wait(barrier, 4 * n_pipe + n_z - 1 - 2 * itself)

    for s in range(per_block):
        uz, uc = spread_to(s)
        for h in range(XH):
            dd = dp_at(h, uz, uc)
            src = wpack.at[pl.ds((XH * s + h) * piece, piece)]

            @pl.when(dd != d)
            def _():
                remote(src, w1b.at[to_pipe], w1_send.at[XH * s + h], w1_recv.at[0], me, dd).start()

            @pl.when(dd == d)
            def _():
                pltpu.make_async_copy(src, w1b.at[to_pipe], w1_recv.at[0]).start()

    wait_bytes(w1b, w1_recv.at[0])
    held = w.at[me, z, c, my_rows]
    for k in range(n_pipe - 1):
        to = peer(k)
        remote(w1b.at[to], held, w2_send.at[0], w2_recv.at[0], to, d).start()
        remote(w1b.at[to], held, w2_send.at[1], w2_recv.at[0], to, xh_peer).start()
    remote(w1b.at[me], held, w2_send.at[1], w2_recv.at[0], me, xh_peer).start()
    pltpu.make_async_copy(w1b.at[me], held, w2_recv.at[0]).start()
    wait_bytes(w.at[:, z, c], w2_recv.at[0])

    two_steps = n_z == 8

    def z_at(step):
        return lax.rem(z + step + n_z, n_z)

    def start_wz(layer):
        mine = w.at[layer, z, c]
        steps = ((1, 0), (-1, 0), (2, 2), (-2, 1)) if two_steps else [(k + 1, 0) for k in range(n_z - 1)]
        for step, sem in steps:
            remote(
                mine, mine, wz_send.at[layer], wz_recv.at[layer, sem], me, dp_at(xh, z_at(step), c)
            ).start()

    def pass_wz(layer):
        if two_steps:
            for side, sem in ((1, 1), (-1, 2)):
                far = w.at[layer, z_at(2 * side), c]
                half = w.at[layer, z_at(2 * side), c, pl.ds(0 if side == 1 else piece, piece)]
                wait_bytes(far, wz_recv.at[layer, sem])
                for ref, step in ((far, -side), (half, -2 * side)):
                    remote(
                        ref, ref, wz_send.at[layer], wz_recv.at[layer, 3], me, dp_at(xh, z_at(step), c)
                    ).start()

    def start_wc(layer):
        if two_steps:
            wait_bytes(w.at[layer, pl.ds(0, 2), c], wz_recv.at[layer, 0])
            wait_bytes(w.at[layer, pl.ds(0, 3), c], wz_recv.at[layer, 3])
        else:
            wait_bytes(w.at[layer, pl.ds(0, n_z - 1), c], wz_recv.at[layer, 0])
        mine = w.at[layer, :, c]
        remote(mine, mine, wc_send.at[layer], wc_recv.at[layer], me, sibling).start()

    def wait_wc(layer):
        wait_bytes(w.at[layer, :, 1 - c], wc_recv.at[layer])

    start_wz(0)
    start_wz(1)

    def weight(layer):
        return w[layer].reshape(feat, width)

    for copy in loads:
        copy.wait()

    own = pl.ds(pl.multiple_of(me * rb, rb), rb)

    def scatter(src, dst, ssem, rsem):
        for k in range(n_pipe - 1):
            to = peer(k)
            remote(
                src.at[pl.ds(pl.multiple_of(to * rb, rb), rb)], dst.at[n_pipe - 2 - k], ssem, rsem, to, d
            ).start()

    def gather(ref, ssem, rsem):
        for k in range(n_pipe - 1):
            remote(ref.at[own], ref.at[own], ssem, rsem, peer(k), d).start()

    def wait_gather(ref, ssem, rsem):
        part = ref.at[pl.ds(0, rows - rb)]
        wait_bytes(part, rsem)
        wait_bytes(part, ssem)

    def start_rs_first(cas, xl, pair):
        xf = xl.astype(F32)
        sq = jnp.sum(xf * xf, axis=-1, keepdims=True)
        first = mm(xl, weight(2 * pair))
        rs_send[cas, 0, :, :q3] = first[:, :q3].astype(BF)
        rs_send[cas, 0, :, q3:] = jnp.broadcast_to(sq, (rows, HEAD)).astype(BF)
        scatter(rs_send.at[cas, 0], rs_recv.at[cas, 0], rs_ssem.at[cas, 0], rs_rsem.at[cas, 0])
        rs_send[cas, 1, :, :HEAD] = first[:, q3:].astype(BF)

    def start_rs_second(cas, xl, pair):
        rs_send[cas, 1, :, HEAD:] = mm(xl, weight(2 * pair + 1)[:, :q3]).astype(BF)
        scatter(rs_send.at[cas, 1], rs_recv.at[cas, 1], rs_ssem.at[cas, 1], rs_rsem.at[cas, 1])

    def start_ag(pair, cas, half):
        wait_bytes(rs_recv.at[cas, half], rs_rsem.at[cas, half])
        wait_bytes(rs_recv.at[cas, half], rs_ssem.at[cas, half])
        total = rs_send[cas, half, own].astype(F32)
        for k in range(n_pipe - 1):
            total = total + rs_recv[cas, half, k].astype(F32)
        if half == 0:
            norm = total[:, q3:]
            r = lax.rsqrt(norm * (1.0 / dim) + 1e-6)
            high = norm.astype(BF).astype(F32)
            lane = lax.broadcasted_iota(jnp.int32, norm.shape, 1)
            agb[pair, cas, 0, own, :q3] = (total[:, :q3] * r[:, :1]).astype(BF)
            agb[pair, cas, 0, own, q3:] = jnp.where(lane < HEAD // 2, high, norm - high).astype(BF)
        else:
            agb[pair, cas, 1, own] = total.astype(BF)
        gather(agb.at[pair, cas, half], ag_ssem.at[cas, half], ag_rsem.at[cas, half])

    def start_rs_gh(pair):
        w0 = weight(2 * pair)[:, q3:]
        gh_send[:, :q3] = mm_tn(w0, weight(2 * pair + 1)[:, :q3]).astype(BF)
        gh_send[:, q3:] = mm_tn(w0, w0).astype(BF)
        for k in range(n_pipe - 1):
            to = peer(k)
            gr = HEAD // n_pipe
            remote(
                gh_send.at[pl.ds(pl.multiple_of(to * gr, gr), gr)], gh_recv.at[pair, n_pipe - 2 - k],
                gh_ssem.at[0], gh_rsem.at[pair], to, d,
            ).start()

    gh_own = pl.ds(pl.multiple_of(me * (HEAD // n_pipe), HEAD // n_pipe), HEAD // n_pipe)

    def start_ag_gh(pair):
        wait_bytes(gh_recv.at[pair], gh_rsem.at[pair])
        wait_bytes(gh_recv.at[pair], gh_ssem.at[0])
        total = gh_send[gh_own].astype(F32)
        for k in range(n_pipe - 1):
            total = total + gh_recv[pair, k].astype(F32)
        ghb[pair, gh_own] = total.astype(BF)
        ref = ghb.at[pair, gh_own]
        for k in range(n_pipe - 1):
            remote(ref, ref, ha_ssem.at[pair], ha_rsem.at[pair], peer(k), d).start()

    def wait_ag_gh(pair):
        part = ghb.at[pair, pl.ds(0, HEAD - HEAD // n_pipe)]
        wait_bytes(part, ha_rsem.at[pair])
        wait_bytes(part, ha_ssem.at[pair])

    def attend(layer, cas, pr):
        s = mm_nt(pr[:, :HEAD], pr[:, HEAD : 2 * HEAD]) * scale
        s = jnp.where(allowed[...] > 0.5, s, -1e30)
        ex = jnp.exp(s - jnp.max(s, axis=-1, keepdims=True))
        sm = (ex / jnp.sum(ex, axis=-1, keepdims=True)).astype(BF)
        soft[layer, cas] = sm
        a = mm(sm, pr[:, 2 * HEAD : q3]).astype(BF)
        att[layer, cas] = a
        return a

    pass_wz(0)
    pass_wz(1)
    if pairs > 1:
        start_wz(2)
        start_wz(3)
    start_wc(0)
    wait_wc(0)
    for cas in range(2):
        start_rs_first(cas, x[0, cas], 0)
    start_wc(1)
    if pairs > 1:
        pass_wz(2)
        pass_wz(3)
    wait_wc(1)
    start_rs_gh(0)
    for cas in range(2):
        start_rs_second(cas, x[0, cas], 0)
    if pairs > 2:
        start_wz(4)
        start_wz(5)

    def start_ds(cas, dyl, pair):
        ds_send[cas, :, :HEAD] = mm(dyl, weight(2 * pair)[:, q3:]).astype(BF)
        ds_send[cas, :, HEAD:] = mm(dyl, weight(2 * pair + 1)[:, q3:]).astype(BF)
        scatter(ds_send.at[cas], ds_recv.at[cas], ds_ssem.at[cas], ds_rsem.at[cas])

    def start_da(cas):
        wait_bytes(ds_recv.at[cas], ds_rsem.at[cas])
        wait_bytes(ds_recv.at[cas], ds_ssem.at[cas])
        total = ds_send[cas, own].astype(F32)
        for k in range(n_pipe - 1):
            total = total + ds_recv[cas, k].astype(F32)
        da[cas, own] = total.astype(BF)
        gather(da.at[cas], da_ssem.at[cas], da_rsem.at[cas])

    def forward(pair, carry):
        l0 = 2 * pair
        l1 = l0 + 1
        for cas in range(2):
            for half in range(2):
                start_ag(pair, cas, half)
                if cas == 0 and half == 0:

                    @pl.when(pair == 0)
                    def _():
                        start_ag_gh(0)

        @pl.when(pair == end)
        def _():
            for cas in range(2):
                start_ds(cas, dy[top, cas], end)

        @pl.when(pair < end)
        def _():
            start_wc(l0 + 2)
            start_wc(l1 + 2)

            @pl.when(pair + 2 < pairs)
            def _():
                pass_wz(l0 + 4)
                pass_wz(l1 + 4)

            @pl.when(pair + 3 < pairs)
            def _():
                start_wz(l0 + 6)
                start_wz(l1 + 6)

            wait_wc(l0 + 2)
            wait_wc(l1 + 2)
            start_rs_gh(pair + 1)

        for cas in range(2):
            wait_gather(agb.at[pair, cas, 0], ag_ssem.at[cas, 0], ag_rsem.at[cas, 0])
            a0 = attend(l0, cas, agb[pair, cas, 0, :, :q3])
            half_lane = width - HEAD // 2
            n0 = (
                agb[pair, cas, 0, :, q3 : q3 + 1].astype(F32)
                + agb[pair, cas, 0, :, half_lane : half_lane + 1].astype(F32)
            )
            x1 = (x[l0, cas].astype(F32) + mm_nt(a0, weight(l0)[:, q3:])).astype(BF)
            x[l1, cas] = x1
            if cas == 0:
                wait_ag_gh(pair)
            agh = mm(a0, ghb[pair])
            wait_gather(agb.at[pair, cas, 1], ag_ssem.at[cas, 1], ag_rsem.at[cas, 1])
            c0 = agb[pair, cas, 1, :, :HEAD].astype(F32)
            v = agh[:, q3:]
            n1 = n0 + jnp.sum(a0.astype(F32) * (2.0 * c0 + v), axis=-1, keepdims=True)
            t1[pair, cas] = c0 + v
            r0 = lax.rsqrt(n0 * (1.0 / dim) + 1e-6)
            r1 = lax.rsqrt(jnp.maximum(n1, 0.0) * (1.0 / dim) + 1e-6)
            rbuf[l0, cas] = jnp.broadcast_to(r0, (rows, HEAD))
            rbuf[l1, cas] = jnp.broadcast_to(r1, (rows, HEAD))
            pr1 = ((agb[pair, cas, 1, :, HEAD:].astype(F32) + agh[:, :q3]) * r1).astype(BF)
            p1[pair, cas] = pr1
            a1 = attend(l1, cas, pr1)

            @pl.when(pair < end)
            def _():
                x2 = (x1.astype(F32) + mm_nt(a1, weight(l1)[:, q3:])).astype(BF)
                x[l1 + 1, cas] = x2
                start_rs_first(cas, x2, pair + 1)
                start_rs_second(cas, x2, pair + 1)

        @pl.when(pair < end)
        def _():
            start_ag_gh(pair + 1)

        return carry

    lax.fori_loop(0, pairs, forward, 0)

    def attend_back(layer, cas, slot, pr, da):
        sm = soft[layer, cas]
        smf = sm.astype(F32)
        r = rbuf[layer, cas]
        dv = mm_tn(sm, da)
        dsm = mm_nt(da, pr[:, 2 * HEAD :])
        ds = (smf * (dsm - jnp.sum(dsm * smf, axis=-1, keepdims=True)) * scale).astype(BF)
        dq = mm(ds, pr[:, HEAD : 2 * HEAD])
        dk = mm_tn(ds, pr[:, :HEAD])
        prf = pr.astype(F32)
        dot = jnp.sum(
            dq * prf[:, :HEAD] + dk * prf[:, HEAD : 2 * HEAD] + dv * prf[:, 2 * HEAD :], axis=-1, keepdims=True
        )
        e_buf[slot, cas, :, :HEAD] = (dq * r).astype(BF)
        e_buf[slot, cas, :, HEAD : 2 * HEAD] = (dk * r).astype(BF)
        e_buf[slot, cas, :, 2 * HEAD :] = (dv * r).astype(BF)
        return r[:, :1] * r[:, :1] * dot * (1.0 / dim)

    def weight_grads(layer, i):
        xl = x[layer].reshape(2 * rows, feat)
        dyl = dy[layer].reshape(2 * rows, feat)
        gq = mm_tn(xl, e_buf[i].reshape(2 * rows, q3)).astype(BF)
        go = mm_tn(dyl, att[layer].reshape(2 * rows, HEAD)).astype(BF)
        g[layer, :, :, :, :q3] = gq.reshape(n_z, CORES, group, q3)
        g[layer, :, :, :, q3:] = go.reshape(n_z, CORES, group, HEAD)
        remote(
            g.at[layer, :, 1 - c], gd.at[layer], gc_send.at[layer], gc_recv.at[layer], me, sibling
        ).start()

    start_da(0)

    def add_cores(lay):
        wait_bytes(gd.at[lay], gc_recv.at[lay])
        mine = (lay, slice(None), pl.ds(c, 1))
        g[mine] = (g[mine].astype(F32) + gd[lay][:, None].astype(F32)).astype(BF)

    def start_gz(lay, src_rows, slot_rows):
        for k in range(n_z - 1):
            to_z = lax.rem(z + 1 + k, n_z)
            remote(
                g.at[lay, to_z, c, src_rows], gz.at[lay, n_z - 2 - k, slot_rows],
                gz_send.at[lay], gz_recv.at[lay], me, z_peer(k),
            ).start()

    def sum_z(pair):
        for i in (1, 0):
            lay = 2 * pair + i
            wait_bytes(gz.at[lay], gz_recv.at[lay])
            total = g[lay, z, c].astype(F32)
            for k in range(n_z - 1):
                total = total + gz[lay, k].astype(F32)
            gx[lay] = total.astype(BF)

    def backward(t, carry):
        pair = end - t
        l0 = 2 * pair
        l1 = l0 + 1

        start_da(1)

        @pl.when(t >= 1)
        def _():
            for i in (1, 0):
                lay = l0 + 2 + i
                add_cores(lay)
                start_gz(lay, pl.ds(0, group), pl.ds(0, group))

        for cas in range(2):
            wait_gather(da.at[cas], da_ssem.at[cas], da_rsem.at[cas])
            cc1 = attend_back(l1, cas, 1, p1[pair, cas], da[cas, :, HEAD:])
            e1 = e_buf[1, cas]
            da0[cas] = (da[cas, :, :HEAD].astype(F32) + mm_nt(e1, ghb[pair][:, :q3]) - cc1 * t1[pair, cas]).astype(BF)
            dy[l0, cas] = (
                dy[l1, cas].astype(F32) + mm_nt(e1, weight(l1)[:, :q3]) - x[l1, cas].astype(F32) * cc1
            ).astype(BF)

            @pl.when(pair > 0)
            def _():
                cc0 = attend_back(l0, cas, 0, agb[pair, cas, 0, :, :q3], da0[cas])
                dy_new = (
                    dy[l0, cas].astype(F32)
                    + mm_nt(e_buf[0, cas], weight(l0)[:, :q3])
                    - x[l0, cas].astype(F32) * cc0
                ).astype(BF)
                dy[l0 - 1, cas] = dy_new
                start_ds(cas, dy_new, pair - 1)

        @pl.when(pair == 0)
        def _():
            weight_grads(l1, 1)
            for cas in range(2):
                attend_back(l0, cas, 0, agb[pair, cas, 0, :, :q3], da0[cas])

        @pl.when(t < end)
        def _():
            start_da(0)

        @pl.when(t >= 2)
        def _():
            sum_z(pair + 2)

        @pl.when(pair > 0)
        def _():
            weight_grads(l1, 1)

        weight_grads(l0, 0)
        return carry

    lax.fori_loop(0, pairs, backward, 0)

    for lay in (1, 0):
        add_cores(lay)
        remote(
            g.at[lay, :, c, other_rows], gxr.at[lay], gs_send.at[lay], gs_recv.at[lay], me, xh_peer
        ).start()
    def start_gy(layers_, sem):
        remote(
            gx.at[layers_, other_rows], gyr.at[layers_], gy_send.at[sem], gy_recv.at[sem], me, xh_peer
        ).start()

    def finish_gy(layers_, sem):
        wait_bytes(gyr.at[layers_], gy_recv.at[sem])
        gf[layers_] = (gx[layers_, my_rows].astype(F32) + gyr[layers_].astype(F32)).astype(BF)

    upper = pl.ds(4, n_pipe - 4)
    if pairs > 2:
        start_gy(upper, 0)
    for lay in (1, 0):
        wait_bytes(gxr.at[lay], gs_recv.at[lay])
        mine = (lay, slice(None), pl.ds(c, 1), my_rows)
        g[mine] = (g[mine].astype(F32) + gxr[lay][:, None].astype(F32)).astype(BF)
        start_gz(lay, my_rows, pl.ds(0, piece))
    if pairs > 1:
        sum_z(1)
        start_gy(pl.ds(2, 2), 1)
    if pairs > 2:
        finish_gy(upper, 0)
    for lay in (1, 0):
        wait_bytes(gz.at[lay, :, pl.ds(0, piece)], gz_recv.at[lay])
        total = g[lay, z, c, my_rows].astype(F32)
        for k in range(n_z - 1):
            total = total + gz[lay, k, :piece].astype(F32)
        gf[lay] = total.astype(BF)
    if pairs > 1:
        finish_gy(pl.ds(2, 2), 1)

    for k in range(n_pipe - 1):
        to = peer(k)
        remote(gf.at[to], hp.at[me], hp_send.at[0], hp_recv.at[0], to, d).start()
    hp[pl.ds(me, 1)] = gf[pl.ds(me, 1)]
    wait_bytes(hp.at[pl.ds(0, n_pipe - 1)], hp_recv.at[0])
    for k in range(n_pipe):
        pp = lax.rem(me + k, n_pipe)
        dd = n_i * pp + my_u // per_block

        @pl.when(dd != d)
        def _():
            remote(hp.at[pp], out.at[my_s, xh], gf_send.at[pp], gf_recv.at[0], me, dd).start()

        @pl.when(dd == d)
        def _():
            pltpu.make_async_copy(hp.at[pp], out.at[my_s, xh], gf_recv.at[0]).start()

    wait_bytes(out, gf_recv.at[0])
    full = out[...].astype(F32).reshape(per_block * group, width)
    gq_ref[0] = full[:, :q3]
    go_ref[0] = full[:, q3:].T

    for s in range(per_block):
        uz, uc = spread_to(s)
        for h in range(XH):
            dd = dp_at(h, uz, uc)

            @pl.when(dd != d)
            def _():
                wait_bytes(wpack.at[pl.ds((XH * s + h) * piece, piece)], w1_send.at[XH * s + h])

    wait_bytes(w1b.at[pl.ds(0, n_pipe - 1)], w2_send.at[0])
    wait_bytes(w1b, w2_send.at[1])
    wait_bytes(hp.at[pl.ds(0, n_pipe - 1)], hp_send.at[0])

    def drain(lay, carry):
        wait_bytes(w.at[lay, pl.ds(0, n_z - 1), c], wz_send.at[lay])
        wait_bytes(w.at[lay, :, c], wc_send.at[lay])
        wait_bytes(gd.at[lay], gc_send.at[lay])

        @pl.when(n_i * lay + my_u // per_block != d)
        def _():
            wait_bytes(hp.at[lay], gf_send.at[lay])

        return carry

    lax.fori_loop(0, n_pipe, drain, 0)
    for lay in range(2):
        wait_bytes(gxr.at[lay], gs_send.at[lay])
        wait_bytes(gz.at[lay, :, pl.ds(0, piece)], gz_send.at[lay])
    if pairs > 2:
        wait_bytes(gyr.at[upper], gy_send.at[0])
    if pairs > 1:
        wait_bytes(gyr.at[pl.ds(2, 2)], gy_send.at[1])

    def drain_z(lay, carry):
        wait_bytes(gz.at[lay], gz_send.at[lay])
        return carry

    lax.fori_loop(2, n_pipe, drain_z, 0)


def per_device(x_down, x_up, cot_down, cot_up, w_qkv, w_out, block_mask):
    n_pipe, n_dp = lax.axis_size("pipe"), lax.axis_size("dp")
    rows, dim = x_down.shape
    feat = dim // n_pipe
    n_z = n_dp // (XH * CORES)
    group = feat // (n_z * CORES)
    per_block = n_pipe // XH
    width = 4 * HEAD
    rb = rows // n_pipe
    layers = n_pipe
    pairs = layers // 2
    any_spec = pl.BlockSpec(memory_space=pl.ANY)
    vmem = pl.BlockSpec(memory_space=pltpu.VMEM)
    dma = pltpu.SemaphoreType.DMA
    return pl.pallas_call(
        functools.partial(kernel, n_pipe, n_dp),
        out_shape=(
            jax.ShapeDtypeStruct(w_qkv.shape, F32),
            jax.ShapeDtypeStruct(w_out.shape, F32),
        ),
        in_specs=[any_spec] * 4 + [vmem] * 2 + [pl.BlockSpec(memory_space=pltpu.SMEM)],
        out_specs=(vmem, vmem),
        scratch_shapes=[
            pltpu.VMEM((rows, rows), F32),
            pltpu.VMEM((per_block * group, width), BF),
            pltpu.VMEM((n_pipe, group // XH, width), BF),
            pltpu.VMEM((layers, n_z, CORES, group, width), BF),
            pltpu.VMEM((layers, 2, rows, feat), BF),
            pltpu.VMEM((layers, 2, rows, feat), BF),
            pltpu.VMEM((pairs, 2, 2, rows, width), BF),
            pltpu.VMEM((pairs, 2, rows, 3 * HEAD), BF),
            pltpu.VMEM((layers, 2, rows, rows), BF),
            pltpu.VMEM((layers, 2, rows, HEAD), BF),
            pltpu.VMEM((pairs, 2, rows, HEAD), F32),
            pltpu.VMEM((layers, 2, rows, HEAD), F32),
            pltpu.VMEM((2, 2, rows, 3 * HEAD), BF),
            pltpu.VMEM((2, 2, rows, width), BF),
            pltpu.VMEM((2, 2, n_pipe - 1, rb, width), BF),
            pltpu.VMEM((HEAD, width), BF),
            pltpu.VMEM((pairs, n_pipe - 1, HEAD // n_pipe, width), BF),
            pltpu.VMEM((pairs, HEAD, width), BF),
            pltpu.VMEM((2, rows, 2 * HEAD), BF),
            pltpu.VMEM((2, n_pipe - 1, rb, 2 * HEAD), BF),
            pltpu.VMEM((2, rows, 2 * HEAD), BF),
            pltpu.VMEM((2, rows, HEAD), BF),
            pltpu.VMEM((layers, n_z, CORES, group, width), BF),
            pltpu.VMEM((layers, n_z, group, width), BF),
            pltpu.VMEM((2, n_z, group // XH, width), BF),
            pltpu.VMEM((layers, n_z - 1, group, width), BF),
            pltpu.VMEM((layers, group, width), BF),
            pltpu.VMEM((layers, group // XH, width), BF),
            pltpu.VMEM((layers, group // XH, width), BF),
            pltpu.VMEM((layers, group // XH, width), BF),
            pltpu.VMEM((per_block, XH, group // XH, width), BF),
            dma((4,)),
            dma((n_pipe,)), dma((1,)),
            dma((2,)), dma((1,)),
            dma((layers,)), dma((layers, 4)),
            dma((layers,)), dma((layers,)),
            dma((2, 2)), dma((2, 2)), dma((2, 2)), dma((2, 2)),
            dma((1,)), dma((pairs,)), dma((pairs,)), dma((pairs,)),
            dma((2,)), dma((2,)), dma((2,)), dma((2,)),
            dma((layers,)), dma((layers,)),
            dma((2,)), dma((2,)),
            dma((2,)), dma((2,)),
            dma((layers,)), dma((layers,)),
            dma((1,)), dma((1,)),
            dma((layers,)), dma((1,)),
        ],
        compiler_params=pltpu.CompilerParams(
            collective_id=0, has_side_effects=True, vmem_limit_bytes=60 * 1024 * 1024
        ),
    )(x_down, x_up, cot_down, cot_up, w_qkv, w_out, block_mask)


def solution(mesh):
    placed = (
        P("dp", None),
        P("dp", None),
        P("dp", None),
        P("dp", None),
        P("pipe", "dp", None),
        P("pipe", None, "dp"),
        P(),
    )
    return jax.shard_map(
        per_device,
        mesh=mesh,
        in_specs=placed,
        out_specs=(P("pipe", "dp", None), P("pipe", None, "dp")),
        check_vma=False,
    )
```
